32 devices in a mesh: replica: 4 (over x, core), fsdp: 8 (over z, y).
Axes of the slice: x: 2, y: 2, z: 4, core: 2. Of those that a mesh axis runs over, the one named last changes fastest.
Arguments:
- tokens: bfloat16 [4, 1024, 8192], P('replica', 'fsdp'), may hold values from -6 to 6
- norm_gain: bfloat16 [8192], replicated, may hold values from 0.099609375 to 1.8984375
- cotangent: bfloat16 [4, 1024, 1024], P('replica', 'fsdp'), may hold values from -6 to 6
- layer_weight: bfloat16 [4, 8192, 1024], P('replica', 'fsdp'), may hold values from -0.09375 to 0.09375
- shared_copy: bfloat16 [8192, 1024], P('fsdp'), may hold values from -0.0625 to 0.0625
- master: float32 [8192, 1024], P('fsdp', 'replica'), may hold values from -0.0625 to 0.0625
- momentum: float32 [8192, 1024], P('fsdp', 'replica'), may hold values from -0.078125 to 0.078125
Outputs:
- layer_next: bfloat16 [4, 8192, 1024], P('replica', 'fsdp')
- master_next: float32 [8192, 1024], P('fsdp', 'replica')
- momentum_next: float32 [8192, 1024], P('fsdp', 'replica')
The draws below stay inside these ranges and needn't reach their ends.
All inputs are finite; a program needn't handle non-finite values.
Results may differ from the reference program's by a relative error of at most 0.013.
Values may be sent and summed in bfloat16 or wider, within the bound.
No kernel may reach another device: no remote copies, remote signals or barrier semaphores. Data moves between devices by JAX's collectives and lax.ppermute only.
A program may use at most 64 MiB of HBM per device.

```python
import math
import jax
import jax.numpy as jnp
from jax import lax

D = 8192
KV = 512
BLOCK = 64
TOKENS_REP = 1024
REPLICAS = 4


def spiked(drawn, stream_key, source, target, parts, factor):
    def block_of(dim):
        return (jnp.arange(drawn.shape[dim]) // (drawn.shape[dim] // parts)).reshape((-1,) + (1,) * (drawn.ndim - 1 - dim))

    first = jax.random.permutation(stream_key, parts)[block_of(target)]
    far = (block_of(target) + parts // 2) % parts
    return jnp.where((block_of(source) == first) | (block_of(source) == far), factor * drawn, drawn)


def block_levels(own_key, extent, cuts, least, high):
    level, own = 1.0, jax.random.fold_in(own_key, 6)
    for position, shards_of in cuts:
        draws = jnp.exp(jax.random.uniform(jax.random.fold_in(own, position), (shards_of,), jnp.float32, least / len(cuts), high / len(cuts)))
        level = level * jnp.repeat(draws, extent[position] // shards_of).reshape([-1 if axis == position else 1 for axis in range(len(extent))])
    return level


def centred(stream_key, extent, spread, limit, cuts=(), kind=jnp.bfloat16):
    level = block_levels(stream_key, extent, cuts, -0.22, 0.18) if cuts else 1.0
    entries = jax.random.normal(stream_key, extent, jnp.float32) * spread * level
    return jnp.minimum(jnp.maximum(entries, -limit), limit).astype(kind)


def noise_with(key, dims, spread, reach, shards, heavy, dtype=jnp.bfloat16):
    result = spread * jax.random.normal(key, dims, jnp.float32)
    if shards:
        result = result * block_levels(key, dims, shards, -0.22, 0.18)
    return jnp.clip(spiked(result, jax.random.fold_in(key, 3), *heavy), -reach, reach).astype(dtype)


def setup_inputs(seed: int = 0) -> dict:
    splits = jax.random.split(jax.random.key(seed), 8)
    tokens = centred(splits[0], (REPLICAS, TOKENS_REP, D), 1.0, 6.0, ((0, 4), (1, 8)))
    norm_gain = jnp.clip(1.0 + 0.18 * jax.random.normal(splits[1], (D,), jnp.float32), 0.099609375, 1.8984375).astype(jnp.bfloat16)
    cotangent = centred(splits[2], (REPLICAS, TOKENS_REP, 2 * KV), 1.0, 6.0, ((0, 4), (1, 8)))
    layer_weight = noise_with(splits[3], (REPLICAS, D, 2 * KV), D ** -0.5, 0.09375, ((0, 4), (1, 8)), (0, 2, 4, 2.0))
    shared_copy = centred(splits[4], (D, 2 * KV), D ** -0.5, 0.0625, ((0, 8),))
    master = centred(splits[5], (D, 2 * KV), D ** -0.5, 0.0625, ((0, 8), (1, 4)), jnp.float32)
    momentum = centred(splits[6], (D, 2 * KV), 0.005, 0.078125, ((0, 8), (1, 4)), jnp.float32)
    return dict(tokens=tokens, norm_gain=norm_gain, cotangent=cotangent, layer_weight=layer_weight, shared_copy=shared_copy, master=master, momentum=momentum)


norm_eps = 1e-05
inner_gain = 0.4
outer_rate = 0.7
outer_beta = 0.9
mix_weight = 0.5
code_range = 448.0

def reference(tokens, norm_gain, cotangent, layer_weight, shared_copy, master, momentum):
    shared_float = shared_copy.astype(jnp.float32)
    inner_rate = inner_gain / math.sqrt(TOKENS_REP)

    def replica_work(inputs):
        tok_block, cot_block, weight_block = inputs
        tok_float = tok_block.astype(jnp.float32)
        inverse = lax.rsqrt(lax.optimization_barrier(jnp.mean(tok_float * tok_float, axis=-1, keepdims=True)) + norm_eps)
        normed = (tok_float * inverse * norm_gain.astype(jnp.float32)).astype(jnp.bfloat16)
        grad = jnp.einsum('td,tk->dk', normed.astype(jnp.float32), cot_block.astype(jnp.float32))
        weight_float = weight_block.astype(jnp.float32)
        stepped = weight_float - inner_rate * grad
        delta = (shared_float - weight_float).reshape(D, 2 * KV // BLOCK, BLOCK)
        largest = lax.optimization_barrier(jnp.max(jnp.abs(delta), axis=-1, keepdims=True))
        scale = ((largest + 1e-06) / code_range).astype(jnp.bfloat16)
        coded = (delta / scale.astype(jnp.float32)).astype(jnp.bfloat16)
        decoded = coded.astype(jnp.float32) * scale.astype(jnp.float32)
        return (stepped, decoded.reshape(D, 2 * KV))
    stepped, decoded = lax.map(replica_work, (tokens, cotangent, layer_weight))
    average = lax.optimization_barrier(jnp.sum(decoded, axis=0)) / REPLICAS
    momentum_next = outer_beta * momentum + average
    master_next = master - outer_rate * (average + outer_beta * momentum_next)
    shared_next = master_next.astype(jnp.bfloat16).astype(jnp.float32)
    layer_next = (mix_weight * stepped + (1.0 - mix_weight) * shared_next[None]).astype(jnp.bfloat16)
    return (layer_next, master_next, momentum_next)
```

```python
import functools
import math

import jax
import jax.numpy as jnp
from jax import lax
from jax.experimental import pallas as pl
from jax.experimental.pallas import tpu as pltpu
from jax.sharding import PartitionSpec as P

BLOCK = 64


norm_eps = 1e-05
inner_gain = 0.4
outer_rate = 0.7
outer_beta = 0.9
mix_weight = 0.5
code_range = 448.0


def swap(value, axis, mask):
    size = lax.axis_size(axis)
    return lax.ppermute(value, axis, [(i, i ^ mask) for i in range(size)])


def code_kernel(shared_ref, weight_ref, decoded_ref):
    lanes = 2 * BLOCK
    lane = lax.broadcasted_iota(jnp.int32, (shared_ref.shape[0], lanes), 1)
    low = lane < BLOCK
    for start in range(0, shared_ref.shape[1], lanes):
        columns = slice(start, start + lanes)
        delta = shared_ref[:, columns].astype(jnp.float32) - weight_ref[:, columns].astype(jnp.float32)
        size = jnp.abs(delta)
        largest = jnp.where(
            low,
            jnp.max(jnp.where(low, size, 0.0), axis=-1, keepdims=True),
            jnp.max(jnp.where(low, 0.0, size), axis=-1, keepdims=True),
        )
        scale = ((largest + 1e-06) / code_range).astype(jnp.bfloat16).astype(jnp.float32)
        coded = (delta / scale).astype(jnp.bfloat16)
        decoded_ref[:, columns] = (coded.astype(jnp.float32) * scale).astype(jnp.bfloat16)


def code_and_decode(shared, weight):
    rows, width = shared.shape
    tile = min(rows, 128)
    spec = pl.BlockSpec((tile, width), lambda i: (i, 0))
    return pl.pallas_call(
        code_kernel,
        out_shape=jax.ShapeDtypeStruct((rows, width), jnp.bfloat16),
        grid=(rows // tile,),
        in_specs=[spec, spec],
        out_specs=spec,
        cost_estimate=pl.CostEstimate(flops=20 * rows * width, bytes_accessed=6 * rows * width, transcendentals=0),
        name="code_and_decode",
    )(shared, weight)


def mix_kernel(parts, *refs):
    tokens, cotangents = refs[:parts], refs[parts : 2 * parts]
    gain_ref, weight_ref, shared_ref, out_ref = refs[2 * parts :]
    total = None
    pair = 2 if parts % 2 == 0 else 1
    for first in range(0, parts, pair):
        product = lax.dot_general(
            jnp.concatenate([ref[...] for ref in tokens[first : first + pair]], axis=0),
            jnp.concatenate([ref[...] for ref in cotangents[first : first + pair]], axis=0),
            (((0,), (0,)), ((), ())),
            preferred_element_type=jnp.float32,
        )
        total = product if total is None else total + product
    weight = weight_ref[...].astype(jnp.float32) + shared_ref[...].astype(jnp.float32)
    out_ref[...] = (mix_weight * weight - gain_ref[...] * total).astype(jnp.bfloat16)


def mix(tokens, cotangents, gain, weight, shared):
    parts = len(tokens)
    rows, width = weight.shape
    tile = min(rows, 256)
    depth = tokens[0].shape[0]
    by_row = pl.BlockSpec((tile, width), lambda i: (i, 0))
    return pl.pallas_call(
        functools.partial(mix_kernel, parts),
        out_shape=jax.ShapeDtypeStruct((rows, width), jnp.bfloat16),
        grid=(rows // tile,),
        in_specs=[pl.BlockSpec((depth, tile), lambda i: (0, i))] * parts
        + [pl.BlockSpec((depth, width), lambda i: (0, 0))] * parts
        + [pl.BlockSpec((tile, 1), lambda i: (i, 0)), by_row, by_row],
        out_specs=by_row,
        compiler_params=pltpu.CompilerParams(vmem_limit_bytes=48 * 2**20),
        cost_estimate=pl.CostEstimate(
            flops=2 * parts * depth * rows * width,
            bytes_accessed=2 * parts * depth * (rows + width) + 6 * rows * width,
            transcendentals=0,
        ),
        name="mix",
    )(*tokens, *cotangents, gain, weight, shared)


def on_device(tokens, norm_gain, cotangent, layer_weight, shared_copy, master, momentum):
    tokens, cotangent, weight = tokens[0], cotangent[0], layer_weight[0]
    shards = lax.axis_size("fsdp")
    groups = lax.axis_size("replica")
    mine = lax.axis_index("fsdp")
    own = lax.axis_index("replica")
    rows, width = weight.shape
    share = width // groups
    inner_rate = inner_gain / math.sqrt(tokens.shape[0] * shards)

    blocks = [lax.dynamic_slice_in_dim(tokens, (mine ^ k) * rows, rows, axis=1) for k in range(shards)]
    *blocks, weight, shared_copy, cotangent = lax.optimization_barrier((*blocks, weight, shared_copy, cotangent))
    columns = [swap(block, "fsdp", k) if k else block for k, block in enumerate(blocks)]

    tok_float = tokens.astype(jnp.float32)
    inverse = lax.rsqrt(jnp.mean(tok_float * tok_float, axis=-1, keepdims=True) + norm_eps)
    scaled = (cotangent.astype(jnp.float32) * inverse).astype(jnp.bfloat16)
    cotangents = {0: scaled}
    bit = shards // 2
    while bit:
        held = sorted(cotangents)
        for part in ([k for k in held if k < shards // 2], [k for k in held if k >= shards // 2]):
            if part:
                arrived = swap(jnp.stack([cotangents[k] for k in part]), "fsdp", bit)
                for place, k in enumerate(part):
                    cotangents[k ^ bit] = arrived[place]
        bit //= 2

    total = code_and_decode(shared_copy, weight)
    bit = 1
    while bit < groups:
        side = (own // bit) % 2
        split = total.reshape(rows, groups // bit // 2, 2, share)
        kept = lax.dynamic_index_in_dim(split, side, axis=2, keepdims=False)
        sent = lax.dynamic_index_in_dim(split, 1 - side, axis=2, keepdims=False)
        total = kept.astype(jnp.float32) + swap(sent, "replica", bit).astype(jnp.float32)
        bit *= 2
        if bit < groups:
            total = total.astype(jnp.bfloat16)
    average = total.reshape(rows, share) / groups
    momentum_next = outer_beta * momentum + average
    master_next = master - outer_rate * (average + outer_beta * momentum_next)

    gathered = master_next.astype(jnp.bfloat16).reshape(rows, 1, share)
    bit = groups // 2
    while bit:
        side = (own // bit) % 2
        other = swap(gathered, "replica", bit)
        gathered = jnp.where(
            side == 0, jnp.stack([gathered, other], axis=2), jnp.stack([other, gathered], axis=2)
        ).reshape(rows, -1, share)
        bit //= 2
    shared_next = gathered.reshape(rows, width)

    gain = lax.dynamic_slice_in_dim(norm_gain, mine * rows, rows).astype(jnp.float32)
    gain = (gain * ((1.0 - mix_weight) * inner_rate)).reshape(rows, 1)
    layer_next = mix(columns, [cotangents[k] for k in range(shards)], gain, weight, shared_next)
    return (layer_next[None], master_next, momentum_next)


def solution(mesh):
    in_specs = (
        P("replica", "fsdp", None),
        P(),
        P("replica", "fsdp", None),
        P("replica", "fsdp", None),
        P("fsdp", None),
        P("fsdp", "replica"),
        P("fsdp", "replica"),
    )
    out_specs = (P("replica", "fsdp", None), P("fsdp", "replica"), P("fsdp", "replica"))
    return jax.shard_map(
        on_device, mesh=mesh, in_specs=in_specs, out_specs=out_specs, check_vma=False
    )
```

```python
import functools
import math

import jax
import jax.numpy as jnp
from jax import lax
from jax.experimental import pallas as pl
from jax.experimental.pallas import tpu as pltpu
from jax.sharding import PartitionSpec as P

BLOCK = 64


norm_eps = 1e-05
inner_gain = 0.4
outer_rate = 0.7
outer_beta = 0.9
mix_weight = 0.5
code_range = 448.0


def swap(value, axis, mask):
    size = lax.axis_size(axis)
    return lax.ppermute(value, axis, [(i, i ^ mask) for i in range(size)])


def prepare_kernel(tokens_ref, cotangent_ref, blocks_ref, scaled_ref):
    shards, _, rows = blocks_ref.shape
    squares = None
    for k in range(shards):
        block = tokens_ref[:, k * rows : (k + 1) * rows]
        blocks_ref[k] = block
        block = block.astype(jnp.float32)
        squares = block * block if squares is None else squares + block * block
    mean = jnp.sum(squares, axis=-1, keepdims=True) / (shards * rows)
    scaled_ref[...] = (cotangent_ref[...].astype(jnp.float32) * lax.rsqrt(mean + norm_eps)).astype(jnp.bfloat16)


def prepare(tokens, cotangent, shards):
    count, features = tokens.shape
    width = cotangent.shape[1]
    rows = features // shards
    tile = min(count, 32)
    return pl.pallas_call(
        prepare_kernel,
        out_shape=(
            jax.ShapeDtypeStruct((shards, count, rows), jnp.bfloat16),
            jax.ShapeDtypeStruct((count, width), jnp.bfloat16),
        ),
        grid=(count // tile,),
        in_specs=[
            pl.BlockSpec((tile, features), lambda i: (i, 0)),
            pl.BlockSpec((tile, width), lambda i: (i, 0)),
        ],
        out_specs=(
            pl.BlockSpec((shards, tile, rows), lambda i: (0, i, 0)),
            pl.BlockSpec((tile, width), lambda i: (i, 0)),
        ),
        cost_estimate=pl.CostEstimate(
            flops=3 * count * features, bytes_accessed=4 * count * (features + width), transcendentals=count
        ),
        name="prepare",
    )(tokens, cotangent)


def code_kernel(side_ref, shared_ref, weight_ref, decoded_ref):
    lanes = 2 * BLOCK
    share = decoded_ref.shape[3]
    lane = lax.broadcasted_iota(jnp.int32, (shared_ref.shape[0], lanes), 1)
    low = lane < BLOCK
    side = side_ref[0]
    for start in range(0, shared_ref.shape[1], lanes):
        columns = slice(start, start + lanes)
        delta = shared_ref[:, columns].astype(jnp.float32) - weight_ref[:, columns].astype(jnp.float32)
        size = jnp.abs(delta)
        largest = jnp.where(
            low,
            jnp.max(jnp.where(low, size, 0.0), axis=-1, keepdims=True),
            jnp.max(jnp.where(low, 0.0, size), axis=-1, keepdims=True),
        )
        scale = ((largest + 1e-06) * (1.0 / code_range)).astype(jnp.bfloat16).astype(jnp.float32)
        coded = (delta / scale).astype(jnp.bfloat16)
        decoded = (coded.astype(jnp.float32) * scale).astype(jnp.bfloat16)
        piece = min(share, lanes)
        for at in range(0, lanes, piece):
            group, offset = divmod(start + at, share)
            decoded_ref[(group % 2) ^ side, group // 2, :, offset : offset + piece] = decoded[:, at : at + piece]


def code_and_decode(shared, weight, groups, side):
    rows, width = shared.shape
    tile = min(rows, 128)
    share = width // groups
    spec = pl.BlockSpec((tile, width), lambda i, side: (i, 0))
    return pl.pallas_call(
        code_kernel,
        out_shape=jax.ShapeDtypeStruct((2, groups // 2, rows, share), jnp.bfloat16),
        grid_spec=pltpu.PrefetchScalarGridSpec(
            num_scalar_prefetch=1,
            grid=(rows // tile,),
            in_specs=[spec, spec],
            out_specs=pl.BlockSpec((2, groups // 2, tile, share), lambda i, side: (0, 0, i, 0)),
        ),
        cost_estimate=pl.CostEstimate(flops=20 * rows * width, bytes_accessed=6 * rows * width, transcendentals=0),
        name="code_and_decode",
    )(side.reshape(1), shared, weight)


def mix_kernel(parts, mine_ref, *refs):
    tokens, cotangents = refs[:parts], refs[parts : 2 * parts]
    gain_ref, weight_ref, shared_ref, out_ref = refs[2 * parts :]
    total = None
    pair = 2 if parts % 2 == 0 else 1
    for first in range(0, parts, pair):
        product = lax.dot_general(
            jnp.concatenate([ref[0] for ref in tokens[first : first + pair]], axis=0),
            jnp.concatenate([ref[...] for ref in cotangents[first : first + pair]], axis=0),
            (((0,), (0,)), ((), ())),
            preferred_element_type=jnp.float32,
        )
        total = product if total is None else total + product
    groups, _, share = shared_ref.shape
    for group in range(groups):
        columns = slice(group * share, (group + 1) * share)
        weight = weight_ref[:, columns].astype(jnp.float32) + shared_ref[group].astype(jnp.float32)
        out_ref[:, columns] = (mix_weight * weight - gain_ref[...] * total[:, columns]).astype(jnp.bfloat16)


def mix(mine, tokens, cotangents, gain, weight, shared):
    parts, depth, rows = tokens.shape
    width = weight.shape[1]
    groups, _, share = shared.shape
    tile = min(rows, 256)

    def token_block(k):
        return pl.BlockSpec((1, depth, tile), lambda i, mine: (mine[0] ^ k, 0, i))

    by_row = pl.BlockSpec((tile, width), lambda i, mine: (i, 0))
    return pl.pallas_call(
        functools.partial(mix_kernel, parts),
        out_shape=jax.ShapeDtypeStruct((rows, width), jnp.bfloat16),
        grid_spec=pltpu.PrefetchScalarGridSpec(
            num_scalar_prefetch=1,
            grid=(rows // tile,),
            in_specs=[token_block(k) for k in range(parts)]
            + [pl.BlockSpec((depth, width), lambda i, mine: (0, 0))] * parts
            + [
                pl.BlockSpec((tile, 1), lambda i, mine: (i, 0)),
                by_row,
                pl.BlockSpec((groups, tile, share), lambda i, mine: (0, i, 0)),
            ],
            out_specs=by_row,
        ),
        compiler_params=pltpu.CompilerParams(vmem_limit_bytes=48 * 2**20),
        cost_estimate=pl.CostEstimate(
            flops=2 * parts * depth * rows * width,
            bytes_accessed=2 * parts * depth * (rows + width) + 6 * rows * width,
            transcendentals=0,
        ),
        name="mix",
    )(mine.reshape(1), *([tokens] * parts), *cotangents, gain, weight, shared)


def on_device(tokens, norm_gain, cotangent, layer_weight, shared_copy, master, momentum):
    tokens, cotangent, weight = tokens[0], cotangent[0], layer_weight[0]
    shards = lax.axis_size("fsdp")
    groups = lax.axis_size("replica")
    mine = lax.axis_index("fsdp")
    own = lax.axis_index("replica")
    rows, width = weight.shape
    share = width // groups
    inner_rate = inner_gain / math.sqrt(tokens.shape[0] * shards)

    blocks, scaled = prepare(tokens, cotangent, shards)
    blocks, scaled, weight, shared_copy = lax.optimization_barrier((blocks, scaled, weight, shared_copy))
    columns = lax.all_to_all(blocks, "fsdp", split_axis=0, concat_axis=0, tiled=True)

    cotangents = {0: scaled}
    bit = shards // 2
    while bit:
        held = sorted(cotangents)
        for part in ([k for k in held if k < shards // 2], [k for k in held if k >= shards // 2]):
            if part:
                arrived = swap(jnp.stack([cotangents[k] for k in part]), "fsdp", bit)
                for place, k in enumerate(part):
                    cotangents[k ^ bit] = arrived[place]
        bit //= 2

    kept, sent = code_and_decode(shared_copy, weight, groups, own % 2)
    total = kept.astype(jnp.float32) + swap(sent, "replica", 1).astype(jnp.float32)
    bit = 2
    while bit < groups:
        side = (own // bit) % 2
        split = total.astype(jnp.bfloat16).reshape(-1, 2, rows, share)
        kept = lax.dynamic_index_in_dim(split, side, axis=1, keepdims=False)
        sent = lax.dynamic_index_in_dim(split, 1 - side, axis=1, keepdims=False)
        total = kept.astype(jnp.float32) + swap(sent, "replica", bit).astype(jnp.float32)
        bit *= 2
    average = total.reshape(rows, share) / groups
    momentum_next = outer_beta * momentum + average
    master_next = master - outer_rate * (average + outer_beta * momentum_next)

    gathered = master_next.astype(jnp.bfloat16).reshape(1, rows, share)
    bit = groups // 2
    while bit:
        side = (own // bit) % 2
        other = swap(gathered, "replica", bit)
        gathered = jnp.where(
            side == 0, jnp.stack([gathered, other], axis=1), jnp.stack([other, gathered], axis=1)
        ).reshape(-1, rows, share)
        bit //= 2

    gain = lax.dynamic_slice_in_dim(norm_gain, mine * rows, rows).astype(jnp.float32)
    gain = (gain * ((1.0 - mix_weight) * inner_rate)).reshape(rows, 1)
    layer_next = mix(mine, columns, [cotangents[k] for k in range(shards)], gain, weight, gathered)
    return (layer_next[None], master_next, momentum_next)


def solution(mesh):
    in_specs = (
        P("replica", "fsdp", None),
        P(),
        P("replica", "fsdp", None),
        P("replica", "fsdp", None),
        P("fsdp", None),
        P("fsdp", "replica"),
        P("fsdp", "replica"),
    )
    out_specs = (P("replica", "fsdp", None), P("fsdp", "replica"), P("fsdp", "replica"))
    return jax.shard_map(
        on_device, mesh=mesh, in_specs=in_specs, out_specs=out_specs, check_vma=False
    )
```

```python
import functools
import math

import jax
import jax.numpy as jnp
from jax import lax
from jax.experimental import pallas as pl
from jax.experimental.pallas import tpu as pltpu
from jax.sharding import PartitionSpec as P

BLOCK = 64


norm_eps = 1e-05
inner_gain = 0.4
outer_rate = 0.7
outer_beta = 0.9
mix_weight = 0.5
code_range = 448.0


def swap(value, axis, mask):
    size = lax.axis_size(axis)
    return lax.ppermute(value, axis, [(i, i ^ mask) for i in range(size)])


def prepare_kernel(tokens_ref, cotangent_ref, blocks_ref, scaled_ref):
    shards, _, rows = blocks_ref.shape
    squares = None
    for k in range(shards):
        block = tokens_ref[:, k * rows : (k + 1) * rows]
        blocks_ref[k] = block
        block = block.astype(jnp.float32)
        squares = block * block if squares is None else squares + block * block
    mean = jnp.sum(squares, axis=-1, keepdims=True) / (shards * rows)
    scaled_ref[...] = (cotangent_ref[...].astype(jnp.float32) * lax.rsqrt(mean + norm_eps)).astype(jnp.bfloat16)


def prepare(tokens, cotangent, shards):
    count, features = tokens.shape
    width = cotangent.shape[1]
    rows = features // shards
    tile = min(count, 32)
    return pl.pallas_call(
        prepare_kernel,
        out_shape=(
            jax.ShapeDtypeStruct((shards, count, rows), jnp.bfloat16),
            jax.ShapeDtypeStruct((count, width), jnp.bfloat16),
        ),
        grid=(count // tile,),
        in_specs=[
            pl.BlockSpec((tile, features), lambda i: (i, 0)),
            pl.BlockSpec((tile, width), lambda i: (i, 0)),
        ],
        out_specs=(
            pl.BlockSpec((shards, tile, rows), lambda i: (0, i, 0)),
            pl.BlockSpec((tile, width), lambda i: (i, 0)),
        ),
        cost_estimate=pl.CostEstimate(
            flops=3 * count * features, bytes_accessed=4 * count * (features + width), transcendentals=count
        ),
        name="prepare",
    )(tokens, cotangent)


def code_kernel(own_ref, shared_ref, weight_ref, kept_ref, sent_ref, decoded_ref):
    lanes = 2 * BLOCK
    groups, rows, share = decoded_ref.shape
    low = lax.broadcasted_iota(jnp.int32, (rows, lanes), 1) < BLOCK
    for start in range(0, groups * share, lanes):
        columns = slice(start, start + lanes)
        delta = shared_ref[:, columns].astype(jnp.float32) - weight_ref[:, columns].astype(jnp.float32)
        size = jnp.abs(delta)
        largest = jnp.where(
            low,
            jnp.max(jnp.where(low, size, 0.0), axis=-1, keepdims=True),
            jnp.max(jnp.where(low, 0.0, size), axis=-1, keepdims=True),
        )
        scale = ((largest + 1e-06) * (1.0 / code_range)).astype(jnp.bfloat16).astype(jnp.float32)
        coded = (delta / scale).astype(jnp.bfloat16)
        decoded = (coded.astype(jnp.float32) * scale).astype(jnp.bfloat16)
        piece = min(share, lanes)
        for at in range(0, lanes, piece):
            group, offset = divmod(start + at, share)
            decoded_ref[group, :, offset : offset + piece] = decoded[:, at : at + piece]
    own = own_ref[0]
    for k in range(0, groups, 2):
        kept_ref[k // 2] = decoded_ref[own ^ k]
        sent_ref[k // 2] = decoded_ref[own ^ (k + 1)]


def code_and_decode(own, shared, weight, groups):
    rows, width = shared.shape
    tile = min(rows, 128)
    share = width // groups
    spec = pl.BlockSpec((tile, width), lambda i, own: (i, 0))
    half = jax.ShapeDtypeStruct((groups // 2, rows, share), jnp.bfloat16)
    half_spec = pl.BlockSpec((groups // 2, tile, share), lambda i, own: (0, i, 0))
    return pl.pallas_call(
        code_kernel,
        out_shape=(half, half),
        grid_spec=pltpu.PrefetchScalarGridSpec(
            num_scalar_prefetch=1,
            grid=(rows // tile,),
            in_specs=[spec, spec],
            out_specs=(half_spec, half_spec),
            scratch_shapes=[pltpu.VMEM((groups, tile, share), jnp.bfloat16)],
        ),
        cost_estimate=pl.CostEstimate(flops=20 * rows * width, bytes_accessed=6 * rows * width, transcendentals=0),
        name="code_and_decode",
    )(own.reshape(1), shared, weight)


def mix_kernel(parts, groups, place_ref, *refs):
    tokens, refs = refs[:parts], refs[parts:]
    cotangents, refs = refs[:parts], refs[parts:]
    pieces, refs = refs[:groups], refs[groups:]
    gain_ref, weight_ref, out_ref, shared_ref = refs
    total = None
    pair = 2 if parts % 2 == 0 else 1
    for first in range(0, parts, pair):
        product = lax.dot_general(
            jnp.concatenate([ref[0] for ref in tokens[first : first + pair]], axis=0),
            jnp.concatenate([ref[...] for ref in cotangents[first : first + pair]], axis=0),
            (((0,), (0,)), ((), ())),
            preferred_element_type=jnp.float32,
        )
        total = product if total is None else total + product
    own = place_ref[1]
    for k, piece in enumerate(pieces):
        shared_ref[own ^ k] = piece[...]
    share = shared_ref.shape[2]
    for group in range(groups):
        columns = slice(group * share, (group + 1) * share)
        weight = weight_ref[:, columns].astype(jnp.float32) + shared_ref[group].astype(jnp.float32)
        out_ref[:, columns] = (mix_weight * weight - gain_ref[...] * total[:, columns]).astype(jnp.bfloat16)


def mix(mine, own, tokens, cotangents, pieces, gain, weight):
    parts, depth, rows = tokens.shape
    width = weight.shape[1]
    groups = len(pieces)
    share = width // groups
    tile = min(rows, 256)

    def token_block(k):
        return pl.BlockSpec((1, depth, tile), lambda i, place: (place[0] ^ k, 0, i))

    by_row = pl.BlockSpec((tile, width), lambda i, place: (i, 0))
    return pl.pallas_call(
        functools.partial(mix_kernel, parts, groups),
        out_shape=jax.ShapeDtypeStruct((rows, width), jnp.bfloat16),
        grid_spec=pltpu.PrefetchScalarGridSpec(
            num_scalar_prefetch=1,
            grid=(rows // tile,),
            in_specs=[token_block(k) for k in range(parts)]
            + [pl.BlockSpec((depth, width), lambda i, place: (0, 0))] * parts
            + [pl.BlockSpec((tile, share), lambda i, place: (i, 0))] * groups
            + [pl.BlockSpec((tile, 1), lambda i, place: (i, 0)), by_row],
            out_specs=by_row,
            scratch_shapes=[pltpu.VMEM((groups, tile, share), jnp.bfloat16)],
        ),
        compiler_params=pltpu.CompilerParams(vmem_limit_bytes=48 * 2**20),
        cost_estimate=pl.CostEstimate(
            flops=2 * parts * depth * rows * width,
            bytes_accessed=2 * parts * depth * (rows + width) + 6 * rows * width,
            transcendentals=0,
        ),
        name="mix",
    )(jnp.stack([mine, own]), *([tokens] * parts), *cotangents, *pieces, gain, weight)


def gather(piece, axis):
    size = lax.axis_size(axis)
    pieces = {0: piece}
    bit = size // 2
    while bit:
        for k in sorted(pieces):
            pieces[k ^ bit] = swap(pieces[k], axis, bit)
        bit //= 2
    return [pieces[k] for k in range(size)]


def on_device(tokens, norm_gain, cotangent, layer_weight, shared_copy, master, momentum):
    tokens, cotangent, weight = tokens[0], cotangent[0], layer_weight[0]
    shards = lax.axis_size("fsdp")
    groups = lax.axis_size("replica")
    mine = lax.axis_index("fsdp")
    own = lax.axis_index("replica")
    rows, width = weight.shape
    inner_rate = inner_gain / math.sqrt(tokens.shape[0] * shards)

    blocks, scaled = prepare(tokens, cotangent, shards)
    cotangents = gather(scaled, "fsdp")
    columns = lax.all_to_all(blocks, "fsdp", split_axis=0, concat_axis=0, tiled=True)

    _, coded_weight, coded_shared = lax.optimization_barrier((cotangents[shards // 2], weight, shared_copy))
    kept, sent = code_and_decode(own, coded_shared, coded_weight, groups)
    total = kept.astype(jnp.float32) + swap(sent, "replica", 1).astype(jnp.float32)
    bit = 2
    while bit < groups:
        sent = swap(total[1::2].astype(jnp.bfloat16), "replica", bit)
        total = total[0::2] + sent.astype(jnp.float32)
        bit *= 2
    average = total[0] / groups
    momentum_next = outer_beta * momentum + average
    master_next = master - outer_rate * (average + outer_beta * momentum_next)
    pieces = gather(master_next.astype(jnp.bfloat16), "replica")

    gain = lax.dynamic_slice_in_dim(norm_gain, mine * rows, rows).astype(jnp.float32)
    gain = (gain * ((1.0 - mix_weight) * inner_rate)).reshape(rows, 1)
    layer_next = mix(mine, own, columns, cotangents, pieces, gain, weight)
    return (layer_next[None], master_next, momentum_next)


def solution(mesh):
    in_specs = (
        P("replica", "fsdp", None),
        P(),
        P("replica", "fsdp", None),
        P("replica", "fsdp", None),
        P("fsdp", None),
        P("fsdp", "replica"),
        P("fsdp", "replica"),
    )
    out_specs = (P("replica", "fsdp", None), P("fsdp", "replica"), P("fsdp", "replica"))
    return jax.shard_map(
        on_device, mesh=mesh, in_specs=in_specs, out_specs=out_specs, check_vma=False
    )
```

```python
import functools
import math

import jax
import jax.numpy as jnp
from jax import lax
from jax.experimental import pallas as pl
from jax.experimental.pallas import tpu as pltpu
from jax.sharding import PartitionSpec as P

BLOCK = 64


norm_eps = 1e-05
inner_gain = 0.4
outer_rate = 0.7
outer_beta = 0.9
mix_weight = 0.5
code_range = 448.0


def swap(value, axis, mask):
    size = lax.axis_size(axis)
    return lax.ppermute(value, axis, [(i, i ^ mask) for i in range(size)])


def prepare_kernel(tokens_ref, cotangent_ref, blocks_ref, scaled_ref):
    shards, _, rows = blocks_ref.shape
    squares = None
    for k in range(shards):
        block = tokens_ref[:, k * rows : (k + 1) * rows]
        blocks_ref[k] = block
        block = block.astype(jnp.float32)
        squares = block * block if squares is None else squares + block * block
    mean = jnp.sum(squares, axis=-1, keepdims=True) / (shards * rows)
    scaled_ref[...] = (cotangent_ref[...].astype(jnp.float32) * lax.rsqrt(mean + norm_eps)).astype(jnp.bfloat16)


def prepare(tokens, cotangent, shards):
    count, features = tokens.shape
    width = cotangent.shape[1]
    rows = features // shards
    tile = min(count, 32)
    return pl.pallas_call(
        prepare_kernel,
        out_shape=(
            jax.ShapeDtypeStruct((shards, count, rows), jnp.bfloat16),
            jax.ShapeDtypeStruct((count, width), jnp.bfloat16),
        ),
        grid=(count // tile,),
        in_specs=[
            pl.BlockSpec((tile, features), lambda i: (i, 0)),
            pl.BlockSpec((tile, width), lambda i: (i, 0)),
        ],
        out_specs=(
            pl.BlockSpec((shards, tile, rows), lambda i: (0, i, 0)),
            pl.BlockSpec((tile, width), lambda i: (i, 0)),
        ),
        cost_estimate=pl.CostEstimate(
            flops=3 * count * features, bytes_accessed=4 * count * (features + width), transcendentals=count
        ),
        name="prepare",
    )(tokens, cotangent)


def code_kernel(own_ref, shared_ref, weight_ref, kept_ref, sent_ref, decoded_ref):
    lanes = 2 * BLOCK
    groups, rows, share = decoded_ref.shape
    low = lax.broadcasted_iota(jnp.int32, (rows, lanes), 1) < BLOCK
    for start in range(0, groups * share, lanes):
        columns = slice(start, start + lanes)
        delta = shared_ref[:, columns].astype(jnp.float32) - weight_ref[:, columns].astype(jnp.float32)
        size = jnp.abs(delta)
        largest = jnp.where(
            low,
            jnp.max(jnp.where(low, size, 0.0), axis=-1, keepdims=True),
            jnp.max(jnp.where(low, 0.0, size), axis=-1, keepdims=True),
        )
        scale = ((largest + 1e-06) * (1.0 / code_range)).astype(jnp.bfloat16).astype(jnp.float32)
        coded = (delta / scale).astype(jnp.bfloat16)
        decoded = (coded.astype(jnp.float32) * scale).astype(jnp.bfloat16)
        piece = min(share, lanes)
        for at in range(0, lanes, piece):
            group, offset = divmod(start + at, share)
            decoded_ref[group, :, offset : offset + piece] = decoded[:, at : at + piece]
    own = own_ref[0]
    for k in range(0, groups, 2):
        kept_ref[k // 2] = decoded_ref[own ^ k]
        sent_ref[k // 2] = decoded_ref[own ^ (k + 1)]


def code_and_decode(own, shared, weight, groups):
    rows, width = shared.shape
    tile = min(rows, 128)
    share = width // groups
    spec = pl.BlockSpec((tile, width), lambda i, own: (i, 0))
    half = jax.ShapeDtypeStruct((groups // 2, rows, share), jnp.bfloat16)
    half_spec = pl.BlockSpec((groups // 2, tile, share), lambda i, own: (0, i, 0))
    return pl.pallas_call(
        code_kernel,
        out_shape=(half, half),
        grid_spec=pltpu.PrefetchScalarGridSpec(
            num_scalar_prefetch=1,
            grid=(rows // tile,),
            in_specs=[spec, spec],
            out_specs=(half_spec, half_spec),
            scratch_shapes=[pltpu.VMEM((groups, tile, share), jnp.bfloat16)],
        ),
        cost_estimate=pl.CostEstimate(flops=20 * rows * width, bytes_accessed=6 * rows * width, transcendentals=0),
        name="code_and_decode",
    )(own.reshape(1), shared, weight)


def mix_kernel(parts, groups, place_ref, *refs):
    tokens, refs = refs[:parts], refs[parts:]
    cotangents, refs = refs[:parts], refs[parts:]
    pieces, refs = refs[:groups], refs[groups:]
    gain_ref, weight_ref, out_ref, shared_ref = refs
    total = None
    pair = 2 if parts % 2 == 0 else 1
    for first in range(0, parts, pair):
        product = lax.dot_general(
            jnp.concatenate([ref[0] for ref in tokens[first : first + pair]], axis=0),
            jnp.concatenate([ref[...] for ref in cotangents[first : first + pair]], axis=0),
            (((0,), (0,)), ((), ())),
            preferred_element_type=jnp.float32,
        )
        total = product if total is None else total + product
    own = place_ref[1]
    for k, piece in enumerate(pieces):
        shared_ref[own ^ k] = piece[...]
    share = shared_ref.shape[2]
    for group in range(groups):
        columns = slice(group * share, (group + 1) * share)
        weight = weight_ref[:, columns].astype(jnp.float32) + shared_ref[group].astype(jnp.float32)
        out_ref[:, columns] = (mix_weight * weight - gain_ref[...] * total[:, columns]).astype(jnp.bfloat16)


def mix(mine, own, tokens, cotangents, pieces, gain, weight):
    parts, depth, rows = tokens.shape
    width = weight.shape[1]
    groups = len(pieces)
    share = width // groups
    tile = min(rows, 256)

    def token_block(k):
        return pl.BlockSpec((1, depth, tile), lambda i, place: (place[0] ^ k, 0, i))

    by_row = pl.BlockSpec((tile, width), lambda i, place: (i, 0))
    return pl.pallas_call(
        functools.partial(mix_kernel, parts, groups),
        out_shape=jax.ShapeDtypeStruct((rows, width), jnp.bfloat16),
        grid_spec=pltpu.PrefetchScalarGridSpec(
            num_scalar_prefetch=1,
            grid=(rows // tile,),
            in_specs=[token_block(k) for k in range(parts)]
            + [pl.BlockSpec((depth, width), lambda i, place: (0, 0))] * parts
            + [pl.BlockSpec((tile, share), lambda i, place: (i, 0))] * groups
            + [pl.BlockSpec((tile, 1), lambda i, place: (i, 0)), by_row],
            out_specs=by_row,
            scratch_shapes=[pltpu.VMEM((groups, tile, share), jnp.bfloat16)],
        ),
        compiler_params=pltpu.CompilerParams(vmem_limit_bytes=48 * 2**20),
        cost_estimate=pl.CostEstimate(
            flops=2 * parts * depth * rows * width,
            bytes_accessed=2 * parts * depth * (rows + width) + 6 * rows * width,
            transcendentals=0,
        ),
        name="mix",
    )(jnp.stack([mine, own]), *([tokens] * parts), *cotangents, *pieces, gain, weight)


def gather(piece, axis):
    size = lax.axis_size(axis)
    pieces = {0: piece}
    bit = size // 2
    while bit:
        for k in sorted(pieces):
            pieces[k ^ bit] = swap(pieces[k], axis, bit)
        bit //= 2
    return [pieces[k] for k in range(size)]


def on_device(tokens, norm_gain, cotangent, layer_weight, shared_copy, master, momentum):
    tokens, cotangent, weight = tokens[0], cotangent[0], layer_weight[0]
    shards = lax.axis_size("fsdp")
    groups = lax.axis_size("replica")
    mine = lax.axis_index("fsdp")
    own = lax.axis_index("replica")
    rows, width = weight.shape
    inner_rate = inner_gain / math.sqrt(tokens.shape[0] * shards)

    blocks, scaled = prepare(tokens, cotangent, shards)
    cotangents = gather(scaled, "fsdp")
    first = [cotangents[1 << bit] for bit in range(shards.bit_length() - 1)]
    *_, blocks, coded_weight, coded_shared = lax.optimization_barrier((*first, blocks, weight, shared_copy))
    columns = lax.all_to_all(blocks, "fsdp", split_axis=0, concat_axis=0, tiled=True)

    kept, sent = code_and_decode(own, coded_shared, coded_weight, groups)
    total = kept.astype(jnp.float32) + swap(sent, "replica", 1).astype(jnp.float32)
    bit = 2
    while bit < groups:
        sent = swap(total[1::2].astype(jnp.bfloat16), "replica", bit)
        total = total[0::2] + sent.astype(jnp.float32)
        bit *= 2
    average = total[0] / groups
    momentum_next = outer_beta * momentum + average
    master_next = master - outer_rate * (average + outer_beta * momentum_next)
    pieces = gather(master_next.astype(jnp.bfloat16), "replica")

    gain = lax.dynamic_slice_in_dim(norm_gain, mine * rows, rows).astype(jnp.float32)
    gain = (gain * ((1.0 - mix_weight) * inner_rate)).reshape(rows, 1)
    layer_next = mix(mine, own, columns, cotangents, pieces, gain, weight)
    return (layer_next[None], master_next, momentum_next)


def solution(mesh):
    in_specs = (
        P("replica", "fsdp", None),
        P(),
        P("replica", "fsdp", None),
        P("replica", "fsdp", None),
        P("fsdp", None),
        P("fsdp", "replica"),
        P("fsdp", "replica"),
    )
    out_specs = (P("replica", "fsdp", None), P("fsdp", "replica"), P("fsdp", "replica"))
    return jax.shard_map(
        on_device, mesh=mesh, in_specs=in_specs, out_specs=out_specs, check_vma=False
    )
```

```python
import functools
import math

import jax
import jax.numpy as jnp
from jax import lax
from jax.experimental import pallas as pl
from jax.experimental.pallas import tpu as pltpu
from jax.sharding import PartitionSpec as P

BLOCK = 64


norm_eps = 1e-05
inner_gain = 0.4
outer_rate = 0.7
outer_beta = 0.9
mix_weight = 0.5
code_range = 448.0


def swap(value, axis, mask):
    size = lax.axis_size(axis)
    return lax.ppermute(value, axis, [(i, i ^ mask) for i in range(size)])


def scale_kernel(tokens_ref, cotangent_ref, scaled_ref):
    count, features = tokens_ref.shape
    lanes = min(features, 1024)
    squares = jnp.zeros((count, lanes), jnp.float32)
    for start in range(0, features, lanes):
        block = tokens_ref[:, start : start + lanes].astype(jnp.float32)
        squares = squares + block * block
    mean = jnp.sum(squares, axis=-1, keepdims=True) / features
    scaled_ref[...] = (cotangent_ref[...].astype(jnp.float32) * lax.rsqrt(mean + norm_eps)).astype(jnp.bfloat16)


def scale_cotangent(tokens, cotangent):
    count, features = tokens.shape
    width = cotangent.shape[1]
    tile = min(count, 32)
    return pl.pallas_call(
        scale_kernel,
        out_shape=jax.ShapeDtypeStruct((count, width), jnp.bfloat16),
        grid=(count // tile,),
        in_specs=[
            pl.BlockSpec((tile, features), lambda i: (i, 0)),
            pl.BlockSpec((tile, width), lambda i: (i, 0)),
        ],
        out_specs=pl.BlockSpec((tile, width), lambda i: (i, 0)),
        cost_estimate=pl.CostEstimate(
            flops=3 * count * features, bytes_accessed=2 * count * (features + 2 * width), transcendentals=count
        ),
        name="scale_cotangent",
    )(tokens, cotangent)


def cut_kernel(tokens_ref, *refs):
    *out_refs, sems = refs
    shards, count, rows = out_refs[0].shape
    copies = [
        pltpu.make_async_copy(
            tokens_ref.at[pl.ds(part * count, count), pl.ds(k * rows, rows)], out_ref.at[k], sems.at[part, k]
        )
        for part, out_ref in enumerate(out_refs)
        for k in range(shards)
    ]
    for copy in copies:
        copy.start()
    for copy in copies:
        copy.wait()


def cut(tokens, shards, parts):
    count, features = tokens.shape
    part = jax.ShapeDtypeStruct((shards, count // parts, features // shards), jnp.bfloat16)
    return pl.pallas_call(
        cut_kernel,
        out_shape=(part,) * parts,
        in_specs=[pl.BlockSpec(memory_space=pl.ANY)],
        out_specs=(pl.BlockSpec(memory_space=pl.ANY),) * parts,
        scratch_shapes=[pltpu.SemaphoreType.DMA((parts, shards))],
        cost_estimate=pl.CostEstimate(flops=0, bytes_accessed=4 * count * features, transcendentals=0),
        name="cut",
    )(tokens)


def code_kernel(own_ref, shared_ref, weight_ref, kept_ref, sent_ref, decoded_ref):
    lanes = 2 * BLOCK
    groups, rows, share = decoded_ref.shape
    low = lax.broadcasted_iota(jnp.int32, (rows, lanes), 1) < BLOCK
    for start in range(0, groups * share, lanes):
        columns = slice(start, start + lanes)
        delta = shared_ref[:, columns].astype(jnp.float32) - weight_ref[:, columns].astype(jnp.float32)
        size = jnp.abs(delta)
        largest = jnp.where(
            low,
            jnp.max(jnp.where(low, size, 0.0), axis=-1, keepdims=True),
            jnp.max(jnp.where(low, 0.0, size), axis=-1, keepdims=True),
        )
        scale = ((largest + 1e-06) * (1.0 / code_range)).astype(jnp.bfloat16).astype(jnp.float32)
        coded = (delta * pl.reciprocal(scale)).astype(jnp.bfloat16)
        decoded = (coded.astype(jnp.float32) * scale).astype(jnp.bfloat16)
        piece = min(share, lanes)
        for at in range(0, lanes, piece):
            group, offset = divmod(start + at, share)
            decoded_ref[group, :, offset : offset + piece] = decoded[:, at : at + piece]
    own = own_ref[0]
    for k in range(0, groups, 2):
        kept_ref[k // 2] = decoded_ref[own ^ k]
        sent_ref[k // 2] = decoded_ref[own ^ (k + 1)]


def code_and_decode(own, shared, weight, groups):
    rows, width = shared.shape
    tile = min(rows, 128)
    share = width // groups
    spec = pl.BlockSpec((tile, width), lambda i, own: (i, 0))
    half = jax.ShapeDtypeStruct((groups // 2, rows, share), jnp.bfloat16)
    half_spec = pl.BlockSpec((groups // 2, tile, share), lambda i, own: (0, i, 0))
    return pl.pallas_call(
        code_kernel,
        out_shape=(half, half),
        grid_spec=pltpu.PrefetchScalarGridSpec(
            num_scalar_prefetch=1,
            grid=(rows // tile,),
            in_specs=[spec, spec],
            out_specs=(half_spec, half_spec),
            scratch_shapes=[pltpu.VMEM((groups, tile, share), jnp.bfloat16)],
        ),
        cost_estimate=pl.CostEstimate(flops=20 * rows * width, bytes_accessed=6 * rows * width, transcendentals=0),
        name="code_and_decode",
    )(own.reshape(1), shared, weight)


def mix_kernel(shards, parts, groups, place_ref, *refs):
    tokens, refs = refs[: shards * parts], refs[shards * parts :]
    cotangents, refs = refs[:shards], refs[shards:]
    pieces, refs = refs[:groups], refs[groups:]
    gain_ref, weight_ref, out_ref, shared_ref = refs
    total = None
    pair = 2
    for first in range(0, shards, pair):
        product = lax.dot_general(
            jnp.concatenate([ref[0] for ref in tokens[first * parts : (first + pair) * parts]], axis=0),
            jnp.concatenate([ref[...] for ref in cotangents[first : first + pair]], axis=0),
            (((0,), (0,)), ((), ())),
            preferred_element_type=jnp.float32,
        )
        total = product if total is None else total + product
    own = place_ref[1]
    for k, piece in enumerate(pieces):
        shared_ref[own ^ k] = piece[...]
    share = shared_ref.shape[2]
    for group in range(groups):
        columns = slice(group * share, (group + 1) * share)
        weight = weight_ref[:, columns].astype(jnp.float32) + shared_ref[group].astype(jnp.float32)
        out_ref[:, columns] = (mix_weight * weight - gain_ref[...] * total[:, columns]).astype(jnp.bfloat16)


def mix(mine, own, tokens, cotangents, pieces, gain, weight):
    parts = len(tokens)
    shards, depth, rows = tokens[0].shape
    width = weight.shape[1]
    groups = len(pieces)
    share = width // groups
    tile = min(rows, 256)

    def token_block(k):
        return pl.BlockSpec((1, depth, tile), lambda i, place: (place[0] ^ k, 0, i))

    by_row = pl.BlockSpec((tile, width), lambda i, place: (i, 0))
    return pl.pallas_call(
        functools.partial(mix_kernel, shards, parts, groups),
        out_shape=jax.ShapeDtypeStruct((rows, width), jnp.bfloat16),
        grid_spec=pltpu.PrefetchScalarGridSpec(
            num_scalar_prefetch=1,
            grid=(rows // tile,),
            in_specs=[token_block(k) for k in range(shards) for _ in range(parts)]
            + [pl.BlockSpec((parts * depth, width), lambda i, place: (0, 0))] * shards
            + [pl.BlockSpec((tile, share), lambda i, place: (i, 0))] * groups
            + [pl.BlockSpec((tile, 1), lambda i, place: (i, 0)), by_row],
            out_specs=by_row,
            scratch_shapes=[pltpu.VMEM((groups, tile, share), jnp.bfloat16)],
        ),
        compiler_params=pltpu.CompilerParams(vmem_limit_bytes=48 * 2**20),
        cost_estimate=pl.CostEstimate(
            flops=2 * parts * depth * shards * rows * width,
            bytes_accessed=2 * parts * depth * shards * (rows + width) + 6 * rows * width,
            transcendentals=0,
        ),
        name="mix",
    )(jnp.stack([mine, own]), *(list(tokens) * shards), *cotangents, *pieces, gain, weight)


def gather(piece, axis):
    size = lax.axis_size(axis)
    pieces = {0: piece}
    bit = size // 2
    while bit:
        for k in sorted(pieces):
            pieces[k ^ bit] = swap(pieces[k], axis, bit)
        bit //= 2
    return [pieces[k] for k in range(size)]


def on_device(tokens, norm_gain, cotangent, layer_weight, shared_copy, master, momentum):
    tokens, cotangent, weight = tokens[0], cotangent[0], layer_weight[0]
    shards = lax.axis_size("fsdp")
    groups = lax.axis_size("replica")
    mine = lax.axis_index("fsdp")
    own = lax.axis_index("replica")
    rows, width = weight.shape
    inner_rate = inner_gain / math.sqrt(tokens.shape[0] * shards)

    scaled = scale_cotangent(tokens, cotangent)
    cotangents = gather(scaled, "fsdp")
    early, late = cut(tokens, shards, 2)
    early = lax.all_to_all(early, "fsdp", split_axis=0, concat_axis=0, tiled=True)
    first = [cotangents[1 << bit] for bit in range(shards.bit_length() - 1)]
    *_, late, coded_shared, coded_weight = lax.optimization_barrier((*first, late, shared_copy, weight))
    late = lax.all_to_all(late, "fsdp", split_axis=0, concat_axis=0, tiled=True)

    kept, sent = code_and_decode(own, coded_shared, coded_weight, groups)
    total = kept.astype(jnp.float32) + swap(sent, "replica", 1).astype(jnp.float32)
    bit = 2
    while bit < groups:
        sent = swap(total[1::2].astype(jnp.bfloat16), "replica", bit)
        total = total[0::2] + sent.astype(jnp.float32)
        bit *= 2
    average = total[0] / groups
    momentum_next = outer_beta * momentum + average
    master_next = master - outer_rate * (average + outer_beta * momentum_next)
    pieces = gather(master_next.astype(jnp.bfloat16), "replica")

    gain = lax.dynamic_slice_in_dim(norm_gain, mine * rows, rows).astype(jnp.float32)
    gain = (gain * ((1.0 - mix_weight) * inner_rate)).reshape(rows, 1)
    layer_next = mix(mine, own, (early, late), cotangents, pieces, gain, weight)
    return (layer_next[None], master_next, momentum_next)


def solution(mesh):
    in_specs = (
        P("replica", "fsdp", None),
        P(),
        P("replica", "fsdp", None),
        P("replica", "fsdp", None),
        P("fsdp", None),
        P("fsdp", "replica"),
        P("fsdp", "replica"),
    )
    out_specs = (P("replica", "fsdp", None), P("fsdp", "replica"), P("fsdp", "replica"))
    return jax.shard_map(
        on_device, mesh=mesh, in_specs=in_specs, out_specs=out_specs, check_vma=False
    )
```

```python
import functools
import math

import jax
import jax.numpy as jnp
from jax import lax
from jax.experimental import pallas as pl
from jax.experimental.pallas import tpu as pltpu
from jax.sharding import PartitionSpec as P

BLOCK = 64


norm_eps = 1e-05
inner_gain = 0.4
outer_rate = 0.7
outer_beta = 0.9
mix_weight = 0.5
code_range = 448.0


def swap(value, axis, mask):
    size = lax.axis_size(axis)
    return lax.ppermute(value, axis, [(i, i ^ mask) for i in range(size)])


def prepare_kernel(tokens_ref, cotangent_ref, blocks_ref, scaled_ref, inverse_ref, squares_ref):
    step, steps = pl.program_id(0), pl.num_programs(0)
    count, rows = tokens_ref.shape
    lanes = squares_ref.shape[1]
    blocks_ref[0] = tokens_ref[...]
    squares = jnp.zeros((count, lanes), jnp.float32)
    for start in range(0, rows, lanes):
        block = tokens_ref[:, start : start + lanes].astype(jnp.float32)
        squares = squares + block * block

    @pl.when(step == 0)
    def _():
        squares_ref[...] = squares

    @pl.when(step > 0)
    def _():
        squares_ref[...] += squares

    @pl.when(step == steps - 1)
    def _():
        mean = jnp.sum(squares_ref[...], axis=-1, keepdims=True) / (steps * rows)
        inverse = lax.rsqrt(mean + norm_eps)
        scaled_ref[...] = (cotangent_ref[...].astype(jnp.float32) * inverse).astype(jnp.bfloat16)
        inverse_ref[...] = jnp.transpose(jnp.broadcast_to(inverse, (count, lanes)))[: inverse_ref.shape[0]]


def prepare(tokens, cotangent, shards):
    count, features = tokens.shape
    width = cotangent.shape[1]
    rows = features // shards
    return pl.pallas_call(
        prepare_kernel,
        out_shape=(
            jax.ShapeDtypeStruct((shards, count, rows), jnp.bfloat16),
            jax.ShapeDtypeStruct((count, width), jnp.bfloat16),
            jax.ShapeDtypeStruct((8, count), jnp.float32),
        ),
        grid=(shards,),
        in_specs=[
            pl.BlockSpec((count, rows), lambda k: (0, k)),
            pl.BlockSpec((count, width), lambda k: (0, 0)),
        ],
        out_specs=(
            pl.BlockSpec((1, count, rows), lambda k: (k, 0, 0)),
            pl.BlockSpec((count, width), lambda k: (0, 0)),
            pl.BlockSpec((8, count), lambda k: (0, 0)),
        ),
        scratch_shapes=[pltpu.VMEM((count, 128), jnp.float32)],
        cost_estimate=pl.CostEstimate(
            flops=3 * count * features, bytes_accessed=4 * count * (features + width), transcendentals=count
        ),
        compiler_params=pltpu.CompilerParams(vmem_limit_bytes=12 * 2**20),
        name="prepare",
    )(tokens, cotangent)


def code_kernel(own_ref, shared_ref, weight_ref, kept_ref, sent_ref, decoded_ref):
    lanes = 2 * BLOCK
    groups, rows, share = decoded_ref.shape
    low = lax.broadcasted_iota(jnp.int32, (rows, lanes), 1) < BLOCK
    for start in range(0, groups * share, lanes):
        columns = slice(start, start + lanes)
        delta = shared_ref[:, columns].astype(jnp.float32) - weight_ref[:, columns].astype(jnp.float32)
        size = jnp.abs(delta)
        largest = jnp.where(
            low,
            jnp.max(jnp.where(low, size, 0.0), axis=-1, keepdims=True),
            jnp.max(jnp.where(low, 0.0, size), axis=-1, keepdims=True),
        )
        scale = ((largest + 1e-06) * (1.0 / code_range)).astype(jnp.bfloat16).astype(jnp.float32)
        coded = (delta * pl.reciprocal(scale)).astype(jnp.bfloat16)
        decoded = (coded.astype(jnp.float32) * scale).astype(jnp.bfloat16)
        piece = min(share, lanes)
        for at in range(0, lanes, piece):
            group, offset = divmod(start + at, share)
            decoded_ref[group, :, offset : offset + piece] = decoded[:, at : at + piece]
    own = own_ref[0]
    for k in range(0, groups, 2):
        kept_ref[k // 2] = decoded_ref[own ^ k]
        sent_ref[k // 2] = decoded_ref[own ^ (k + 1)]


def code_and_decode(own, shared, weight, groups):
    rows, width = shared.shape
    tile = min(rows, 128)
    share = width // groups
    spec = pl.BlockSpec((tile, width), lambda i, own: (i, 0))
    half = jax.ShapeDtypeStruct((groups // 2, rows, share), jnp.bfloat16)
    half_spec = pl.BlockSpec((groups // 2, tile, share), lambda i, own: (0, i, 0))
    return pl.pallas_call(
        code_kernel,
        out_shape=(half, half),
        grid_spec=pltpu.PrefetchScalarGridSpec(
            num_scalar_prefetch=1,
            grid=(rows // tile,),
            in_specs=[spec, spec],
            out_specs=(half_spec, half_spec),
            scratch_shapes=[pltpu.VMEM((groups, tile, share), jnp.bfloat16)],
        ),
        cost_estimate=pl.CostEstimate(flops=20 * rows * width, bytes_accessed=6 * rows * width, transcendentals=0),
        compiler_params=pltpu.CompilerParams(vmem_limit_bytes=12 * 2**20),
        name="code_and_decode",
    )(own.reshape(1), shared, weight)


def mix_kernel(parts, groups, place_ref, *refs):
    tokens, refs = refs[:parts], refs[parts:]
    cotangents, refs = refs[:parts], refs[parts:]
    pieces, refs = refs[:groups], refs[groups:]
    gain_ref, weight_ref, out_ref, shared_ref = refs
    total = None
    pair = 2 if parts % 2 == 0 else 1
    for first in range(0, parts, pair):
        product = lax.dot_general(
            jnp.concatenate([ref[0] for ref in tokens[first : first + pair]], axis=0),
            jnp.concatenate([ref[...] for ref in cotangents[first : first + pair]], axis=0),
            (((0,), (0,)), ((), ())),
            preferred_element_type=jnp.float32,
        )
        total = product if total is None else total + product
    own = place_ref[1]
    for k, piece in enumerate(pieces):
        shared_ref[own ^ k] = piece[...]
    share = shared_ref.shape[2]
    for group in range(groups):
        columns = slice(group * share, (group + 1) * share)
        weight = weight_ref[:, columns].astype(jnp.float32) + shared_ref[group].astype(jnp.float32)
        out_ref[:, columns] = (mix_weight * weight - gain_ref[...] * total[:, columns]).astype(jnp.bfloat16)


def mix(mine, own, tokens, cotangents, pieces, gain, weight):
    parts, depth, rows = tokens.shape
    width = weight.shape[1]
    groups = len(pieces)
    share = width // groups
    tile = min(rows, 256)

    def token_block(k):
        return pl.BlockSpec((1, depth, tile), lambda i, place: (place[0] ^ k, 0, i))

    by_row = pl.BlockSpec((tile, width), lambda i, place: (i, 0))
    return pl.pallas_call(
        functools.partial(mix_kernel, parts, groups),
        out_shape=jax.ShapeDtypeStruct((rows, width), jnp.bfloat16),
        grid_spec=pltpu.PrefetchScalarGridSpec(
            num_scalar_prefetch=1,
            grid=(rows // tile,),
            in_specs=[token_block(k) for k in range(parts)]
            + [pl.BlockSpec((depth, width), lambda i, place: (0, 0))] * parts
            + [pl.BlockSpec((tile, share), lambda i, place: (i, 0))] * groups
            + [pl.BlockSpec((tile, 1), lambda i, place: (i, 0)), by_row],
            out_specs=by_row,
            scratch_shapes=[pltpu.VMEM((groups, tile, share), jnp.bfloat16)],
        ),
        compiler_params=pltpu.CompilerParams(vmem_limit_bytes=20 * 2**20),
        cost_estimate=pl.CostEstimate(
            flops=2 * parts * depth * rows * width,
            bytes_accessed=2 * parts * depth * (rows + width) + 6 * rows * width,
            transcendentals=0,
        ),
        name="mix",
    )(jnp.stack([mine, own]), *([tokens] * parts), *cotangents, *pieces, gain, weight)


def gather(piece, axis, size, after=()):
    pieces = {0: piece}
    bit = size // 2
    while bit:
        if bit == 1 and after:
            (*held, _) = lax.optimization_barrier((*(pieces[k] for k in sorted(pieces)[1:]), after))
            pieces.update(zip(sorted(pieces)[1:], held))
        for k in sorted(pieces):
            pieces[k ^ bit] = swap(pieces[k], axis, bit)
        bit //= 2
    return [pieces[k] for k in range(size)]


def on_device(tokens, norm_gain, cotangent, layer_weight, shared_copy, master, momentum):
    tokens, cotangent, weight = tokens[0], cotangent[0], layer_weight[0]
    shards = lax.axis_size("fsdp")
    groups = lax.axis_size("replica")
    mine = lax.axis_index("fsdp")
    own = lax.axis_index("replica")
    rows, width = weight.shape
    inner_rate = inner_gain / math.sqrt(tokens.shape[0] * shards)

    half = shards // 2
    far = swap(cotangent, "fsdp", half)
    blocks, scaled, inverse = prepare(tokens, cotangent, shards)
    inverse = swap(inverse, "fsdp", half)
    near = gather(scaled, "fsdp", half)
    far, *near[1:3], blocks, coded_shared, coded_weight = lax.optimization_barrier(
        (far, *near[1:3], blocks, shared_copy, weight)
    )
    columns = lax.all_to_all(blocks, "fsdp", split_axis=0, concat_axis=0, tiled=True)
    far = (far.astype(jnp.float32) * inverse[0][:, None]).astype(jnp.bfloat16)
    cotangents = near + gather(far, "fsdp", half)

    kept, sent = code_and_decode(own, coded_shared, coded_weight, groups)
    total = kept.astype(jnp.float32) + swap(sent, "replica", 1).astype(jnp.float32)
    bit = 2
    while bit < groups:
        sent = swap(total[1::2].astype(jnp.bfloat16), "replica", bit)
        total = total[0::2] + sent.astype(jnp.float32)
        bit *= 2
    average = total[0] / groups
    momentum_next = outer_beta * momentum + average
    master_next = master - outer_rate * (average + outer_beta * momentum_next)
    pieces = gather(master_next.astype(jnp.bfloat16), "replica", groups, after=cotangents[:-1])

    gain = lax.dynamic_slice_in_dim(norm_gain, mine * rows, rows).astype(jnp.float32)
    gain = (gain * ((1.0 - mix_weight) * inner_rate)).reshape(rows, 1)
    layer_next = mix(mine, own, columns, cotangents, pieces, gain, weight)
    return (layer_next[None], master_next, momentum_next)


def solution(mesh):
    in_specs = (
        P("replica", "fsdp", None),
        P(),
        P("replica", "fsdp", None),
        P("replica", "fsdp", None),
        P("fsdp", None),
        P("fsdp", "replica"),
        P("fsdp", "replica"),
    )
    out_specs = (P("replica", "fsdp", None), P("fsdp", "replica"), P("fsdp", "replica"))
    return jax.shard_map(
        on_device, mesh=mesh, in_specs=in_specs, out_specs=out_specs, check_vma=False
    )
```

```python
import functools
import math

import jax
import jax.numpy as jnp
from jax import lax
from jax.experimental import pallas as pl
from jax.experimental.pallas import tpu as pltpu
from jax.sharding import PartitionSpec as P

BLOCK = 64


norm_eps = 1e-05
inner_gain = 0.4
outer_rate = 0.7
outer_beta = 0.9
mix_weight = 0.5
code_range = 448.0


def swap(value, axis, mask):
    size = lax.axis_size(axis)
    return lax.ppermute(value, axis, [(i, i ^ mask) for i in range(size)])


def prepare_kernel(tokens_ref, gain_ref, blocks_ref, inverse_ref):
    lanes = 128
    count, features = tokens_ref.shape
    rows = blocks_ref.shape[1]

    @pl.when(pl.program_id(0) == 0)
    def _():
        squares = jnp.zeros((count, lanes), jnp.float32)
        for start in range(0, features, lanes):
            block = tokens_ref[:, start : start + lanes].astype(jnp.float32)
            squares = squares + block * block
        mean = jnp.sum(squares, axis=-1, keepdims=True) / features
        inverse_ref[...] = jnp.broadcast_to(lax.rsqrt(mean + norm_eps), inverse_ref.shape)

    first = pl.program_id(0) * rows
    for start in range(0, rows, lanes):
        columns = pl.ds(pl.multiple_of(first + start, lanes), lanes)
        normed = tokens_ref[:, columns].astype(jnp.float32) * inverse_ref[...] * gain_ref[:, columns]
        blocks_ref[0, start : start + lanes] = jnp.transpose(normed).astype(jnp.bfloat16)


def prepare(tokens, gain, shards):
    count, features = tokens.shape
    rows = features // shards
    return pl.pallas_call(
        prepare_kernel,
        out_shape=jax.ShapeDtypeStruct((shards, rows, count), jnp.bfloat16),
        grid=(shards,),
        in_specs=[
            pl.BlockSpec((count, features), lambda k: (0, 0)),
            pl.BlockSpec((1, features), lambda k: (0, 0)),
        ],
        out_specs=pl.BlockSpec((1, rows, count), lambda k: (k, 0, 0)),
        scratch_shapes=[pltpu.VMEM((count, 128), jnp.float32)],
        cost_estimate=pl.CostEstimate(
            flops=5 * count * features, bytes_accessed=4 * count * features, transcendentals=count
        ),
        name="prepare",
    )(tokens, gain.astype(jnp.float32).reshape(1, features))


def code_kernel(own_ref, shared_ref, weight_ref, kept_ref, sent_ref, decoded_ref):
    lanes = 2 * BLOCK
    groups, rows, share = decoded_ref.shape
    low = lax.broadcasted_iota(jnp.int32, (rows, lanes), 1) < BLOCK
    for start in range(0, groups * share, lanes):
        columns = slice(start, start + lanes)
        delta = shared_ref[:, columns].astype(jnp.float32) - weight_ref[:, columns].astype(jnp.float32)
        size = jnp.abs(delta)
        largest = jnp.where(
            low,
            jnp.max(jnp.where(low, size, 0.0), axis=-1, keepdims=True),
            jnp.max(jnp.where(low, 0.0, size), axis=-1, keepdims=True),
        )
        scale = ((largest + 1e-06) * (1.0 / code_range)).astype(jnp.bfloat16).astype(jnp.float32)
        coded = (delta * pl.reciprocal(scale)).astype(jnp.bfloat16)
        decoded = (coded.astype(jnp.float32) * scale).astype(jnp.bfloat16)
        piece = min(share, lanes)
        for at in range(0, lanes, piece):
            group, offset = divmod(start + at, share)
            decoded_ref[group, :, offset : offset + piece] = decoded[:, at : at + piece]
    own = own_ref[0]
    for k in range(0, groups, 2):
        kept_ref[k // 2] = decoded_ref[own ^ k]
        sent_ref[k // 2] = decoded_ref[own ^ (k + 1)]


def code_and_decode(own, shared, weight, groups):
    rows, width = shared.shape
    tile = min(rows, 128)
    share = width // groups
    spec = pl.BlockSpec((tile, width), lambda i, own: (i, 0))
    half = jax.ShapeDtypeStruct((groups // 2, rows, share), jnp.bfloat16)
    half_spec = pl.BlockSpec((groups // 2, tile, share), lambda i, own: (0, i, 0))
    return pl.pallas_call(
        code_kernel,
        out_shape=(half, half),
        grid_spec=pltpu.PrefetchScalarGridSpec(
            num_scalar_prefetch=1,
            grid=(rows // tile,),
            in_specs=[spec, spec],
            out_specs=(half_spec, half_spec),
            scratch_shapes=[pltpu.VMEM((groups, tile, share), jnp.bfloat16)],
        ),
        cost_estimate=pl.CostEstimate(flops=20 * rows * width, bytes_accessed=6 * rows * width, transcendentals=0),
        name="code_and_decode",
    )(own.reshape(1), shared, weight)


def mix_kernel(shards, groups, rate, place_ref, *refs):
    tokens_ref, refs = refs[0], refs[1:]
    cotangent_refs, refs = refs[:shards], refs[shards:]
    piece_refs, refs = refs[:groups], refs[groups:]
    weight_ref, out_ref, refs = refs[0], refs[1], refs[2:]
    tokens, cotangents, pieces, weights, outs, token_sem, cotangent_sems, piece_sems, weight_sem, out_sems = refs
    mine, own = place_ref[0], place_ref[1]
    depth, width = cotangent_refs[0].shape
    share = pieces.shape[2]
    tile = outs.shape[2]

    def own_row(k):
        return pl.ds(pl.multiple_of((mine ^ k) * depth, depth), depth)

    loads = [pltpu.make_async_copy(tokens_ref, tokens, token_sem)]
    for k, ref in enumerate(cotangent_refs):
        loads.append(pltpu.make_async_copy(ref, cotangents.at[own_row(k)], cotangent_sems.at[k]))
    loads.append(pltpu.make_async_copy(weight_ref, weights, weight_sem))
    for k, ref in enumerate(piece_refs):
        loads.append(pltpu.make_async_copy(ref, pieces.at[own ^ k], piece_sems.at[k]))
    for load in loads:
        load.start()
    for load in loads[: 1 + shards]:
        load.wait()
    left = jnp.concatenate([tokens[k] for k in range(shards)], axis=1)
    stores = []
    for step in range(width // tile):
        columns = slice(step * tile, (step + 1) * tile)
        total = jnp.dot(left, cotangents[:, columns], preferred_element_type=jnp.float32)
        if step == 0:
            for load in loads[1 + shards :]:
                load.wait()
        for group in range(step * tile // share, (step + 1) * tile // share):
            place = slice(group * share, (group + 1) * share)
            part = slice(group * share - step * tile, (group + 1) * share - step * tile)
            mixed = weights[:, place].astype(jnp.float32) + pieces[group].astype(jnp.float32)
            outs[step, :, part] = (mix_weight * mixed - rate * total[:, part]).astype(jnp.bfloat16)
        stores.append(pltpu.make_async_copy(outs.at[step], out_ref.at[:, pl.ds(step * tile, tile)], out_sems.at[step]))
        stores[-1].start()
    for store in stores:
        store.wait()


def mix(mine, own, tokens, cotangents, pieces, weight, rate):
    shards, rows, depth = tokens.shape
    width = weight.shape[1]
    groups = len(pieces)
    share = width // groups
    tile = max(share, 256)
    return pl.pallas_call(
        functools.partial(mix_kernel, shards, groups, rate),
        out_shape=jax.ShapeDtypeStruct((rows, width), jnp.bfloat16),
        in_specs=[pl.BlockSpec(memory_space=pltpu.SMEM)]
        + [pl.BlockSpec(memory_space=pltpu.HBM)] * (2 + shards + groups),
        out_specs=pl.BlockSpec(memory_space=pltpu.HBM),
        scratch_shapes=[
            pltpu.VMEM((shards, rows, depth), jnp.bfloat16),
            pltpu.VMEM((shards * depth, width), jnp.bfloat16),
            pltpu.VMEM((groups, rows, share), jnp.bfloat16),
            pltpu.VMEM((rows, width), jnp.bfloat16),
            pltpu.VMEM((width // tile, rows, tile), jnp.bfloat16),
            pltpu.SemaphoreType.DMA,
            pltpu.SemaphoreType.DMA((shards,)),
            pltpu.SemaphoreType.DMA((groups,)),
            pltpu.SemaphoreType.DMA,
            pltpu.SemaphoreType.DMA((width // tile,)),
        ],
        compiler_params=pltpu.CompilerParams(vmem_limit_bytes=48 * 2**20),
        cost_estimate=pl.CostEstimate(
            flops=2 * depth * shards * rows * width,
            bytes_accessed=2 * depth * shards * (rows + width) + 6 * rows * width,
            transcendentals=0,
        ),
        name="mix",
    )(jnp.stack([mine, own]), tokens, *cotangents, *pieces, weight)


def gather(piece, axis, size, after=()):
    pieces = {0: piece}
    bit = size // 2
    while bit:
        if bit == 1 and after:
            (*held, _) = lax.optimization_barrier((*(pieces[k] for k in sorted(pieces)[1:]), after))
            pieces.update(zip(sorted(pieces)[1:], held))
        for k in sorted(pieces):
            pieces[k ^ bit] = swap(pieces[k], axis, bit)
        bit //= 2
    return [pieces[k] for k in range(size)]


def on_device(tokens, norm_gain, cotangent, layer_weight, shared_copy, master, momentum):
    tokens, cotangent, weight = tokens[0], cotangent[0], layer_weight[0]
    shards = lax.axis_size("fsdp")
    groups = lax.axis_size("replica")
    mine = lax.axis_index("fsdp")
    own = lax.axis_index("replica")
    rows, width = weight.shape
    inner_rate = inner_gain / math.sqrt(tokens.shape[0] * shards)

    own_exchanges = [1 << bit for bit in range(shards.bit_length() - 1)]
    cotangents = gather(cotangent, "fsdp", shards)
    blocks = prepare(tokens, norm_gain, shards)
    *_, blocks, coded_shared, coded_weight = lax.optimization_barrier(
        (*(cotangents[k] for k in own_exchanges), blocks, shared_copy, weight)
    )
    columns = lax.all_to_all(blocks, "fsdp", split_axis=0, concat_axis=0, tiled=True)

    kept, sent = code_and_decode(own, coded_shared, coded_weight, groups)
    total = kept.astype(jnp.float32) + swap(sent, "replica", 1).astype(jnp.float32)
    bit = 2
    while bit < groups:
        sent = swap(total[1::2].astype(jnp.bfloat16), "replica", bit)
        total = total[0::2] + sent.astype(jnp.float32)
        bit *= 2
    average = total[0] / groups
    momentum_next = outer_beta * momentum + average
    master_next = master - outer_rate * (average + outer_beta * momentum_next)
    pieces = gather(master_next.astype(jnp.bfloat16), "replica", groups, after=cotangents[:-1])

    layer_next = mix(mine, own, columns, cotangents, pieces, weight, (1.0 - mix_weight) * inner_rate)
    return (layer_next[None], master_next, momentum_next)


def solution(mesh):
    in_specs = (
        P("replica", "fsdp", None),
        P(),
        P("replica", "fsdp", None),
        P("replica", "fsdp", None),
        P("fsdp", None),
        P("fsdp", "replica"),
        P("fsdp", "replica"),
    )
    out_specs = (P("replica", "fsdp", None), P("fsdp", "replica"), P("fsdp", "replica"))
    return jax.shard_map(
        on_device, mesh=mesh, in_specs=in_specs, out_specs=out_specs, check_vma=False
    )
```

```python
import functools
import math

import jax
import jax.numpy as jnp
from jax import lax
from jax.experimental import pallas as pl
from jax.experimental.pallas import tpu as pltpu
from jax.sharding import PartitionSpec as P

BLOCK = 64


norm_eps = 1e-05
inner_gain = 0.4
outer_rate = 0.7
outer_beta = 0.9
mix_weight = 0.5
code_range = 448.0


def swap(value, axis, mask):
    size = lax.axis_size(axis)
    return lax.ppermute(value, axis, [(i, i ^ mask) for i in range(size)])


def prepare_kernel(tokens_ref, gain_ref, blocks_ref, tokens, blocks, load_sems, store_sems):
    lanes = 128
    shards, rows, count = blocks.shape
    features = shards * rows
    loads, stores = [], []
    for k in range(shards):
        columns = pl.ds(k * rows, rows)
        loads.append(pltpu.make_async_copy(tokens_ref.at[:, columns], tokens.at[:, columns], load_sems.at[k]))
        loads[k].start()
        stores.append(pltpu.make_async_copy(blocks.at[k], blocks_ref.at[k], store_sems.at[k]))
    squares = jnp.zeros((count, lanes), jnp.float32)
    for k in range(shards):
        loads[k].wait()
        for start in range(k * rows, (k + 1) * rows, lanes):
            block = tokens[:, start : start + lanes].astype(jnp.float32)
            squares = squares + block * block
    mean = jnp.sum(squares, axis=-1, keepdims=True) / features
    inverse = jnp.broadcast_to(lax.rsqrt(mean + norm_eps), (count, lanes))
    for k in range(shards):
        for start in range(0, rows, lanes):
            columns = slice(k * rows + start, k * rows + start + lanes)
            normed = tokens[:, columns].astype(jnp.float32) * inverse * gain_ref[:, columns]
            blocks[k, start : start + lanes] = jnp.transpose(normed).astype(jnp.bfloat16)
        stores[k].start()
    for store in stores:
        store.wait()


def prepare(tokens, gain, shards):
    count, features = tokens.shape
    rows = features // shards
    return pl.pallas_call(
        prepare_kernel,
        out_shape=jax.ShapeDtypeStruct((shards, rows, count), jnp.bfloat16),
        in_specs=[pl.BlockSpec(memory_space=pltpu.HBM), pl.BlockSpec(memory_space=pltpu.VMEM)],
        out_specs=pl.BlockSpec(memory_space=pltpu.HBM),
        scratch_shapes=[
            pltpu.VMEM((count, features), jnp.bfloat16),
            pltpu.VMEM((shards, rows, count), jnp.bfloat16),
            pltpu.SemaphoreType.DMA((shards,)),
            pltpu.SemaphoreType.DMA((shards,)),
        ],
        compiler_params=pltpu.CompilerParams(vmem_limit_bytes=16 * 2**20),
        cost_estimate=pl.CostEstimate(
            flops=5 * count * features, bytes_accessed=4 * count * features, transcendentals=count
        ),
        name="prepare",
    )(tokens, gain.astype(jnp.float32).reshape(1, features))


def code_kernel(own_ref, shared_ref, weight_ref, kept_ref, sent_ref, shared, weight, decoded, sems):
    lanes = 2 * BLOCK
    groups, tile, share = decoded.shape
    rows, width = shared.shape
    own = own_ref[0]
    low = lax.broadcasted_iota(jnp.int32, (tile, lanes), 1) < BLOCK

    def loads(i):
        part = pl.ds(pl.multiple_of(i * tile, tile), tile)
        return (
            pltpu.make_async_copy(shared_ref.at[part], shared.at[part], sems.at[0, i]),
            pltpu.make_async_copy(weight_ref.at[part], weight.at[part], sems.at[1, i]),
        )

    for i in range(rows // tile):
        for load in loads(i):
            load.start()

    def step(i, _):
        for load in loads(i):
            load.wait()
        part = pl.ds(pl.multiple_of(i * tile, tile), tile)
        for start in range(0, width, lanes):
            columns = slice(start, start + lanes)
            delta = shared[part, columns].astype(jnp.float32) - weight[part, columns].astype(jnp.float32)
            size = jnp.abs(delta)
            largest = jnp.where(
                low,
                jnp.max(jnp.where(low, size, 0.0), axis=-1, keepdims=True),
                jnp.max(jnp.where(low, 0.0, size), axis=-1, keepdims=True),
            )
            scale = ((largest + 1e-06) * (1.0 / code_range)).astype(jnp.bfloat16).astype(jnp.float32)
            coded = (delta * pl.reciprocal(scale)).astype(jnp.bfloat16)
            value = (coded.astype(jnp.float32) * scale).astype(jnp.bfloat16)
            piece = min(share, lanes)
            for at in range(0, lanes, piece):
                group, offset = divmod(start + at, share)
                decoded[group, :, offset : offset + piece] = value[:, at : at + piece]
        for k in range(0, groups, 2):
            kept_ref[k // 2, part] = decoded[own ^ k]
            sent_ref[k // 2, part] = decoded[own ^ (k + 1)]
        return 0

    lax.fori_loop(0, rows // tile, step, 0)


def code_and_decode(own, shared, weight, groups):
    rows, width = shared.shape
    tile = min(rows, 128)
    share = width // groups
    half = jax.ShapeDtypeStruct((groups // 2, rows, share), jnp.bfloat16)
    return pl.pallas_call(
        code_kernel,
        out_shape=(half, half),
        in_specs=[pl.BlockSpec(memory_space=pltpu.SMEM)] + [pl.BlockSpec(memory_space=pltpu.HBM)] * 2,
        out_specs=(pl.BlockSpec(memory_space=pltpu.VMEM),) * 2,
        scratch_shapes=[
            pltpu.VMEM((rows, width), jnp.bfloat16),
            pltpu.VMEM((rows, width), jnp.bfloat16),
            pltpu.VMEM((groups, tile, share), jnp.bfloat16),
            pltpu.SemaphoreType.DMA((2, rows // tile)),
        ],
        compiler_params=pltpu.CompilerParams(vmem_limit_bytes=16 * 2**20),
        cost_estimate=pl.CostEstimate(flops=20 * rows * width, bytes_accessed=6 * rows * width, transcendentals=0),
        name="code_and_decode",
    )(own.reshape(1), shared, weight)


def mix_kernel(shards, groups, rate, place_ref, *refs):
    tokens_ref, refs = refs[0], refs[1:]
    cotangent_refs, refs = refs[:shards], refs[shards:]
    piece_refs, refs = refs[:groups], refs[groups:]
    weight_ref, out_ref, cotangents, pieces, outs, out_sems = refs
    mine, own = place_ref[0], place_ref[1]
    depth, width = cotangent_refs[0].shape
    share = pieces.shape[2]
    tile = outs.shape[2]
    for k, ref in enumerate(cotangent_refs):
        cotangents[mine ^ k] = ref[...]
    for k, ref in enumerate(piece_refs):
        pieces[own ^ k] = ref[...]
    left = jnp.concatenate([tokens_ref[k] for k in range(shards)], axis=1)
    stores = []
    for step in range(width // tile):
        columns = slice(step * tile, (step + 1) * tile)
        right = jnp.concatenate([cotangents[k, :, columns] for k in range(shards)], axis=0)
        total = jnp.dot(left, right, preferred_element_type=jnp.float32)
        for group in range(step * tile // share, (step + 1) * tile // share):
            place = slice(group * share, (group + 1) * share)
            part = slice(group * share - step * tile, (group + 1) * share - step * tile)
            mixed = weight_ref[:, place].astype(jnp.float32) + pieces[group].astype(jnp.float32)
            outs[step, :, part] = (mix_weight * mixed - rate * total[:, part]).astype(jnp.bfloat16)
        stores.append(pltpu.make_async_copy(outs.at[step], out_ref.at[:, pl.ds(step * tile, tile)], out_sems.at[step]))
        stores[-1].start()
    for store in stores:
        store.wait()


def mix(mine, own, tokens, cotangents, pieces, weight, rate):
    shards, rows, depth = tokens.shape
    width = weight.shape[1]
    groups = len(pieces)
    share = width // groups
    tile = max(share, 256)
    return pl.pallas_call(
        functools.partial(mix_kernel, shards, groups, rate),
        out_shape=jax.ShapeDtypeStruct((rows, width), jnp.bfloat16),
        in_specs=[pl.BlockSpec(memory_space=pltpu.SMEM)]
        + [pl.BlockSpec(memory_space=pltpu.VMEM)] * (2 + shards + groups),
        out_specs=pl.BlockSpec(memory_space=pltpu.HBM),
        scratch_shapes=[
            pltpu.VMEM((shards, depth, width), jnp.bfloat16),
            pltpu.VMEM((groups, rows, share), jnp.bfloat16),
            pltpu.VMEM((width // tile, rows, tile), jnp.bfloat16),
            pltpu.SemaphoreType.DMA((width // tile,)),
        ],
        compiler_params=pltpu.CompilerParams(vmem_limit_bytes=24 * 2**20),
        cost_estimate=pl.CostEstimate(
            flops=2 * depth * shards * rows * width,
            bytes_accessed=2 * depth * shards * (rows + width) + 6 * rows * width,
            transcendentals=0,
        ),
        name="mix",
    )(jnp.stack([mine, own]), tokens, *cotangents, *pieces, weight)


def gather(piece, axis, size, after=()):
    pieces = {0: piece}
    bit = size // 2
    while bit:
        if bit == 1 and after:
            (*held, _) = lax.optimization_barrier((*(pieces[k] for k in sorted(pieces)[1:]), after))
            pieces.update(zip(sorted(pieces)[1:], held))
        for k in sorted(pieces):
            pieces[k ^ bit] = swap(pieces[k], axis, bit)
        bit //= 2
    return [pieces[k] for k in range(size)]


def on_device(tokens, norm_gain, cotangent, layer_weight, shared_copy, master, momentum):
    tokens, cotangent, weight = tokens[0], cotangent[0], layer_weight[0]
    shards = lax.axis_size("fsdp")
    groups = lax.axis_size("replica")
    mine = lax.axis_index("fsdp")
    own = lax.axis_index("replica")
    rows, width = weight.shape
    inner_rate = inner_gain / math.sqrt(tokens.shape[0] * shards)

    own_exchanges = [1 << bit for bit in range(shards.bit_length() - 1)]
    cotangents = gather(cotangent, "fsdp", shards)
    blocks = prepare(tokens, norm_gain, shards)
    *_, blocks, coded_shared, coded_weight = lax.optimization_barrier(
        (*(cotangents[k] for k in own_exchanges), blocks, shared_copy, weight)
    )
    columns = lax.all_to_all(blocks, "fsdp", split_axis=0, concat_axis=0, tiled=True)

    kept, sent = code_and_decode(own, coded_shared, coded_weight, groups)
    total = kept.astype(jnp.float32) + swap(sent, "replica", 1).astype(jnp.float32)
    bit = 2
    while bit < groups:
        sent = swap(total[1::2].astype(jnp.bfloat16), "replica", bit)
        bit *= 2
        if bit >= groups:
            *_, sent = lax.optimization_barrier((*cotangents[: shards // 2 + 2], sent))
        total = total[0::2] + sent.astype(jnp.float32)
    average = total[0] / groups
    momentum_next = outer_beta * momentum + average
    master_next = master - outer_rate * (average + outer_beta * momentum_next)
    pieces = gather(master_next.astype(jnp.bfloat16), "replica", groups, after=cotangents)

    layer_next = mix(mine, own, columns, cotangents, pieces, weight, (1.0 - mix_weight) * inner_rate)
    return (layer_next[None], master_next, momentum_next)


def solution(mesh):
    in_specs = (
        P("replica", "fsdp", None),
        P(),
        P("replica", "fsdp", None),
        P("replica", "fsdp", None),
        P("fsdp", None),
        P("fsdp", "replica"),
        P("fsdp", "replica"),
    )
    out_specs = (P("replica", "fsdp", None), P("fsdp", "replica"), P("fsdp", "replica"))
    return jax.shard_map(
        on_device, mesh=mesh, in_specs=in_specs, out_specs=out_specs, check_vma=False
    )
```

```python
import functools
import math

import jax
import jax.numpy as jnp
from jax import lax
from jax.experimental import pallas as pl
from jax.experimental.pallas import tpu as pltpu
from jax.sharding import PartitionSpec as P

BLOCK = 64


norm_eps = 1e-05
inner_gain = 0.4
outer_rate = 0.7
outer_beta = 0.9
mix_weight = 0.5
code_range = 448.0


def swap(value, axis, mask):
    size = lax.axis_size(axis)
    return lax.ppermute(value, axis, [(i, i ^ mask) for i in range(size)])


def prepare_kernel(tokens_ref, gain_ref, blocks_ref, tokens, blocks, load_sems, store_sems):
    lanes = 128
    shards, rows, count = blocks.shape
    features = shards * rows
    loads, stores = [], []
    for k in range(shards):
        columns = pl.ds(k * rows, rows)
        loads.append(pltpu.make_async_copy(tokens_ref.at[:, columns], tokens.at[:, columns], load_sems.at[k]))
        loads[k].start()
        stores.append(pltpu.make_async_copy(blocks.at[k], blocks_ref.at[k], store_sems.at[k]))
    squares = jnp.zeros((count, lanes), jnp.float32)
    for k in range(shards):
        loads[k].wait()
        for start in range(k * rows, (k + 1) * rows, lanes):
            block = tokens[:, start : start + lanes].astype(jnp.float32)
            squares = squares + block * block
    mean = jnp.sum(squares, axis=-1, keepdims=True) / features
    inverse = jnp.broadcast_to(lax.rsqrt(mean + norm_eps), (count, lanes))
    for k in range(shards):
        for start in range(0, rows, lanes):
            columns = slice(k * rows + start, k * rows + start + lanes)
            normed = tokens[:, columns].astype(jnp.float32) * inverse * gain_ref[:, columns]
            blocks[k, start : start + lanes] = jnp.transpose(normed).astype(jnp.bfloat16)
        stores[k].start()
    for store in stores:
        store.wait()


def prepare(tokens, gain, shards):
    count, features = tokens.shape
    rows = features // shards
    return pl.pallas_call(
        prepare_kernel,
        out_shape=jax.ShapeDtypeStruct((shards, rows, count), jnp.bfloat16),
        in_specs=[pl.BlockSpec(memory_space=pltpu.HBM), pl.BlockSpec(memory_space=pltpu.VMEM)],
        out_specs=pl.BlockSpec(memory_space=pltpu.HBM),
        scratch_shapes=[
            pltpu.VMEM((count, features), jnp.bfloat16),
            pltpu.VMEM((shards, rows, count), jnp.bfloat16),
            pltpu.SemaphoreType.DMA((shards,)),
            pltpu.SemaphoreType.DMA((shards,)),
        ],
        compiler_params=pltpu.CompilerParams(vmem_limit_bytes=16 * 2**20),
        cost_estimate=pl.CostEstimate(
            flops=5 * count * features, bytes_accessed=4 * count * features, transcendentals=count
        ),
        name="prepare",
    )(tokens, gain.astype(jnp.float32).reshape(1, features))


def code_kernel(own_ref, shared_ref, weight_ref, kept_ref, sent_ref, shared, weight, decoded, sems):
    lanes = 2 * BLOCK
    groups, tile, share = decoded.shape
    rows, width = shared.shape
    own = own_ref[0]
    low = lax.broadcasted_iota(jnp.int32, (tile, lanes), 1) < BLOCK

    def loads(i):
        part = pl.ds(pl.multiple_of(i * tile, tile), tile)
        return (
            pltpu.make_async_copy(shared_ref.at[part], shared.at[part], sems.at[0, i]),
            pltpu.make_async_copy(weight_ref.at[part], weight.at[part], sems.at[1, i]),
        )

    for i in range(rows // tile):
        for load in loads(i):
            load.start()

    def step(i, _):
        for load in loads(i):
            load.wait()
        part = pl.ds(pl.multiple_of(i * tile, tile), tile)
        for start in range(0, width, lanes):
            columns = slice(start, start + lanes)
            delta = shared[part, columns].astype(jnp.float32) - weight[part, columns].astype(jnp.float32)
            size = jnp.abs(delta)
            largest = jnp.where(
                low,
                jnp.max(jnp.where(low, size, 0.0), axis=-1, keepdims=True),
                jnp.max(jnp.where(low, 0.0, size), axis=-1, keepdims=True),
            )
            scale = ((largest + 1e-06) * (1.0 / code_range)).astype(jnp.bfloat16).astype(jnp.float32)
            coded = (delta * pl.reciprocal(scale)).astype(jnp.bfloat16)
            value = (coded.astype(jnp.float32) * scale).astype(jnp.bfloat16)
            piece = min(share, lanes)
            for at in range(0, lanes, piece):
                group, offset = divmod(start + at, share)
                decoded[group, :, offset : offset + piece] = value[:, at : at + piece]
        for k in range(0, groups, 2):
            kept_ref[k // 2, part] = decoded[own ^ k]
            sent_ref[k // 2, part] = decoded[own ^ (k + 1)]
        return 0

    lax.fori_loop(0, rows // tile, step, 0)


def code_and_decode(own, shared, weight, groups):
    rows, width = shared.shape
    tile = min(rows, 128)
    share = width // groups
    half = jax.ShapeDtypeStruct((groups // 2, rows, share), jnp.bfloat16)
    return pl.pallas_call(
        code_kernel,
        out_shape=(half, half),
        in_specs=[pl.BlockSpec(memory_space=pltpu.SMEM)] + [pl.BlockSpec(memory_space=pltpu.HBM)] * 2,
        out_specs=(pl.BlockSpec(memory_space=pltpu.VMEM),) * 2,
        scratch_shapes=[
            pltpu.VMEM((rows, width), jnp.bfloat16),
            pltpu.VMEM((rows, width), jnp.bfloat16),
            pltpu.VMEM((groups, tile, share), jnp.bfloat16),
            pltpu.SemaphoreType.DMA((2, rows // tile)),
        ],
        compiler_params=pltpu.CompilerParams(vmem_limit_bytes=16 * 2**20),
        cost_estimate=pl.CostEstimate(flops=20 * rows * width, bytes_accessed=6 * rows * width, transcendentals=0),
        name="code_and_decode",
    )(own.reshape(1), shared, weight)


def mix_kernel(shards, groups, rate, place_ref, *refs):
    tokens_ref, refs = refs[0], refs[1:]
    cotangent_refs, refs = refs[:shards], refs[shards:]
    piece_refs, refs = refs[:groups], refs[groups:]
    weight_ref, out_ref, refs = refs[0], refs[1], refs[2:]
    tokens, cotangents, pieces, weights, totals, outs, token_sems, cotangent_sems, piece_sems, weight_sem, out_sems = refs
    mine, own = place_ref[0], place_ref[1]
    depth, width = cotangent_refs[0].shape
    share = pieces.shape[2]
    steps, _, tile = outs.shape

    first = [pltpu.make_async_copy(tokens_ref.at[k], tokens.at[k], token_sems.at[k]) for k in range(shards)]
    for k, ref in enumerate(cotangent_refs):
        row = pl.ds(pl.multiple_of((mine ^ k) * depth, depth), depth)
        first.append(pltpu.make_async_copy(ref, cotangents.at[row], cotangent_sems.at[k]))
    second = [pltpu.make_async_copy(weight_ref, weights, weight_sem)]
    for k, ref in enumerate(piece_refs):
        second.append(pltpu.make_async_copy(ref, pieces.at[own ^ k], piece_sems.at[k]))
    for load in first:
        load.start()
    for load in first:
        load.wait()
    for load in second:
        load.start()
    left = jnp.concatenate([tokens[k] for k in range(shards)], axis=1)
    stores = [
        pltpu.make_async_copy(outs.at[step], out_ref.at[:, pl.ds(step * tile, tile)], out_sems.at[step])
        for step in range(steps)
    ]
    ahead = min(2, steps)
    for step in range(steps + ahead):
        if step < steps:
            columns = slice(step * tile, (step + 1) * tile)
            totals[step] = jnp.dot(left, cotangents[:, columns], preferred_element_type=jnp.float32)
        done = step - ahead
        if done < 0:
            continue
        if done == 0:
            for load in second:
                load.wait()
        for group in range(done * tile // share, (done + 1) * tile // share):
            place = slice(group * share, (group + 1) * share)
            part = slice(group * share - done * tile, (group + 1) * share - done * tile)
            mixed = weights[:, place].astype(jnp.float32) + pieces[group].astype(jnp.float32)
            outs[done, :, part] = (mix_weight * mixed - rate * totals[done, :, part]).astype(jnp.bfloat16)
        stores[done].start()
    for store in stores:
        store.wait()


def mix(mine, own, tokens, cotangents, pieces, weight, rate):
    shards, rows, depth = tokens.shape
    width = weight.shape[1]
    groups = len(pieces)
    share = width // groups
    tile = max(share, 256)
    return pl.pallas_call(
        functools.partial(mix_kernel, shards, groups, rate),
        out_shape=jax.ShapeDtypeStruct((rows, width), jnp.bfloat16),
        in_specs=[pl.BlockSpec(memory_space=pltpu.SMEM)]
        + [pl.BlockSpec(memory_space=pltpu.HBM)] * (2 + shards + groups),
        out_specs=pl.BlockSpec(memory_space=pltpu.HBM),
        scratch_shapes=[
            pltpu.VMEM((shards, rows, depth), jnp.bfloat16),
            pltpu.VMEM((shards * depth, width), jnp.bfloat16),
            pltpu.VMEM((groups, rows, share), jnp.bfloat16),
            pltpu.VMEM((rows, width), jnp.bfloat16),
            pltpu.VMEM((width // tile, rows, tile), jnp.float32),
            pltpu.VMEM((width // tile, rows, tile), jnp.bfloat16),
            pltpu.SemaphoreType.DMA((shards,)),
            pltpu.SemaphoreType.DMA((shards,)),
            pltpu.SemaphoreType.DMA((groups,)),
            pltpu.SemaphoreType.DMA,
            pltpu.SemaphoreType.DMA((width // tile,)),
        ],
        compiler_params=pltpu.CompilerParams(vmem_limit_bytes=44 * 2**20),
        cost_estimate=pl.CostEstimate(
            flops=2 * depth * shards * rows * width,
            bytes_accessed=2 * depth * shards * (rows + width) + 6 * rows * width,
            transcendentals=0,
        ),
        name="mix",
    )(jnp.stack([mine, own]), tokens, *cotangents, *pieces, weight)


def gather(piece, axis, size, after=()):
    pieces = {0: piece}
    bit = size // 2
    while bit:
        if bit == 1 and after:
            (*held, _) = lax.optimization_barrier((*(pieces[k] for k in sorted(pieces)[1:]), after))
            pieces.update(zip(sorted(pieces)[1:], held))
        for k in sorted(pieces):
            pieces[k ^ bit] = swap(pieces[k], axis, bit)
        bit //= 2
    return [pieces[k] for k in range(size)]


def on_device(tokens, norm_gain, cotangent, layer_weight, shared_copy, master, momentum):
    tokens, cotangent, weight = tokens[0], cotangent[0], layer_weight[0]
    shards = lax.axis_size("fsdp")
    groups = lax.axis_size("replica")
    mine = lax.axis_index("fsdp")
    own = lax.axis_index("replica")
    rows, width = weight.shape
    inner_rate = inner_gain / math.sqrt(tokens.shape[0] * shards)

    cotangents = gather(cotangent, "fsdp", shards)
    blocks = prepare(tokens, norm_gain, shards)
    *_, blocks, coded_shared, coded_weight = lax.optimization_barrier(
        (*cotangents[: shards // 2 + 1], blocks, shared_copy, weight)
    )
    columns = lax.all_to_all(blocks, "fsdp", split_axis=0, concat_axis=0, tiled=True)

    kept, sent = code_and_decode(own, coded_shared, coded_weight, groups)
    total = kept.astype(jnp.float32) + swap(sent, "replica", 1).astype(jnp.float32)
    bit = 2
    while bit < groups:
        sent = swap(total[1::2].astype(jnp.bfloat16), "replica", bit)
        bit *= 2
        total = total[0::2] + sent.astype(jnp.float32)
    average = total[0] / groups
    momentum_next = outer_beta * momentum + average
    master_next = master - outer_rate * (average + outer_beta * momentum_next)
    pieces = gather(master_next.astype(jnp.bfloat16), "replica", groups, after=cotangents[:-1])

    layer_next = mix(mine, own, columns, cotangents, pieces, weight, (1.0 - mix_weight) * inner_rate)
    return (layer_next[None], master_next, momentum_next)


def solution(mesh):
    in_specs = (
        P("replica", "fsdp", None),
        P(),
        P("replica", "fsdp", None),
        P("replica", "fsdp", None),
        P("fsdp", None),
        P("fsdp", "replica"),
        P("fsdp", "replica"),
    )
    out_specs = (P("replica", "fsdp", None), P("fsdp", "replica"), P("fsdp", "replica"))
    return jax.shard_map(
        on_device, mesh=mesh, in_specs=in_specs, out_specs=out_specs, check_vma=False
    )
```

```python
import functools
import math

import jax
import jax.numpy as jnp
from jax import lax
from jax.experimental import pallas as pl
from jax.experimental.pallas import tpu as pltpu
from jax.sharding import PartitionSpec as P

BLOCK = 64


norm_eps = 1e-05
inner_gain = 0.4
outer_rate = 0.7
outer_beta = 0.9
mix_weight = 0.5
code_range = 448.0


def swap(value, axis, mask):
    size = lax.axis_size(axis)
    return lax.ppermute(value, axis, [(i, i ^ mask) for i in range(size)])


def prepare_kernel(tokens_ref, gain_ref, blocks_ref, tokens, blocks, load_sems, store_sems):
    lanes = 128
    shards, rows, count = blocks.shape
    features = shards * rows
    loads, stores = [], []
    for k in range(shards):
        columns = pl.ds(k * rows, rows)
        loads.append(pltpu.make_async_copy(tokens_ref.at[:, columns], tokens.at[:, columns], load_sems.at[k]))
        loads[k].start()
        stores.append(pltpu.make_async_copy(blocks.at[k], blocks_ref.at[k], store_sems.at[k]))
    squares = jnp.zeros((count, lanes), jnp.float32)
    for k in range(shards):
        loads[k].wait()
        for start in range(k * rows, (k + 1) * rows, lanes):
            block = tokens[:, start : start + lanes].astype(jnp.float32)
            squares = squares + block * block
    mean = jnp.sum(squares, axis=-1, keepdims=True) / features
    inverse = jnp.broadcast_to(lax.rsqrt(mean + norm_eps), (count, lanes))
    for k in range(shards):
        for start in range(0, rows, lanes):
            columns = slice(k * rows + start, k * rows + start + lanes)
            normed = tokens[:, columns].astype(jnp.float32) * inverse * gain_ref[:, columns]
            blocks[k, start : start + lanes] = jnp.transpose(normed).astype(jnp.bfloat16)
        stores[k].start()
    for store in stores:
        store.wait()


def prepare(tokens, gain, shards):
    count, features = tokens.shape
    rows = features // shards
    return pl.pallas_call(
        prepare_kernel,
        out_shape=jax.ShapeDtypeStruct((shards, rows, count), jnp.bfloat16),
        in_specs=[pl.BlockSpec(memory_space=pltpu.HBM), pl.BlockSpec(memory_space=pltpu.VMEM)],
        out_specs=pl.BlockSpec(memory_space=pltpu.HBM),
        scratch_shapes=[
            pltpu.VMEM((count, features), jnp.bfloat16),
            pltpu.VMEM((shards, rows, count), jnp.bfloat16),
            pltpu.SemaphoreType.DMA((shards,)),
            pltpu.SemaphoreType.DMA((shards,)),
        ],
        compiler_params=pltpu.CompilerParams(vmem_limit_bytes=16 * 2**20),
        cost_estimate=pl.CostEstimate(
            flops=5 * count * features, bytes_accessed=4 * count * features, transcendentals=count
        ),
        name="prepare",
    )(tokens, gain.astype(jnp.float32).reshape(1, features))


def code_kernel(own_ref, shared_ref, weight_ref, kept_ref, sent_ref, shared, weight, decoded, sems):
    lanes = 2 * BLOCK
    groups, tile, share = decoded.shape
    rows, width = shared.shape
    own = own_ref[0]
    low = lax.broadcasted_iota(jnp.int32, (tile, lanes), 1) < BLOCK

    def loads(i):
        part = pl.ds(pl.multiple_of(i * tile, tile), tile)
        return (
            pltpu.make_async_copy(shared_ref.at[part], shared.at[part], sems.at[0, i]),
            pltpu.make_async_copy(weight_ref.at[part], weight.at[part], sems.at[1, i]),
        )

    for i in range(rows // tile):
        for load in loads(i):
            load.start()

    def step(i, _):
        for load in loads(i):
            load.wait()
        part = pl.ds(pl.multiple_of(i * tile, tile), tile)
        for start in range(0, width, lanes):
            columns = slice(start, start + lanes)
            delta = shared[part, columns].astype(jnp.float32) - weight[part, columns].astype(jnp.float32)
            size = jnp.abs(delta)
            largest = jnp.where(
                low,
                jnp.max(jnp.where(low, size, 0.0), axis=-1, keepdims=True),
                jnp.max(jnp.where(low, 0.0, size), axis=-1, keepdims=True),
            )
            scale = ((largest + 1e-06) * (1.0 / code_range)).astype(jnp.bfloat16).astype(jnp.float32)
            coded = (delta * pl.reciprocal(scale)).astype(jnp.bfloat16)
            value = (coded.astype(jnp.float32) * scale).astype(jnp.bfloat16)
            piece = min(share, lanes)
            for at in range(0, lanes, piece):
                group, offset = divmod(start + at, share)
                decoded[group, :, offset : offset + piece] = value[:, at : at + piece]
        for k in range(0, groups, 2):
            kept_ref[k // 2, part] = decoded[own ^ k]
            sent_ref[k // 2, part] = decoded[own ^ (k + 1)]
        return 0

    lax.fori_loop(0, rows // tile, step, 0)


def code_and_decode(own, shared, weight, groups):
    rows, width = shared.shape
    tile = min(rows, 128)
    share = width // groups
    half = jax.ShapeDtypeStruct((groups // 2, rows, share), jnp.bfloat16)
    return pl.pallas_call(
        code_kernel,
        out_shape=(half, half),
        in_specs=[pl.BlockSpec(memory_space=pltpu.SMEM)] + [pl.BlockSpec(memory_space=pltpu.HBM)] * 2,
        out_specs=(pl.BlockSpec(memory_space=pltpu.VMEM),) * 2,
        scratch_shapes=[
            pltpu.VMEM((rows, width), jnp.bfloat16),
            pltpu.VMEM((rows, width), jnp.bfloat16),
            pltpu.VMEM((groups, tile, share), jnp.bfloat16),
            pltpu.SemaphoreType.DMA((2, rows // tile)),
        ],
        compiler_params=pltpu.CompilerParams(vmem_limit_bytes=16 * 2**20),
        cost_estimate=pl.CostEstimate(flops=20 * rows * width, bytes_accessed=360 * rows * width, transcendentals=0),
        name="code_and_decode",
    )(own.reshape(1), shared, weight)


def stage_kernel(*refs):
    *part_refs, out_ref, sems = refs
    depth = part_refs[0].shape[0]
    loads = [
        pltpu.make_async_copy(ref, out_ref.at[pl.ds(k * depth, depth)], sems.at[k]) for k, ref in enumerate(part_refs)
    ]
    for load in loads:
        load.start()
    for load in loads:
        load.wait()


def stage(parts):
    depth, width = parts[0].shape
    return pl.pallas_call(
        stage_kernel,
        out_shape=jax.ShapeDtypeStruct((len(parts) * depth, width), parts[0].dtype),
        in_specs=[pl.BlockSpec(memory_space=pltpu.HBM)] * len(parts),
        out_specs=pl.BlockSpec(memory_space=pltpu.VMEM),
        scratch_shapes=[pltpu.SemaphoreType.DMA((len(parts),))],
        compiler_params=pltpu.CompilerParams(vmem_limit_bytes=16 * 2**20),
        cost_estimate=pl.CostEstimate(flops=0, bytes_accessed=4 * len(parts) * depth * width, transcendentals=0),
        name="stage",
    )(*parts)


def accumulate_kernel(groups, rate, place_ref, cotangent_ref, tokens_ref, weight_ref, *refs):
    piece_refs, refs = refs[:groups], refs[groups:]
    total_ref, last_ref, tokens, weight, pieces, token_sems, weight_sem, piece_sems, last_sem = refs
    mine, own = place_ref[0], place_ref[1]
    parts, rows, depth = tokens.shape
    width = total_ref.shape[1]
    share = pieces.shape[2]
    tile = max(share, 256)
    loads = [pltpu.make_async_copy(tokens_ref.at[mine ^ k], tokens.at[k], token_sems.at[k]) for k in range(parts)]
    rest = [pltpu.make_async_copy(weight_ref, weight, weight_sem)]
    for k, ref in enumerate(piece_refs):
        rest.append(pltpu.make_async_copy(ref, pieces.at[own ^ k], piece_sems.at[k]))
    rest.append(pltpu.make_async_copy(tokens_ref.at[mine ^ parts], last_ref, last_sem))
    for load in loads + rest:
        load.start()
    for load in loads:
        load.wait()
    left = jnp.concatenate([tokens[k] for k in range(parts)], axis=1)
    for start in range(0, width, tile):
        product = jnp.dot(left, cotangent_ref[:, start : start + tile], preferred_element_type=jnp.float32)
        if start == 0:
            for load in rest:
                load.wait()
        for group in range(start // share, (start + tile) // share):
            columns = slice(group * share, (group + 1) * share)
            mixed = weight[:, columns].astype(jnp.float32) + pieces[group].astype(jnp.float32)
            part = slice(group * share - start, (group + 1) * share - start)
            total_ref[:, columns] = mix_weight * mixed - rate * product[:, part]


def accumulate(mine, own, cotangents, tokens, weight, pieces, rate):
    shards, rows, depth = tokens.shape
    width = weight.shape[1]
    groups = len(pieces)
    parts = shards - 1
    return pl.pallas_call(
        functools.partial(accumulate_kernel, groups, rate),
        out_shape=(jax.ShapeDtypeStruct((rows, width), jnp.float32), jax.ShapeDtypeStruct((rows, depth), jnp.bfloat16)),
        in_specs=[pl.BlockSpec(memory_space=pltpu.SMEM), pl.BlockSpec(memory_space=pltpu.VMEM)]
        + [pl.BlockSpec(memory_space=pltpu.HBM)] * (2 + groups),
        out_specs=(pl.BlockSpec(memory_space=pltpu.VMEM),) * 2,
        scratch_shapes=[
            pltpu.VMEM((parts, rows, depth), jnp.bfloat16),
            pltpu.VMEM((rows, width), jnp.bfloat16),
            pltpu.VMEM((groups, rows, width // groups), jnp.bfloat16),
            pltpu.SemaphoreType.DMA((parts,)),
            pltpu.SemaphoreType.DMA,
            pltpu.SemaphoreType.DMA((groups,)),
            pltpu.SemaphoreType.DMA,
        ],
        compiler_params=pltpu.CompilerParams(vmem_limit_bytes=36 * 2**20),
        cost_estimate=pl.CostEstimate(
            flops=2 * parts * depth * rows * width,
            bytes_accessed=2 * parts * depth * (rows + width) + 8 * rows * width,
            transcendentals=0,
        ),
        name="accumulate",
    )(jnp.stack([mine, own]), cotangents, tokens, weight, *pieces)


def finish_kernel(rate, tokens_ref, cotangent_ref, total_ref, out_ref, outs, sems):
    steps, _, tile = outs.shape
    stores = []
    for step in range(steps):
        columns = slice(step * tile, (step + 1) * tile)
        product = jnp.dot(tokens_ref[...], cotangent_ref[:, columns], preferred_element_type=jnp.float32)
        outs[step] = (total_ref[:, columns] - rate * product).astype(jnp.bfloat16)
        stores.append(pltpu.make_async_copy(outs.at[step], out_ref.at[:, pl.ds(step * tile, tile)], sems.at[step]))
        stores[step].start()
    for store in stores:
        store.wait()


def finish(tokens, cotangent, total, rate):
    rows, width = total.shape
    depth = tokens.shape[1]
    tile = min(width, 256)
    return pl.pallas_call(
        functools.partial(finish_kernel, rate),
        out_shape=jax.ShapeDtypeStruct((rows, width), jnp.bfloat16),
        in_specs=[pl.BlockSpec(memory_space=pltpu.VMEM)] * 3,
        out_specs=pl.BlockSpec(memory_space=pltpu.HBM),
        scratch_shapes=[pltpu.VMEM((width // tile, rows, tile), jnp.bfloat16), pltpu.SemaphoreType.DMA((width // tile,))],
        compiler_params=pltpu.CompilerParams(vmem_limit_bytes=16 * 2**20),
        cost_estimate=pl.CostEstimate(
            flops=2 * depth * rows * width, bytes_accessed=2 * depth * (rows + width) + 6 * rows * width, transcendentals=0
        ),
        name="finish",
    )(tokens, cotangent, total)


def gather(piece, axis, size):
    pieces = {0: piece}
    bit = size // 2
    while bit:
        for k in sorted(pieces):
            pieces[k ^ bit] = swap(pieces[k], axis, bit)
        bit //= 2
    return [pieces[k] for k in range(size)]


def on_device(tokens, norm_gain, cotangent, layer_weight, shared_copy, master, momentum):
    tokens, cotangent, weight = tokens[0], cotangent[0], layer_weight[0]
    shards = lax.axis_size("fsdp")
    groups = lax.axis_size("replica")
    mine = lax.axis_index("fsdp")
    own = lax.axis_index("replica")
    rows, width = weight.shape
    inner_rate = inner_gain / math.sqrt(tokens.shape[0] * shards)

    rate = (1.0 - mix_weight) * inner_rate

    cotangents = gather(cotangent, "fsdp", shards)
    blocks = prepare(tokens, norm_gain, shards)
    columns = lax.all_to_all(blocks, "fsdp", split_axis=0, concat_axis=0, tiled=True)
    first = [cotangents[1 << bit] for bit in range(shards.bit_length() - 1)]
    *_, coded_shared, coded_weight = lax.optimization_barrier((*first, blocks, shared_copy, weight))

    kept, sent = code_and_decode(own, coded_shared, coded_weight, groups)
    total = kept.astype(jnp.float32) + swap(sent, "replica", 1).astype(jnp.float32)
    bit = 2
    while bit < groups:
        sent = swap(total[1::2].astype(jnp.bfloat16), "replica", bit)
        bit *= 2
        total = total[0::2] + sent.astype(jnp.float32)
    average = total[0] / groups
    momentum_next = outer_beta * momentum + average
    master_next = master - outer_rate * (average + outer_beta * momentum_next)
    pieces = gather(master_next.astype(jnp.bfloat16), "replica", groups)

    total, last = accumulate(mine, own, stage(cotangents[:-1]), columns, weight, pieces, rate)
    layer_next = finish(last, cotangents[-1], total, rate)
    return (layer_next[None], master_next, momentum_next)


def solution(mesh):
    in_specs = (
        P("replica", "fsdp", None),
        P(),
        P("replica", "fsdp", None),
        P("replica", "fsdp", None),
        P("fsdp", None),
        P("fsdp", "replica"),
        P("fsdp", "replica"),
    )
    out_specs = (P("replica", "fsdp", None), P("fsdp", "replica"), P("fsdp", "replica"))
    return jax.shard_map(
        on_device, mesh=mesh, in_specs=in_specs, out_specs=out_specs, check_vma=False
    )
```

```python
import functools
import math

import jax
import jax.numpy as jnp
from jax import lax
from jax.experimental import pallas as pl
from jax.experimental.pallas import tpu as pltpu
from jax.sharding import PartitionSpec as P

BLOCK = 64


norm_eps = 1e-05
inner_gain = 0.4
outer_rate = 0.7
outer_beta = 0.9
mix_weight = 0.5
code_range = 448.0


def swap(value, axis, mask):
    size = lax.axis_size(axis)
    return lax.ppermute(value, axis, [(i, i ^ mask) for i in range(size)])


def prepare_kernel(shards, skip, mine_ref, tokens_ref, gain_ref, group_ref, *refs):
    other_refs, (tokens, group, load_sems, store_sems) = refs[: shards // 2], refs[shards // 2 :]
    lanes = 128
    rows, count = other_refs[0].shape
    features = shards * rows
    mine = mine_ref[0]
    loads = []
    for k in range(shards):
        columns = pl.ds(k * rows, rows)
        loads.append(pltpu.make_async_copy(tokens_ref.at[:, columns], tokens.at[:, columns], load_sems.at[k]))
        loads[k].start()
    squares = jnp.zeros((count, lanes), jnp.float32)
    for k in range(shards):
        loads[k].wait()
        for start in range(k * rows, (k + 1) * rows, lanes):
            block = tokens[:, start : start + lanes].astype(jnp.float32)
            squares = squares + block * block
    mean = jnp.sum(squares, axis=-1, keepdims=True) / features
    inverse = jnp.broadcast_to(lax.rsqrt(mean + norm_eps), (count, lanes))

    def write(ref, shard):
        for start in range(0, rows, lanes):
            columns = pl.ds(pl.multiple_of(shard * rows + start, lanes), lanes)
            normed = tokens[:, columns].astype(jnp.float32) * inverse * gain_ref[:, columns]
            ref[start : start + lanes] = jnp.transpose(normed).astype(jnp.bfloat16)

    stores = []
    for place, k in enumerate(without(skip, shards)):
        write(group.at[place], k + mine % (2 * skip) // skip * skip)
        stores.append(pltpu.make_async_copy(group.at[place], group_ref.at[place], store_sems.at[place]))
        stores[place].start()
    for ref, k in zip(other_refs, without(skip, shards)):
        write(ref, mine ^ (k + skip))
    for store in stores:
        store.wait()


def prepare(mine, tokens, gain, shards, skip):
    count, features = tokens.shape
    rows = features // shards
    half = shards // 2
    block = jax.ShapeDtypeStruct((rows, count), jnp.bfloat16)
    group, *others = pl.pallas_call(
        functools.partial(prepare_kernel, shards, skip),
        out_shape=(jax.ShapeDtypeStruct((half, rows, count), jnp.bfloat16),) + (block,) * half,
        in_specs=[
            pl.BlockSpec(memory_space=pltpu.SMEM),
            pl.BlockSpec(memory_space=pltpu.HBM),
            pl.BlockSpec(memory_space=pltpu.VMEM),
        ],
        out_specs=(pl.BlockSpec(memory_space=pltpu.HBM),) + (pl.BlockSpec(memory_space=pltpu.VMEM),) * half,
        scratch_shapes=[
            pltpu.VMEM((count, features), jnp.bfloat16),
            pltpu.VMEM((half, rows, count), jnp.bfloat16),
            pltpu.SemaphoreType.DMA((shards,)),
            pltpu.SemaphoreType.DMA((half,)),
        ],
        compiler_params=pltpu.CompilerParams(vmem_limit_bytes=16 * 2**20),
        cost_estimate=pl.CostEstimate(
            flops=5 * count * features, bytes_accessed=4 * count * features, transcendentals=count
        ),
        name="prepare",
    )(mine.reshape(1), tokens, gain.astype(jnp.float32).reshape(1, features))
    return group, others


def code_kernel(own_ref, shared_ref, weight_ref, kept_ref, sent_ref, shared, weight, decoded, sems):
    lanes = 2 * BLOCK
    groups, tile, share = decoded.shape
    rows, width = shared.shape
    own = own_ref[0]
    low = lax.broadcasted_iota(jnp.int32, (tile, lanes), 1) < BLOCK

    def loads(i):
        part = pl.ds(pl.multiple_of(i * tile, tile), tile)
        return (
            pltpu.make_async_copy(shared_ref.at[part], shared.at[part], sems.at[0, i]),
            pltpu.make_async_copy(weight_ref.at[part], weight.at[part], sems.at[1, i]),
        )

    for i in range(rows // tile):
        for load in loads(i):
            load.start()

    def step(i, _):
        for load in loads(i):
            load.wait()
        part = pl.ds(pl.multiple_of(i * tile, tile), tile)
        for start in range(0, width, lanes):
            columns = slice(start, start + lanes)
            delta = shared[part, columns].astype(jnp.float32) - weight[part, columns].astype(jnp.float32)
            size = jnp.abs(delta)
            largest = jnp.where(
                low,
                jnp.max(jnp.where(low, size, 0.0), axis=-1, keepdims=True),
                jnp.max(jnp.where(low, 0.0, size), axis=-1, keepdims=True),
            )
            scale = ((largest + 1e-06) * (1.0 / code_range)).astype(jnp.bfloat16).astype(jnp.float32)
            coded = (delta * pl.reciprocal(scale)).astype(jnp.bfloat16)
            value = (coded.astype(jnp.float32) * scale).astype(jnp.bfloat16)
            piece = min(share, lanes)
            for at in range(0, lanes, piece):
                group, offset = divmod(start + at, share)
                decoded[group, :, offset : offset + piece] = value[:, at : at + piece]
        for k in range(0, groups, 2):
            kept_ref[k // 2, part] = decoded[own ^ k]
            sent_ref[k // 2, part] = decoded[own ^ (k + 1)]
        return 0

    lax.fori_loop(0, rows // tile, step, 0)


def code_and_decode(own, shared, weight, groups):
    rows, width = shared.shape
    tile = min(rows, 128)
    share = width // groups
    half = jax.ShapeDtypeStruct((groups // 2, rows, share), jnp.bfloat16)
    return pl.pallas_call(
        code_kernel,
        out_shape=(half, half),
        in_specs=[pl.BlockSpec(memory_space=pltpu.SMEM)] + [pl.BlockSpec(memory_space=pltpu.HBM)] * 2,
        out_specs=(pl.BlockSpec(memory_space=pltpu.VMEM),) * 2,
        scratch_shapes=[
            pltpu.VMEM((rows, width), jnp.bfloat16),
            pltpu.VMEM((rows, width), jnp.bfloat16),
            pltpu.VMEM((groups, tile, share), jnp.bfloat16),
            pltpu.SemaphoreType.DMA((2, rows // tile)),
        ],
        compiler_params=pltpu.CompilerParams(vmem_limit_bytes=16 * 2**20),
        cost_estimate=pl.CostEstimate(flops=20 * rows * width, bytes_accessed=6 * rows * width, transcendentals=0),
        name="code_and_decode",
    )(own.reshape(1), shared, weight)


def accumulate_kernel(offsets, others, rate, place_ref, tokens_ref, weight_ref, *refs):
    parts = len(offsets)
    group_refs, refs = refs[:parts], refs[parts:]
    other_refs, refs = refs[:others], refs[others : 2 * others] + refs[2 * others :]
    cotangent_refs, refs = refs[:others], refs[others:]
    total_ref, tokens, weight, token_sems, weight_sem = refs
    loads = [
        pltpu.make_async_copy(tokens_ref.at[place_ref[0] ^ place], tokens.at[place], token_sems.at[place])
        for place in range(parts)
    ]
    loads.append(pltpu.make_async_copy(weight_ref, weight, weight_sem))
    for load in loads:
        load.start()
    width = total_ref.shape[1]
    tile = min(width, 256)
    for load in loads[:-1]:
        load.wait()
    left = jnp.concatenate([tokens[place] for place in range(parts)] + [ref[...] for ref in other_refs], axis=1)
    for start in range(0, width, tile):
        columns = slice(start, start + tile)
        right = jnp.concatenate([ref[:, columns] for ref in group_refs + cotangent_refs], axis=0)
        product = jnp.dot(left, right, preferred_element_type=jnp.float32)
        if start == 0:
            loads[-1].wait()
        total_ref[:, columns] = mix_weight * weight[:, columns].astype(jnp.float32) - rate * product


def accumulate(place, offsets, tokens, group, other_tokens, others, weight, rate):
    parts, rows, depth = tokens.shape
    width = weight.shape[1]
    whole = pl.BlockSpec(memory_space=pltpu.VMEM)
    remote = pl.BlockSpec(memory_space=pltpu.HBM)
    return pl.pallas_call(
        functools.partial(accumulate_kernel, offsets, len(others), rate),
        out_shape=jax.ShapeDtypeStruct((rows, width), jnp.float32),
        in_specs=[pl.BlockSpec(memory_space=pltpu.SMEM), remote, remote] + [whole] * (parts + 2 * len(others)),
        out_specs=whole,
        scratch_shapes=[
            pltpu.VMEM((parts, rows, depth), jnp.bfloat16),
            pltpu.VMEM((rows, width), jnp.bfloat16),
            pltpu.SemaphoreType.DMA((parts,)),
            pltpu.SemaphoreType.DMA,
        ],
        compiler_params=pltpu.CompilerParams(vmem_limit_bytes=20 * 2**20),
        cost_estimate=pl.CostEstimate(
            flops=2 * (parts + len(others)) * depth * rows * width,
            bytes_accessed=2 * (parts + len(others)) * depth * (rows + width) + 6 * rows * width,
            transcendentals=0,
        ),
        name="accumulate",
    )(place.reshape(1), tokens, weight, *group, *other_tokens, *others)


def place_kernel(own_ref, *refs):
    *piece_refs, out_ref = refs
    for k, ref in enumerate(piece_refs):
        out_ref[own_ref[0] ^ k] = ref[...]


def put_in_place(own, pieces):
    rows, share = pieces[0].shape
    return pl.pallas_call(
        place_kernel,
        out_shape=jax.ShapeDtypeStruct((len(pieces), rows, share), jnp.bfloat16),
        in_specs=[pl.BlockSpec(memory_space=pltpu.SMEM)] + [pl.BlockSpec(memory_space=pltpu.VMEM)] * len(pieces),
        out_specs=pl.BlockSpec(memory_space=pltpu.VMEM),
        compiler_params=pltpu.CompilerParams(vmem_limit_bytes=16 * 2**20),
        cost_estimate=pl.CostEstimate(flops=0, bytes_accessed=4 * len(pieces) * rows * share, transcendentals=0),
        name="put_in_place",
    )(own.reshape(1), *pieces)


def finish_kernel(parts, rate, *refs):
    token_refs, refs = refs[:parts], refs[parts:]
    cotangent_refs, refs = refs[:parts], refs[parts:]
    total_ref, shared_ref, out_ref, outs, sems = refs
    share = shared_ref.shape[2]
    steps, _, tile = outs.shape
    left = jnp.concatenate([ref[...] for ref in token_refs], axis=1)
    stores = []
    for step in range(steps):
        columns = slice(step * tile, (step + 1) * tile)
        right = jnp.concatenate([ref[:, columns] for ref in cotangent_refs], axis=0)
        total = total_ref[:, columns] - rate * jnp.dot(left, right, preferred_element_type=jnp.float32)
        for group in range(step * tile // share, (step + 1) * tile // share):
            part = slice(group * share - step * tile, (group + 1) * share - step * tile)
            shared = shared_ref[group].astype(jnp.float32)
            outs[step, :, part] = (total[:, part] + (1.0 - mix_weight) * shared).astype(jnp.bfloat16)
        stores.append(pltpu.make_async_copy(outs.at[step], out_ref.at[:, pl.ds(step * tile, tile)], sems.at[step]))
        stores[step].start()
    for store in stores:
        store.wait()


def finish(tokens, cotangents, total, shared, rate):
    parts = len(tokens)
    rows, width = total.shape
    depth = tokens[0].shape[1]
    tile = max(shared.shape[2], 256)
    return pl.pallas_call(
        functools.partial(finish_kernel, parts, rate),
        out_shape=jax.ShapeDtypeStruct((rows, width), jnp.bfloat16),
        in_specs=[pl.BlockSpec(memory_space=pltpu.VMEM)] * (2 * parts + 2),
        out_specs=pl.BlockSpec(memory_space=pltpu.HBM),
        scratch_shapes=[pltpu.VMEM((width // tile, rows, tile), jnp.bfloat16), pltpu.SemaphoreType.DMA((width // tile,))],
        compiler_params=pltpu.CompilerParams(vmem_limit_bytes=20 * 2**20),
        cost_estimate=pl.CostEstimate(
            flops=2 * parts * depth * rows * width,
            bytes_accessed=2 * parts * depth * (rows + width) + 8 * rows * width,
            transcendentals=0,
        ),
        name="finish",
    )(*tokens, *cotangents, total, shared)


def without(bit, size):
    return [k for k in range(size) if not k & bit]


def after(value, *others):
    return lax.optimization_barrier((value, *others))[0]


def gather(piece, axis, size, gates={}):
    pieces = {0: piece}
    bit = size // 2
    while bit:
        for k in sorted(pieces):
            pieces[k ^ bit] = swap(after(pieces[k], *gates.get(k ^ bit, ())), axis, bit)
        bit //= 2
    return [pieces[k] for k in range(size)]


def on_device(tokens, norm_gain, cotangent, layer_weight, shared_copy, master, momentum):
    tokens, cotangent, weight = tokens[0], cotangent[0], layer_weight[0]
    shards = lax.axis_size("fsdp")
    groups = lax.axis_size("replica")
    mine = lax.axis_index("fsdp")
    own = lax.axis_index("replica")
    rows, width = weight.shape
    inner_rate = inner_gain / math.sqrt(tokens.shape[0] * shards)

    rate = (1.0 - mix_weight) * inner_rate
    half, skip = shards // 2, shards // 4

    cotangents = gather(cotangent, "fsdp", shards)
    first = [cotangents[1 << bit] for bit in range(shards.bit_length() - 1)]
    group, others = prepare(mine, tokens, norm_gain, shards, skip)
    coded_shared, coded_weight, *_ = lax.optimization_barrier((shared_copy, weight, group))
    kept, sent = code_and_decode(own, coded_shared, coded_weight, groups)

    inside = without(skip, shards)
    group = after(group, *first, sent)
    members = [inside, [k + skip for k in inside]]
    columns = lax.all_to_all(group, "fsdp", split_axis=0, concat_axis=0, axis_index_groups=members, tiled=True)
    arrived = {}
    for k, block in zip(members[1], others):
        gate = [arrived[k - 1]] if k - 1 in arrived and k > half else [cotangents[half]]
        arrived[k] = swap(after(block, *gate), "fsdp", k)

    total = kept.astype(jnp.float32) + swap(sent, "replica", 1).astype(jnp.float32)
    bit = 2
    while bit < groups:
        sent = swap(total[1::2].astype(jnp.bfloat16), "replica", bit)
        bit *= 2
        total = total[0::2] + sent.astype(jnp.float32)
    average = total[0] / groups
    momentum_next = outer_beta * momentum + average
    master_next = master - outer_rate * (average + outer_beta * momentum_next)
    pieces = gather(master_next.astype(jnp.bfloat16), "replica", groups)

    near = [k for k in members[1] if k < half]
    far = [k for k in members[1] if k > half]
    place = mine // (2 * skip) * skip + mine % skip
    total = accumulate(
        place,
        inside,
        columns,
        [cotangents[k] for k in inside],
        [arrived[k] for k in near],
        [cotangents[k] for k in near],
        weight,
        rate,
    )
    shared = put_in_place(own, pieces)
    layer_next = finish([arrived[k] for k in far], [cotangents[k] for k in far], total, shared, rate)
    return (layer_next[None], master_next, momentum_next)


def solution(mesh):
    in_specs = (
        P("replica", "fsdp", None),
        P(),
        P("replica", "fsdp", None),
        P("replica", "fsdp", None),
        P("fsdp", None),
        P("fsdp", "replica"),
        P("fsdp", "replica"),
    )
    out_specs = (P("replica", "fsdp", None), P("fsdp", "replica"), P("fsdp", "replica"))
    return jax.shard_map(
        on_device, mesh=mesh, in_specs=in_specs, out_specs=out_specs, check_vma=False
    )
```

```python
import functools
import math

import jax
import jax.numpy as jnp
from jax import lax
from jax.experimental import pallas as pl
from jax.experimental.pallas import tpu as pltpu
from jax.sharding import PartitionSpec as P

BLOCK = 64


norm_eps = 1e-05
inner_gain = 0.4
outer_rate = 0.7
outer_beta = 0.9
mix_weight = 0.5
code_range = 448.0


def swap(value, axis, mask):
    size = lax.axis_size(axis)
    return lax.ppermute(value, axis, [(i, i ^ mask) for i in range(size)])


def prepare_kernel(tokens_ref, gain_ref, blocks_ref, tokens, blocks, load_sems, store_sems):
    lanes = 128
    shards, rows, count = blocks.shape
    features = shards * rows
    loads, stores = [], []
    for k in range(shards):
        columns = pl.ds(k * rows, rows)
        loads.append(pltpu.make_async_copy(tokens_ref.at[:, columns], tokens.at[:, columns], load_sems.at[k]))
        loads[k].start()
        stores.append(pltpu.make_async_copy(blocks.at[k], blocks_ref.at[k], store_sems.at[k]))
    squares = jnp.zeros((count, lanes), jnp.float32)
    for k in range(shards):
        loads[k].wait()
        for start in range(k * rows, (k + 1) * rows, lanes):
            block = tokens[:, start : start + lanes].astype(jnp.float32)
            squares = squares + block * block
    mean = jnp.sum(squares, axis=-1, keepdims=True) / features
    inverse = jnp.broadcast_to(lax.rsqrt(mean + norm_eps), (count, lanes))
    for k in range(shards):
        for start in range(0, rows, lanes):
            columns = slice(k * rows + start, k * rows + start + lanes)
            normed = tokens[:, columns].astype(jnp.float32) * inverse * gain_ref[:, columns]
            blocks[k, start : start + lanes] = jnp.transpose(normed).astype(jnp.bfloat16)
        stores[k].start()
    for store in stores:
        store.wait()


def prepare(tokens, gain, shards):
    count, features = tokens.shape
    rows = features // shards
    return pl.pallas_call(
        prepare_kernel,
        out_shape=jax.ShapeDtypeStruct((shards, rows, count), jnp.bfloat16),
        in_specs=[pl.BlockSpec(memory_space=pltpu.HBM), pl.BlockSpec(memory_space=pltpu.VMEM)],
        out_specs=pl.BlockSpec(memory_space=pltpu.HBM),
        scratch_shapes=[
            pltpu.VMEM((count, features), jnp.bfloat16),
            pltpu.VMEM((shards, rows, count), jnp.bfloat16),
            pltpu.SemaphoreType.DMA((shards,)),
            pltpu.SemaphoreType.DMA((shards,)),
        ],
        compiler_params=pltpu.CompilerParams(vmem_limit_bytes=16 * 2**20),
        cost_estimate=pl.CostEstimate(
            flops=5 * count * features, bytes_accessed=4 * count * features, transcendentals=count
        ),
        name="prepare",
    )(tokens, gain.astype(jnp.float32).reshape(1, features))


def code_kernel(own_ref, shared_ref, weight_ref, kept_ref, sent_ref, shared, weight, decoded, sems):
    lanes = 2 * BLOCK
    groups, tile, share = decoded.shape
    rows, width = shared.shape
    own = own_ref[0]
    low = lax.broadcasted_iota(jnp.int32, (tile, lanes), 1) < BLOCK

    def loads(i):
        part = pl.ds(pl.multiple_of(i * tile, tile), tile)
        return (
            pltpu.make_async_copy(shared_ref.at[part], shared.at[part], sems.at[0, i]),
            pltpu.make_async_copy(weight_ref.at[part], weight.at[part], sems.at[1, i]),
        )

    for i in range(rows // tile):
        for load in loads(i):
            load.start()

    def step(i, _):
        for load in loads(i):
            load.wait()
        part = pl.ds(pl.multiple_of(i * tile, tile), tile)
        for start in range(0, width, lanes):
            columns = slice(start, start + lanes)
            delta = shared[part, columns].astype(jnp.float32) - weight[part, columns].astype(jnp.float32)
            size = jnp.abs(delta)
            largest = jnp.where(
                low,
                jnp.max(jnp.where(low, size, 0.0), axis=-1, keepdims=True),
                jnp.max(jnp.where(low, 0.0, size), axis=-1, keepdims=True),
            )
            scale = ((largest + 1e-06) * (1.0 / code_range)).astype(jnp.bfloat16).astype(jnp.float32)
            coded = (delta * pl.reciprocal(scale)).astype(jnp.bfloat16)
            value = (coded.astype(jnp.float32) * scale).astype(jnp.bfloat16)
            piece = min(share, lanes)
            for at in range(0, lanes, piece):
                group, offset = divmod(start + at, share)
                decoded[group, :, offset : offset + piece] = value[:, at : at + piece]
        for k in range(0, groups, 2):
            kept_ref[k // 2, part] = decoded[own ^ k]
            sent_ref[k // 2, part] = decoded[own ^ (k + 1)]
        return 0

    lax.fori_loop(0, rows // tile, step, 0)


def code_and_decode(own, shared, weight, groups):
    rows, width = shared.shape
    tile = min(rows, 128)
    share = width // groups
    half = jax.ShapeDtypeStruct((groups // 2, rows, share), jnp.bfloat16)
    return pl.pallas_call(
        code_kernel,
        out_shape=(half, half),
        in_specs=[pl.BlockSpec(memory_space=pltpu.SMEM)] + [pl.BlockSpec(memory_space=pltpu.HBM)] * 2,
        out_specs=(pl.BlockSpec(memory_space=pltpu.VMEM),) * 2,
        scratch_shapes=[
            pltpu.VMEM((rows, width), jnp.bfloat16),
            pltpu.VMEM((rows, width), jnp.bfloat16),
            pltpu.VMEM((groups, tile, share), jnp.bfloat16),
            pltpu.SemaphoreType.DMA((2, rows // tile)),
        ],
        compiler_params=pltpu.CompilerParams(vmem_limit_bytes=16 * 2**20),
        cost_estimate=pl.CostEstimate(flops=20 * rows * width, bytes_accessed=6 * rows * width, transcendentals=0),
        name="code_and_decode",
    )(own.reshape(1), shared, weight)


def mix_kernel(shards, groups, rate, place_ref, *refs):
    tokens_ref, refs = refs[0], refs[1:]
    cotangent_refs, refs = refs[:shards], refs[shards:]
    piece_refs, refs = refs[:groups], refs[groups:]
    weight_ref, out_ref, refs = refs[0], refs[1], refs[2:]
    tokens, cotangents, pieces, weights, outs, token_sem, cotangent_sems, piece_sems, weight_sem, out_sems = refs
    mine, own = place_ref[0], place_ref[1]
    depth, width = cotangent_refs[0].shape
    share = pieces.shape[2]
    tile = outs.shape[2]

    def own_row(k):
        return pl.ds(pl.multiple_of((mine ^ k) * depth, depth), depth)

    loads = [pltpu.make_async_copy(tokens_ref, tokens, token_sem)]
    for k, ref in enumerate(cotangent_refs):
        loads.append(pltpu.make_async_copy(ref, cotangents.at[own_row(k)], cotangent_sems.at[k]))
    loads.append(pltpu.make_async_copy(weight_ref, weights, weight_sem))
    for k, ref in enumerate(piece_refs):
        loads.append(pltpu.make_async_copy(ref, pieces.at[own ^ k], piece_sems.at[k]))
    for load in loads:
        load.start()
    for load in loads[: 1 + shards]:
        load.wait()
    left = jnp.concatenate([tokens[k] for k in range(shards)], axis=1)
    stores = []
    for step in range(width // tile):
        columns = slice(step * tile, (step + 1) * tile)
        total = jnp.dot(left, cotangents[:, columns], preferred_element_type=jnp.float32)
        if step == 0:
            for load in loads[1 + shards :]:
                load.wait()
        for group in range(step * tile // share, (step + 1) * tile // share):
            place = slice(group * share, (group + 1) * share)
            part = slice(group * share - step * tile, (group + 1) * share - step * tile)
            mixed = weights[:, place].astype(jnp.float32) + pieces[group].astype(jnp.float32)
            outs[step, :, part] = (mix_weight * mixed - rate * total[:, part]).astype(jnp.bfloat16)
        stores.append(pltpu.make_async_copy(outs.at[step], out_ref.at[:, pl.ds(step * tile, tile)], out_sems.at[step]))
        stores[-1].start()
    for store in stores:
        store.wait()


def mix(mine, own, tokens, cotangents, pieces, weight, rate):
    shards, rows, depth = tokens.shape
    width = weight.shape[1]
    groups = len(pieces)
    share = width // groups
    tile = max(share, 256)
    return pl.pallas_call(
        functools.partial(mix_kernel, shards, groups, rate),
        out_shape=jax.ShapeDtypeStruct((rows, width), jnp.bfloat16),
        in_specs=[pl.BlockSpec(memory_space=pltpu.SMEM)]
        + [pl.BlockSpec(memory_space=pltpu.HBM)] * (2 + shards + groups),
        out_specs=pl.BlockSpec(memory_space=pltpu.HBM),
        scratch_shapes=[
            pltpu.VMEM((shards, rows, depth), jnp.bfloat16),
            pltpu.VMEM((shards * depth, width), jnp.bfloat16),
            pltpu.VMEM((groups, rows, share), jnp.bfloat16),
            pltpu.VMEM((rows, width), jnp.bfloat16),
            pltpu.VMEM((width // tile, rows, tile), jnp.bfloat16),
            pltpu.SemaphoreType.DMA,
            pltpu.SemaphoreType.DMA((shards,)),
            pltpu.SemaphoreType.DMA((groups,)),
            pltpu.SemaphoreType.DMA,
            pltpu.SemaphoreType.DMA((width // tile,)),
        ],
        compiler_params=pltpu.CompilerParams(vmem_limit_bytes=50 * 2**20),
        cost_estimate=pl.CostEstimate(
            flops=2 * depth * shards * rows * width,
            bytes_accessed=2 * depth * shards * (rows + width) + 6 * rows * width,
            transcendentals=0,
        ),
        name="mix",
    )(jnp.stack([mine, own]), tokens, *cotangents, *pieces, weight)


def gather(piece, axis, size, after=()):
    pieces = {0: piece}
    bit = size // 2
    while bit:
        if bit == 1 and after:
            (*held, _) = lax.optimization_barrier((*(pieces[k] for k in sorted(pieces)[1:]), after))
            pieces.update(zip(sorted(pieces)[1:], held))
        for k in sorted(pieces):
            pieces[k ^ bit] = swap(pieces[k], axis, bit)
        bit //= 2
    return [pieces[k] for k in range(size)]


def on_device(tokens, norm_gain, cotangent, layer_weight, shared_copy, master, momentum):
    tokens, cotangent, weight = tokens[0], cotangent[0], layer_weight[0]
    shards = lax.axis_size("fsdp")
    groups = lax.axis_size("replica")
    mine = lax.axis_index("fsdp")
    own = lax.axis_index("replica")
    rows, width = weight.shape
    inner_rate = inner_gain / math.sqrt(tokens.shape[0] * shards)

    own_exchanges = [1 << bit for bit in range(shards.bit_length() - 1)]
    cotangents = gather(cotangent, "fsdp", shards)
    blocks = prepare(tokens, norm_gain, shards)
    *_, blocks, coded_shared, coded_weight = lax.optimization_barrier(
        (*(cotangents[k] for k in own_exchanges), blocks, shared_copy, weight)
    )
    columns = lax.all_to_all(blocks, "fsdp", split_axis=0, concat_axis=0, tiled=True)

    kept, sent = code_and_decode(own, coded_shared, coded_weight, groups)
    total = kept.astype(jnp.float32) + swap(sent, "replica", 1).astype(jnp.float32)
    bit = 2
    while bit < groups:
        sent = swap(total[1::2].astype(jnp.bfloat16), "replica", bit)
        bit *= 2
        if bit >= groups:
            *_, sent = lax.optimization_barrier((cotangents[shards // 2 + 1], sent))
        total = total[0::2] + sent.astype(jnp.float32)
    average = total[0] / groups
    momentum_next = outer_beta * momentum + average
    master_next = master - outer_rate * (average + outer_beta * momentum_next)
    pieces = gather(master_next.astype(jnp.bfloat16), "replica", groups, after=cotangents[-2:-1])

    layer_next = mix(mine, own, columns, cotangents, pieces, weight, (1.0 - mix_weight) * inner_rate)
    return (layer_next[None], master_next, momentum_next)


def solution(mesh):
    in_specs = (
        P("replica", "fsdp", None),
        P(),
        P("replica", "fsdp", None),
        P("replica", "fsdp", None),
        P("fsdp", None),
        P("fsdp", "replica"),
        P("fsdp", "replica"),
    )
    out_specs = (P("replica", "fsdp", None), P("fsdp", "replica"), P("fsdp", "replica"))
    return jax.shard_map(
        on_device, mesh=mesh, in_specs=in_specs, out_specs=out_specs, check_vma=False
    )
```

```python
import functools
import math

import jax
import jax.numpy as jnp
from jax import lax
from jax.experimental import pallas as pl
from jax.experimental.pallas import tpu as pltpu
from jax.sharding import PartitionSpec as P

BLOCK = 64


norm_eps = 1e-05
inner_gain = 0.4
outer_rate = 0.7
outer_beta = 0.9
mix_weight = 0.5
code_range = 448.0


def swap(value, axis, mask):
    size = lax.axis_size(axis)
    return lax.ppermute(value, axis, [(i, i ^ mask) for i in range(size)])


def prepare_kernel(tokens_ref, gain_ref, blocks_ref, tokens, blocks, load_sems, store_sems):
    lanes = 128
    shards, rows, count = blocks.shape
    features = shards * rows
    loads, stores = [], []
    for k in range(shards):
        columns = pl.ds(k * rows, rows)
        loads.append(pltpu.make_async_copy(tokens_ref.at[:, columns], tokens.at[:, columns], load_sems.at[k]))
        loads[k].start()
        stores.append(pltpu.make_async_copy(blocks.at[k], blocks_ref.at[k], store_sems.at[k]))
    squares = jnp.zeros((count, lanes), jnp.float32)
    for k in range(shards):
        loads[k].wait()
        for start in range(k * rows, (k + 1) * rows, lanes):
            block = tokens[:, start : start + lanes].astype(jnp.float32)
            squares = squares + block * block
    mean = jnp.sum(squares, axis=-1, keepdims=True) / features
    inverse = jnp.broadcast_to(lax.rsqrt(mean + norm_eps), (count, lanes))
    for k in range(shards):
        for start in range(0, rows, lanes):
            columns = slice(k * rows + start, k * rows + start + lanes)
            normed = tokens[:, columns].astype(jnp.float32) * inverse * gain_ref[:, columns]
            blocks[k, start : start + lanes] = jnp.transpose(normed).astype(jnp.bfloat16)
        stores[k].start()
    for store in stores:
        store.wait()


def prepare(tokens, gain, shards):
    count, features = tokens.shape
    rows = features // shards
    return pl.pallas_call(
        prepare_kernel,
        out_shape=jax.ShapeDtypeStruct((shards, rows, count), jnp.bfloat16),
        in_specs=[pl.BlockSpec(memory_space=pltpu.HBM), pl.BlockSpec(memory_space=pltpu.VMEM)],
        out_specs=pl.BlockSpec(memory_space=pltpu.HBM),
        scratch_shapes=[
            pltpu.VMEM((count, features), jnp.bfloat16),
            pltpu.VMEM((shards, rows, count), jnp.bfloat16),
            pltpu.SemaphoreType.DMA((shards,)),
            pltpu.SemaphoreType.DMA((shards,)),
        ],
        compiler_params=pltpu.CompilerParams(vmem_limit_bytes=16 * 2**20),
        cost_estimate=pl.CostEstimate(
            flops=5 * count * features, bytes_accessed=4 * count * features, transcendentals=count
        ),
        name="prepare",
    )(tokens, gain.astype(jnp.float32).reshape(1, features))


def code_kernel(own_ref, shared_ref, weight_ref, kept_ref, sent_ref, shared, weight, decoded, sems):
    lanes = 2 * BLOCK
    groups, tile, share = decoded.shape
    rows, width = shared.shape
    own = own_ref[0]
    low = lax.broadcasted_iota(jnp.int32, (tile, lanes), 1) < BLOCK

    def loads(i):
        part = pl.ds(pl.multiple_of(i * tile, tile), tile)
        return (
            pltpu.make_async_copy(shared_ref.at[part], shared.at[part], sems.at[0, i]),
            pltpu.make_async_copy(weight_ref.at[part], weight.at[part], sems.at[1, i]),
        )

    for i in range(rows // tile):
        for load in loads(i):
            load.start()

    def step(i, _):
        for load in loads(i):
            load.wait()
        part = pl.ds(pl.multiple_of(i * tile, tile), tile)
        for start in range(0, width, lanes):
            columns = slice(start, start + lanes)
            delta = shared[part, columns].astype(jnp.float32) - weight[part, columns].astype(jnp.float32)
            size = jnp.abs(delta)
            largest = jnp.where(
                low,
                jnp.max(jnp.where(low, size, 0.0), axis=-1, keepdims=True),
                jnp.max(jnp.where(low, 0.0, size), axis=-1, keepdims=True),
            )
            scale = ((largest + 1e-06) * (1.0 / code_range)).astype(jnp.bfloat16).astype(jnp.float32)
            coded = (delta * pl.reciprocal(scale)).astype(jnp.bfloat16)
            value = (coded.astype(jnp.float32) * scale).astype(jnp.bfloat16)
            piece = min(share, lanes)
            for at in range(0, lanes, piece):
                group, offset = divmod(start + at, share)
                decoded[group, :, offset : offset + piece] = value[:, at : at + piece]
        for k in range(0, groups, 2):
            kept_ref[k // 2, part] = decoded[own ^ k]
            sent_ref[k // 2, part] = decoded[own ^ (k + 1)]
        return 0

    lax.fori_loop(0, rows // tile, step, 0)


def code_and_decode(own, shared, weight, groups):
    rows, width = shared.shape
    tile = min(rows, 128)
    share = width // groups
    half = jax.ShapeDtypeStruct((groups // 2, rows, share), jnp.bfloat16)
    return pl.pallas_call(
        code_kernel,
        out_shape=(half, half),
        in_specs=[pl.BlockSpec(memory_space=pltpu.SMEM)] + [pl.BlockSpec(memory_space=pltpu.HBM)] * 2,
        out_specs=(pl.BlockSpec(memory_space=pltpu.VMEM),) * 2,
        scratch_shapes=[
            pltpu.VMEM((rows, width), jnp.bfloat16),
            pltpu.VMEM((rows, width), jnp.bfloat16),
            pltpu.VMEM((groups, tile, share), jnp.bfloat16),
            pltpu.SemaphoreType.DMA((2, rows // tile)),
        ],
        compiler_params=pltpu.CompilerParams(vmem_limit_bytes=16 * 2**20),
        cost_estimate=pl.CostEstimate(flops=20 * rows * width, bytes_accessed=6 * rows * width, transcendentals=0),
        name="code_and_decode",
    )(own.reshape(1), shared, weight)


def base_kernel(own_ref, weight_ref, *refs):
    piece_refs, (base_ref, weight, pieces, base, load_sem, piece_sems, store_sem) = refs[:-7], refs[-7:]
    own = own_ref[0]
    groups, rows, share = pieces.shape
    loads = [pltpu.make_async_copy(weight_ref, weight, load_sem)]
    for k, ref in enumerate(piece_refs):
        loads.append(pltpu.make_async_copy(ref, pieces.at[own ^ k], piece_sems.at[k]))
    for load in loads:
        load.start()
    for load in loads:
        load.wait()
    for group in range(groups):
        columns = slice(group * share, (group + 1) * share)
        mixed = mix_weight * weight[:, columns].astype(jnp.float32)
        mixed = mixed + (1.0 - mix_weight) * pieces[group].astype(jnp.float32)
        base[:, columns] = mixed.astype(jnp.bfloat16)
    store = pltpu.make_async_copy(base, base_ref, store_sem)
    store.start()
    store.wait()


def base_of(own, weight, pieces):
    rows, width = weight.shape
    groups = len(pieces)
    return pl.pallas_call(
        base_kernel,
        out_shape=jax.ShapeDtypeStruct((rows, width), jnp.bfloat16),
        in_specs=[pl.BlockSpec(memory_space=pltpu.SMEM)] + [pl.BlockSpec(memory_space=pltpu.HBM)] * (1 + groups),
        out_specs=pl.BlockSpec(memory_space=pltpu.HBM),
        scratch_shapes=[
            pltpu.VMEM((rows, width), jnp.bfloat16),
            pltpu.VMEM((groups, rows, width // groups), jnp.bfloat16),
            pltpu.VMEM((rows, width), jnp.bfloat16),
            pltpu.SemaphoreType.DMA,
            pltpu.SemaphoreType.DMA((groups,)),
            pltpu.SemaphoreType.DMA,
        ],
        compiler_params=pltpu.CompilerParams(vmem_limit_bytes=16 * 2**20),
        cost_estimate=pl.CostEstimate(flops=3 * rows * width, bytes_accessed=6 * rows * width, transcendentals=0),
        name="base",
    )(own.reshape(1), weight, *pieces)


def mix_kernel(shards, rate, mine_ref, tokens_ref, base_ref, *refs):
    cotangent_refs, out_ref, refs = refs[:shards], refs[shards], refs[shards + 1 :]
    tokens, cotangents, base, totals, outs, token_sems, cotangent_sems, base_sem, out_sems = refs
    mine = mine_ref[0]
    depth, width = cotangent_refs[0].shape
    steps, _, tile = outs.shape

    loads = []
    for k, ref in enumerate(cotangent_refs):
        loads.append(pltpu.make_async_copy(tokens_ref.at[mine ^ k], tokens.at[k], token_sems.at[k]))
        loads.append(pltpu.make_async_copy(ref, cotangents.at[pl.ds(k * depth, depth)], cotangent_sems.at[k]))
    loads.append(pltpu.make_async_copy(base_ref, base, base_sem))
    for load in loads:
        load.start()
    stores = []
    some = 2
    for first in range(0, shards, some):
        for load in loads[2 * first : 2 * (first + some)]:
            load.wait()
        last = first + some == shards
        if last:
            loads[-1].wait()
        left = jnp.concatenate([tokens[k] for k in range(first, first + some)], axis=1)
        for step in range(steps):
            columns = slice(step * tile, (step + 1) * tile)
            right = cotangents[first * depth : (first + some) * depth, columns]
            total = jnp.dot(left, right, preferred_element_type=jnp.float32)
            if first:
                total = totals[step] + total
            if not last:
                totals[step] = total
                continue
            outs[step] = (base[:, columns].astype(jnp.float32) - rate * total).astype(jnp.bfloat16)
            place = pl.ds(step * tile, tile)
            stores.append(pltpu.make_async_copy(outs.at[step], out_ref.at[:, place], out_sems.at[step]))
            stores[step].start()
    for store in stores:
        store.wait()


def mix(mine, tokens, cotangents, base, rate):
    shards, rows, depth = tokens.shape
    width = base.shape[1]
    tile = min(width, 256)
    return pl.pallas_call(
        functools.partial(mix_kernel, shards, rate),
        out_shape=jax.ShapeDtypeStruct((rows, width), jnp.bfloat16),
        in_specs=[pl.BlockSpec(memory_space=pltpu.SMEM)] + [pl.BlockSpec(memory_space=pltpu.HBM)] * (2 + shards),
        out_specs=pl.BlockSpec(memory_space=pltpu.HBM),
        scratch_shapes=[
            pltpu.VMEM((shards, rows, depth), jnp.bfloat16),
            pltpu.VMEM((shards * depth, width), jnp.bfloat16),
            pltpu.VMEM((rows, width), jnp.bfloat16),
            pltpu.VMEM((width // tile, rows, tile), jnp.float32),
            pltpu.VMEM((width // tile, rows, tile), jnp.bfloat16),
            pltpu.SemaphoreType.DMA((shards,)),
            pltpu.SemaphoreType.DMA((shards,)),
            pltpu.SemaphoreType.DMA,
            pltpu.SemaphoreType.DMA((width // tile,)),
        ],
        compiler_params=pltpu.CompilerParams(vmem_limit_bytes=50 * 2**20),
        cost_estimate=pl.CostEstimate(
            flops=2 * depth * shards * rows * width,
            bytes_accessed=2 * depth * shards * (rows + width) + 4 * rows * width,
            transcendentals=0,
        ),
        name="mix",
    )(mine.reshape(1), tokens, base, *cotangents)


def later(value, *others):
    return lax.optimization_barrier((value, *others))[0]


def gather(piece, axis, size, after=()):
    pieces = {0: piece}
    bit = size // 2
    while bit:
        for k in sorted(pieces):
            value = later(pieces[k], *after) if bit == 1 and k else pieces[k]
            pieces[k ^ bit] = swap(value, axis, bit)
        bit //= 2
    return [pieces[k] for k in range(size)]


def gather_far(piece, axis, size):
    pieces = {0: swap(piece, axis, size)}
    pieces[1] = swap(pieces[0], axis, 1)
    bit = size // 2
    while bit:
        for k in [k for k in sorted(pieces) if k ^ bit not in pieces and not k % (2 * bit) % bit and not (bit > 1 and k % 2)]:
            pieces[k ^ bit] = swap(later(pieces[k], pieces[1]), axis, bit)
        bit //= 2
    return [pieces[k] for k in range(size)]


def on_device(tokens, norm_gain, cotangent, layer_weight, shared_copy, master, momentum):
    tokens, cotangent, weight = tokens[0], cotangent[0], layer_weight[0]
    shards = lax.axis_size("fsdp")
    groups = lax.axis_size("replica")
    mine = lax.axis_index("fsdp")
    own = lax.axis_index("replica")
    rows, width = weight.shape
    inner_rate = inner_gain / math.sqrt(tokens.shape[0] * shards)

    own_exchanges = [1 << bit for bit in range(shards.bit_length() - 1)]
    half = shards // 2
    cotangents = gather(cotangent, "fsdp", half) + gather_far(cotangent, "fsdp", half)
    blocks = prepare(tokens, norm_gain, shards)
    *_, blocks, coded_shared, coded_weight = lax.optimization_barrier(
        (*(cotangents[k] for k in own_exchanges), blocks, shared_copy, weight)
    )
    columns = lax.all_to_all(blocks, "fsdp", split_axis=0, concat_axis=0, tiled=True)

    kept, sent = code_and_decode(own, coded_shared, coded_weight, groups)
    total = kept.astype(jnp.float32) + swap(sent, "replica", 1).astype(jnp.float32)
    bit = 2
    while bit < groups:
        sent = swap(total[1::2].astype(jnp.bfloat16), "replica", bit)
        bit *= 2
        total = total[0::2] + sent.astype(jnp.float32)
    average = total[0] / groups
    momentum_next = outer_beta * momentum + average
    master_next = master - outer_rate * (average + outer_beta * momentum_next)
    pieces = gather(master_next.astype(jnp.bfloat16), "replica", groups, after=cotangents[-2:-1])

    base = base_of(own, weight, pieces)
    layer_next = mix(mine, columns, cotangents, base, (1.0 - mix_weight) * inner_rate)
    return (layer_next[None], master_next, momentum_next)


def solution(mesh):
    in_specs = (
        P("replica", "fsdp", None),
        P(),
        P("replica", "fsdp", None),
        P("replica", "fsdp", None),
        P("fsdp", None),
        P("fsdp", "replica"),
        P("fsdp", "replica"),
    )
    out_specs = (P("replica", "fsdp", None), P("fsdp", "replica"), P("fsdp", "replica"))
    return jax.shard_map(
        on_device, mesh=mesh, in_specs=in_specs, out_specs=out_specs, check_vma=False
    )
```

```python
import functools
import math

import jax
import jax.numpy as jnp
from jax import lax
from jax.experimental import pallas as pl
from jax.experimental.pallas import tpu as pltpu
from jax.sharding import PartitionSpec as P

BLOCK = 64


norm_eps = 1e-05
inner_gain = 0.4
outer_rate = 0.7
outer_beta = 0.9
mix_weight = 0.5
code_range = 448.0


def swap(value, axis, mask):
    size = lax.axis_size(axis)
    return lax.ppermute(value, axis, [(i, i ^ mask) for i in range(size)])


def prepare_kernel(tokens_ref, gain_ref, blocks_ref, tokens, blocks, load_sems, store_sems):
    lanes = 128
    shards, rows, count = blocks.shape
    features = shards * rows
    loads, stores = [], []
    for k in range(shards):
        columns = pl.ds(k * rows, rows)
        loads.append(pltpu.make_async_copy(tokens_ref.at[:, columns], tokens.at[:, columns], load_sems.at[k]))
        loads[k].start()
        stores.append(pltpu.make_async_copy(blocks.at[k], blocks_ref.at[k], store_sems.at[k]))
    squares = jnp.zeros((count, lanes), jnp.float32)
    for k in range(shards):
        loads[k].wait()
        for start in range(k * rows, (k + 1) * rows, lanes):
            block = tokens[:, start : start + lanes].astype(jnp.float32)
            squares = squares + block * block
    mean = jnp.sum(squares, axis=-1, keepdims=True) / features
    inverse = jnp.broadcast_to(lax.rsqrt(mean + norm_eps), (count, lanes))
    for k in range(shards):
        for start in range(0, rows, lanes):
            columns = slice(k * rows + start, k * rows + start + lanes)
            normed = tokens[:, columns].astype(jnp.float32) * inverse * gain_ref[:, columns]
            blocks[k, start : start + lanes] = jnp.transpose(normed).astype(jnp.bfloat16)
        stores[k].start()
    for store in stores:
        store.wait()


def prepare(tokens, gain, shards):
    count, features = tokens.shape
    rows = features // shards
    return pl.pallas_call(
        prepare_kernel,
        out_shape=jax.ShapeDtypeStruct((shards, rows, count), jnp.bfloat16),
        in_specs=[pl.BlockSpec(memory_space=pltpu.HBM), pl.BlockSpec(memory_space=pltpu.VMEM)],
        out_specs=pl.BlockSpec(memory_space=pltpu.HBM),
        scratch_shapes=[
            pltpu.VMEM((count, features), jnp.bfloat16),
            pltpu.VMEM((shards, rows, count), jnp.bfloat16),
            pltpu.SemaphoreType.DMA((shards,)),
            pltpu.SemaphoreType.DMA((shards,)),
        ],
        compiler_params=pltpu.CompilerParams(vmem_limit_bytes=16 * 2**20),
        cost_estimate=pl.CostEstimate(
            flops=5 * count * features, bytes_accessed=4 * count * features, transcendentals=count
        ),
        name="prepare",
    )(tokens, gain.astype(jnp.float32).reshape(1, features))


def code_kernel(own_ref, shared_ref, weight_ref, kept_ref, sent_ref, shared, weight, decoded, sems):
    lanes = 2 * BLOCK
    groups, tile, share = decoded.shape
    rows, width = shared.shape
    own = own_ref[0]
    low = lax.broadcasted_iota(jnp.int32, (tile, lanes), 1) < BLOCK

    def loads(i):
        part = pl.ds(pl.multiple_of(i * tile, tile), tile)
        return (
            pltpu.make_async_copy(shared_ref.at[part], shared.at[part], sems.at[0, i]),
            pltpu.make_async_copy(weight_ref.at[part], weight.at[part], sems.at[1, i]),
        )

    for i in range(rows // tile):
        for load in loads(i):
            load.start()

    def step(i, _):
        for load in loads(i):
            load.wait()
        part = pl.ds(pl.multiple_of(i * tile, tile), tile)
        for start in range(0, width, lanes):
            columns = slice(start, start + lanes)
            delta = shared[part, columns].astype(jnp.float32) - weight[part, columns].astype(jnp.float32)
            size = jnp.abs(delta)
            largest = jnp.where(
                low,
                jnp.max(jnp.where(low, size, 0.0), axis=-1, keepdims=True),
                jnp.max(jnp.where(low, 0.0, size), axis=-1, keepdims=True),
            )
            scale = ((largest + 1e-06) * (1.0 / code_range)).astype(jnp.bfloat16).astype(jnp.float32)
            coded = (delta * pl.reciprocal(scale)).astype(jnp.bfloat16)
            value = (coded.astype(jnp.float32) * scale).astype(jnp.bfloat16)
            piece = min(share, lanes)
            for at in range(0, lanes, piece):
                group, offset = divmod(start + at, share)
                decoded[group, :, offset : offset + piece] = value[:, at : at + piece]
        for k in range(0, groups, 2):
            kept_ref[k // 2, part] = decoded[own ^ k]
            sent_ref[k // 2, part] = decoded[own ^ (k + 1)]
        return 0

    lax.fori_loop(0, rows // tile, step, 0)


def code_and_decode(own, shared, weight, groups):
    rows, width = shared.shape
    tile = min(rows, 128)
    share = width // groups
    half = jax.ShapeDtypeStruct((groups // 2, rows, share), jnp.bfloat16)
    return pl.pallas_call(
        code_kernel,
        out_shape=(half, half),
        in_specs=[pl.BlockSpec(memory_space=pltpu.SMEM)] + [pl.BlockSpec(memory_space=pltpu.HBM)] * 2,
        out_specs=(pl.BlockSpec(memory_space=pltpu.VMEM),) * 2,
        scratch_shapes=[
            pltpu.VMEM((rows, width), jnp.bfloat16),
            pltpu.VMEM((rows, width), jnp.bfloat16),
            pltpu.VMEM((groups, tile, share), jnp.bfloat16),
            pltpu.SemaphoreType.DMA((2, rows // tile)),
        ],
        compiler_params=pltpu.CompilerParams(vmem_limit_bytes=16 * 2**20),
        cost_estimate=pl.CostEstimate(flops=20 * rows * width, bytes_accessed=6 * rows * width, transcendentals=0),
        name="code_and_decode",
    )(own.reshape(1), shared, weight)


def base_kernel(own_ref, weight_ref, *refs):
    piece_refs, (base_ref, weight, pieces, load_sem, piece_sems) = refs[:-5], refs[-5:]
    own = own_ref[0]
    groups, rows, share = pieces.shape
    loads = [pltpu.make_async_copy(weight_ref, weight, load_sem)]
    for k, ref in enumerate(piece_refs):
        loads.append(pltpu.make_async_copy(ref, pieces.at[own ^ k], piece_sems.at[k]))
    for load in loads:
        load.start()
    for load in loads:
        load.wait()
    for group in range(groups):
        columns = slice(group * share, (group + 1) * share)
        mixed = mix_weight * weight[:, columns].astype(jnp.float32)
        mixed = mixed + (1.0 - mix_weight) * pieces[group].astype(jnp.float32)
        base_ref[:, columns] = mixed.astype(jnp.bfloat16)


def base_of(own, weight, pieces):
    rows, width = weight.shape
    groups = len(pieces)
    return pl.pallas_call(
        base_kernel,
        out_shape=jax.ShapeDtypeStruct((rows, width), jnp.bfloat16),
        in_specs=[pl.BlockSpec(memory_space=pltpu.SMEM)] + [pl.BlockSpec(memory_space=pltpu.HBM)] * (1 + groups),
        out_specs=pl.BlockSpec(memory_space=pltpu.VMEM),
        scratch_shapes=[
            pltpu.VMEM((rows, width), jnp.bfloat16),
            pltpu.VMEM((groups, rows, width // groups), jnp.bfloat16),
            pltpu.SemaphoreType.DMA,
            pltpu.SemaphoreType.DMA((groups,)),
        ],
        compiler_params=pltpu.CompilerParams(vmem_limit_bytes=16 * 2**20),
        cost_estimate=pl.CostEstimate(flops=3 * rows * width, bytes_accessed=6 * rows * width, transcendentals=0),
        name="base",
    )(own.reshape(1), weight, *pieces)


def accumulate_kernel(parts, mine_ref, tokens_ref, *refs):
    cotangent_refs, refs = refs[:parts], refs[parts:]
    total_ref, last_ref, tokens, cotangents, token_sems, cotangent_sems, last_sem = refs
    mine = mine_ref[0]
    depth, width = cotangent_refs[0].shape
    tile = min(width, 256)

    loads = []
    for k, ref in enumerate(cotangent_refs):
        loads.append(pltpu.make_async_copy(tokens_ref.at[mine ^ k], tokens.at[k], token_sems.at[k]))
        loads.append(pltpu.make_async_copy(ref, cotangents.at[pl.ds(k * depth, depth)], cotangent_sems.at[k]))
    loads.append(pltpu.make_async_copy(tokens_ref.at[mine ^ parts], last_ref, last_sem))
    for load in loads:
        load.start()
    some = 2
    for first in range(0, parts, some):
        end = min(first + some, parts)
        for load in loads[2 * first : 2 * end]:
            load.wait()
        left = jnp.concatenate([tokens[k] for k in range(first, end)], axis=1)
        for start in range(0, width, tile):
            columns = slice(start, start + tile)
            right = cotangents[first * depth : end * depth, columns]
            total = jnp.dot(left, right, preferred_element_type=jnp.float32)
            total_ref[:, columns] = total_ref[:, columns] + total if first else total
    loads[-1].wait()


def accumulate(mine, tokens, cotangents):
    shards, rows, depth = tokens.shape
    parts = shards - 1
    width = cotangents[0].shape[1]
    return pl.pallas_call(
        functools.partial(accumulate_kernel, parts),
        out_shape=(jax.ShapeDtypeStruct((rows, width), jnp.float32), jax.ShapeDtypeStruct((rows, depth), jnp.bfloat16)),
        in_specs=[pl.BlockSpec(memory_space=pltpu.SMEM)] + [pl.BlockSpec(memory_space=pltpu.HBM)] * (1 + parts),
        out_specs=(pl.BlockSpec(memory_space=pltpu.VMEM),) * 2,
        scratch_shapes=[
            pltpu.VMEM((parts, rows, depth), jnp.bfloat16),
            pltpu.VMEM((parts * depth, width), jnp.bfloat16),
            pltpu.SemaphoreType.DMA((parts,)),
            pltpu.SemaphoreType.DMA((parts,)),
            pltpu.SemaphoreType.DMA,
        ],
        compiler_params=pltpu.CompilerParams(vmem_limit_bytes=44 * 2**20),
        cost_estimate=pl.CostEstimate(
            flops=2 * depth * parts * rows * width,
            bytes_accessed=2 * depth * shards * (rows + width) + 4 * rows * width,
            transcendentals=0,
        ),
        name="accumulate",
    )(mine.reshape(1), tokens, *cotangents)


def finish_kernel(rate, tokens_ref, cotangent_ref, total_ref, base_ref, out_ref, outs, sems):
    steps, _, tile = outs.shape
    stores = []
    for step in range(steps):
        columns = slice(step * tile, (step + 1) * tile)
        product = jnp.dot(tokens_ref[...], cotangent_ref[:, columns], preferred_element_type=jnp.float32)
        total = total_ref[:, columns] + product
        outs[step] = (base_ref[:, columns].astype(jnp.float32) - rate * total).astype(jnp.bfloat16)
        stores.append(pltpu.make_async_copy(outs.at[step], out_ref.at[:, pl.ds(step * tile, tile)], sems.at[step]))
        stores[step].start()
    for store in stores:
        store.wait()


def finish(tokens, cotangent, total, base, rate):
    rows, width = total.shape
    depth = tokens.shape[1]
    tile = min(width, 256)
    return pl.pallas_call(
        functools.partial(finish_kernel, rate),
        out_shape=jax.ShapeDtypeStruct((rows, width), jnp.bfloat16),
        in_specs=[pl.BlockSpec(memory_space=pltpu.VMEM)] * 4,
        out_specs=pl.BlockSpec(memory_space=pltpu.HBM),
        scratch_shapes=[pltpu.VMEM((width // tile, rows, tile), jnp.bfloat16), pltpu.SemaphoreType.DMA((width // tile,))],
        compiler_params=pltpu.CompilerParams(vmem_limit_bytes=16 * 2**20),
        cost_estimate=pl.CostEstimate(
            flops=2 * depth * rows * width, bytes_accessed=2 * depth * (rows + width) + 8 * rows * width, transcendentals=0
        ),
        name="finish",
    )(tokens, cotangent, total, base)


def gather(piece, axis, size):
    pieces = {0: piece}
    bit = size // 2
    while bit:
        for k in sorted(pieces):
            pieces[k ^ bit] = swap(pieces[k], axis, bit)
        bit //= 2
    return [pieces[k] for k in range(size)]


def on_device(tokens, norm_gain, cotangent, layer_weight, shared_copy, master, momentum):
    tokens, cotangent, weight = tokens[0], cotangent[0], layer_weight[0]
    shards = lax.axis_size("fsdp")
    groups = lax.axis_size("replica")
    mine = lax.axis_index("fsdp")
    own = lax.axis_index("replica")
    rows, width = weight.shape
    inner_rate = inner_gain / math.sqrt(tokens.shape[0] * shards)

    own_exchanges = [1 << bit for bit in range(shards.bit_length() - 1)]
    cotangents = gather(cotangent, "fsdp", shards)
    blocks = prepare(tokens, norm_gain, shards)
    *_, blocks, coded_shared, coded_weight = lax.optimization_barrier(
        (*(cotangents[k] for k in own_exchanges), blocks, shared_copy, weight)
    )
    columns = lax.all_to_all(blocks, "fsdp", split_axis=0, concat_axis=0, tiled=True)

    kept, sent = code_and_decode(own, coded_shared, coded_weight, groups)
    total = kept.astype(jnp.float32) + swap(sent, "replica", 1).astype(jnp.float32)
    bit = 2
    while bit < groups:
        sent = swap(total[1::2].astype(jnp.bfloat16), "replica", bit)
        bit *= 2
        total = total[0::2] + sent.astype(jnp.float32)
    average = total[0] / groups
    momentum_next = outer_beta * momentum + average
    master_next = master - outer_rate * (average + outer_beta * momentum_next)
    pieces = gather(master_next.astype(jnp.bfloat16), "replica", groups)

    total, last = accumulate(mine, columns, cotangents[:-1])
    layer_next = finish(last, cotangents[-1], total, base_of(own, weight, pieces), (1.0 - mix_weight) * inner_rate)
    return (layer_next[None], master_next, momentum_next)


def solution(mesh):
    in_specs = (
        P("replica", "fsdp", None),
        P(),
        P("replica", "fsdp", None),
        P("replica", "fsdp", None),
        P("fsdp", None),
        P("fsdp", "replica"),
        P("fsdp", "replica"),
    )
    out_specs = (P("replica", "fsdp", None), P("fsdp", "replica"), P("fsdp", "replica"))
    return jax.shard_map(
        on_device, mesh=mesh, in_specs=in_specs, out_specs=out_specs, check_vma=False
    )
```

```python
import functools
import math

import jax
import jax.numpy as jnp
from jax import lax
from jax.experimental import pallas as pl
from jax.experimental.pallas import tpu as pltpu
from jax.sharding import PartitionSpec as P

BLOCK = 64


norm_eps = 1e-05
inner_gain = 0.4
outer_rate = 0.7
outer_beta = 0.9
mix_weight = 0.5
code_range = 448.0


def swap(value, axis, mask):
    size = lax.axis_size(axis)
    return lax.ppermute(value, axis, [(i, i ^ mask) for i in range(size)])


def prepare_kernel(tokens_ref, gain_ref, blocks_ref, tokens, blocks, load_sems, store_sems):
    lanes = 128
    shards, rows, count = blocks.shape
    features = shards * rows
    loads, stores = [], []
    for k in range(shards):
        columns = pl.ds(k * rows, rows)
        loads.append(pltpu.make_async_copy(tokens_ref.at[:, columns], tokens.at[:, columns], load_sems.at[k]))
        loads[k].start()
        stores.append(pltpu.make_async_copy(blocks.at[k], blocks_ref.at[k], store_sems.at[k]))
    squares = jnp.zeros((count, lanes), jnp.float32)
    for k in range(shards):
        loads[k].wait()
        for start in range(k * rows, (k + 1) * rows, lanes):
            block = tokens[:, start : start + lanes].astype(jnp.float32)
            squares = squares + block * block
    mean = jnp.sum(squares, axis=-1, keepdims=True) / features
    inverse = jnp.broadcast_to(lax.rsqrt(mean + norm_eps), (count, lanes))
    for k in range(shards):
        for start in range(0, rows, lanes):
            columns = slice(k * rows + start, k * rows + start + lanes)
            normed = tokens[:, columns].astype(jnp.float32) * inverse * gain_ref[:, columns]
            blocks[k, start : start + lanes] = jnp.transpose(normed).astype(jnp.bfloat16)
        stores[k].start()
    for store in stores:
        store.wait()


def prepare(tokens, gain, shards):
    count, features = tokens.shape
    rows = features // shards
    return pl.pallas_call(
        prepare_kernel,
        out_shape=jax.ShapeDtypeStruct((shards, rows, count), jnp.bfloat16),
        in_specs=[pl.BlockSpec(memory_space=pltpu.HBM), pl.BlockSpec(memory_space=pltpu.VMEM)],
        out_specs=pl.BlockSpec(memory_space=pltpu.HBM),
        scratch_shapes=[
            pltpu.VMEM((count, features), jnp.bfloat16),
            pltpu.VMEM((shards, rows, count), jnp.bfloat16),
            pltpu.SemaphoreType.DMA((shards,)),
            pltpu.SemaphoreType.DMA((shards,)),
        ],
        compiler_params=pltpu.CompilerParams(vmem_limit_bytes=16 * 2**20),
        cost_estimate=pl.CostEstimate(
            flops=5 * count * features, bytes_accessed=4 * count * features, transcendentals=count
        ),
        name="prepare",
    )(tokens, gain.astype(jnp.float32).reshape(1, features))


def code_kernel(own_ref, shared_ref, weight_ref, kept_ref, sent_ref, shared, weight, decoded, sems):
    lanes = 2 * BLOCK
    groups, tile, share = decoded.shape
    rows, width = shared.shape
    own = own_ref[0]
    low = lax.broadcasted_iota(jnp.int32, (tile, lanes), 1) < BLOCK

    def loads(i):
        part = pl.ds(pl.multiple_of(i * tile, tile), tile)
        return (
            pltpu.make_async_copy(shared_ref.at[part], shared.at[part], sems.at[0, i]),
            pltpu.make_async_copy(weight_ref.at[part], weight.at[part], sems.at[1, i]),
        )

    for i in range(rows // tile):
        for load in loads(i):
            load.start()

    def step(i, _):
        for load in loads(i):
            load.wait()
        part = pl.ds(pl.multiple_of(i * tile, tile), tile)
        for start in range(0, width, lanes):
            columns = slice(start, start + lanes)
            delta = shared[part, columns].astype(jnp.float32) - weight[part, columns].astype(jnp.float32)
            size = jnp.abs(delta)
            largest = jnp.where(
                low,
                jnp.max(jnp.where(low, size, 0.0), axis=-1, keepdims=True),
                jnp.max(jnp.where(low, 0.0, size), axis=-1, keepdims=True),
            )
            scale = ((largest + 1e-06) * (1.0 / code_range)).astype(jnp.bfloat16).astype(jnp.float32)
            coded = (delta * pl.reciprocal(scale)).astype(jnp.bfloat16)
            value = (coded.astype(jnp.float32) * scale).astype(jnp.bfloat16)
            piece = min(share, lanes)
            for at in range(0, lanes, piece):
                group, offset = divmod(start + at, share)
                decoded[group, :, offset : offset + piece] = value[:, at : at + piece]
        for k in range(0, groups, 2):
            kept_ref[k // 2, part] = decoded[own ^ k]
            sent_ref[k // 2, part] = decoded[own ^ (k + 1)]
        return 0

    lax.fori_loop(0, rows // tile, step, 0)


def code_and_decode(own, shared, weight, groups):
    rows, width = shared.shape
    tile = min(rows, 128)
    share = width // groups
    half = jax.ShapeDtypeStruct((groups // 2, rows, share), jnp.bfloat16)
    return pl.pallas_call(
        code_kernel,
        out_shape=(half, half),
        in_specs=[pl.BlockSpec(memory_space=pltpu.SMEM)] + [pl.BlockSpec(memory_space=pltpu.HBM)] * 2,
        out_specs=(pl.BlockSpec(memory_space=pltpu.VMEM),) * 2,
        scratch_shapes=[
            pltpu.VMEM((rows, width), jnp.bfloat16),
            pltpu.VMEM((rows, width), jnp.bfloat16),
            pltpu.VMEM((groups, tile, share), jnp.bfloat16),
            pltpu.SemaphoreType.DMA((2, rows // tile)),
        ],
        compiler_params=pltpu.CompilerParams(vmem_limit_bytes=16 * 2**20),
        cost_estimate=pl.CostEstimate(flops=20 * rows * width, bytes_accessed=6 * rows * width, transcendentals=0),
        name="code_and_decode",
    )(own.reshape(1), shared, weight)


def accumulate_kernel(parts, rate, mine_ref, tokens_ref, weight_ref, *refs):
    cotangent_refs, refs = refs[:parts], refs[parts:]
    total_ref, last_ref, tokens, cotangents, weight, token_sems, cotangent_sems, last_sem, weight_sem = refs
    mine = mine_ref[0]
    depth, width = cotangent_refs[0].shape
    tile = min(width, 256)

    loads = []
    for k, ref in enumerate(cotangent_refs):
        loads.append(pltpu.make_async_copy(tokens_ref.at[mine ^ k], tokens.at[k], token_sems.at[k]))
        loads.append(pltpu.make_async_copy(ref, cotangents.at[pl.ds(k * depth, depth)], cotangent_sems.at[k]))
    loads.append(pltpu.make_async_copy(weight_ref, weight, weight_sem))
    loads.append(pltpu.make_async_copy(tokens_ref.at[mine ^ parts], last_ref, last_sem))
    for load in loads:
        load.start()
    some = 2
    for first in range(0, parts, some):
        end = min(first + some, parts)
        for load in loads[2 * first : 2 * end]:
            load.wait()
        left = jnp.concatenate([tokens[k] for k in range(first, end)], axis=1)
        for start in range(0, width, tile):
            columns = slice(start, start + tile)
            right = cotangents[first * depth : end * depth, columns]
            total = jnp.dot(left, right, preferred_element_type=jnp.float32)
            if first:
                total = total_ref[:, columns] + total
            if end == parts:
                if start == 0:
                    loads[-2].wait()
                total = mix_weight * weight[:, columns].astype(jnp.float32) - rate * total
            total_ref[:, columns] = total
    loads[-1].wait()


def accumulate(mine, tokens, cotangents, weight, rate):
    shards, rows, depth = tokens.shape
    parts = shards - 1
    width = cotangents[0].shape[1]
    return pl.pallas_call(
        functools.partial(accumulate_kernel, parts, rate),
        out_shape=(jax.ShapeDtypeStruct((rows, width), jnp.float32), jax.ShapeDtypeStruct((rows, depth), jnp.bfloat16)),
        in_specs=[pl.BlockSpec(memory_space=pltpu.SMEM)] + [pl.BlockSpec(memory_space=pltpu.HBM)] * (2 + parts),
        out_specs=(pl.BlockSpec(memory_space=pltpu.VMEM),) * 2,
        scratch_shapes=[
            pltpu.VMEM((parts, rows, depth), jnp.bfloat16),
            pltpu.VMEM((parts * depth, width), jnp.bfloat16),
            pltpu.VMEM((rows, width), jnp.bfloat16),
            pltpu.SemaphoreType.DMA((parts,)),
            pltpu.SemaphoreType.DMA((parts,)),
            pltpu.SemaphoreType.DMA,
            pltpu.SemaphoreType.DMA,
        ],
        compiler_params=pltpu.CompilerParams(vmem_limit_bytes=40 * 2**20),
        cost_estimate=pl.CostEstimate(
            flops=2 * depth * parts * rows * width,
            bytes_accessed=2 * depth * shards * (rows + width) + 4 * rows * width,
            transcendentals=0,
        ),
        name="accumulate",
    )(mine.reshape(1), tokens, weight, *cotangents)


def finish_kernel(groups, rate, own_ref, tokens_ref, cotangent_ref, total_ref, *refs):
    piece_refs, (out_ref, pieces, outs, sems) = refs[:groups], refs[groups:]
    share = pieces.shape[2]
    steps, _, tile = outs.shape
    for k, ref in enumerate(piece_refs):
        pieces[own_ref[0] ^ k] = ref[...]
    stores = []
    for step in range(steps):
        columns = slice(step * tile, (step + 1) * tile)
        product = jnp.dot(tokens_ref[...], cotangent_ref[:, columns], preferred_element_type=jnp.float32)
        total = total_ref[:, columns] - rate * product
        for group in range(step * tile // share, (step + 1) * tile // share):
            part = slice(group * share - step * tile, (group + 1) * share - step * tile)
            shared = pieces[group].astype(jnp.float32)
            outs[step, :, part] = (total[:, part] + (1.0 - mix_weight) * shared).astype(jnp.bfloat16)
        stores.append(pltpu.make_async_copy(outs.at[step], out_ref.at[:, pl.ds(step * tile, tile)], sems.at[step]))
        stores[step].start()
    for store in stores:
        store.wait()


def finish(own, tokens, cotangent, total, pieces, rate):
    rows, width = total.shape
    depth = tokens.shape[1]
    groups = len(pieces)
    share = width // groups
    tile = max(share, 256)
    return pl.pallas_call(
        functools.partial(finish_kernel, groups, rate),
        out_shape=jax.ShapeDtypeStruct((rows, width), jnp.bfloat16),
        in_specs=[pl.BlockSpec(memory_space=pltpu.SMEM)] + [pl.BlockSpec(memory_space=pltpu.VMEM)] * (3 + groups),
        out_specs=pl.BlockSpec(memory_space=pltpu.HBM),
        scratch_shapes=[
            pltpu.VMEM((groups, rows, share), jnp.bfloat16),
            pltpu.VMEM((width // tile, rows, tile), jnp.bfloat16),
            pltpu.SemaphoreType.DMA((width // tile,)),
        ],
        compiler_params=pltpu.CompilerParams(vmem_limit_bytes=16 * 2**20),
        cost_estimate=pl.CostEstimate(
            flops=2 * depth * rows * width, bytes_accessed=2 * depth * (rows + width) + 8 * rows * width, transcendentals=0
        ),
        name="finish",
    )(own.reshape(1), tokens, cotangent, total, *pieces)


def gather(piece, axis, size):
    pieces = {0: piece}
    bit = size // 2
    while bit:
        for k in sorted(pieces):
            pieces[k ^ bit] = swap(pieces[k], axis, bit)
        bit //= 2
    return [pieces[k] for k in range(size)]


def on_device(tokens, norm_gain, cotangent, layer_weight, shared_copy, master, momentum):
    tokens, cotangent, weight = tokens[0], cotangent[0], layer_weight[0]
    shards = lax.axis_size("fsdp")
    groups = lax.axis_size("replica")
    mine = lax.axis_index("fsdp")
    own = lax.axis_index("replica")
    rows, width = weight.shape
    inner_rate = inner_gain / math.sqrt(tokens.shape[0] * shards)

    own_exchanges = [1 << bit for bit in range(shards.bit_length() - 1)]
    cotangents = gather(cotangent, "fsdp", shards)
    blocks = prepare(tokens, norm_gain, shards)
    *_, blocks, coded_shared, coded_weight = lax.optimization_barrier(
        (*(cotangents[k] for k in own_exchanges), blocks, shared_copy, weight)
    )
    columns = lax.all_to_all(blocks, "fsdp", split_axis=0, concat_axis=0, tiled=True)

    kept, sent = code_and_decode(own, coded_shared, coded_weight, groups)
    total = kept.astype(jnp.float32) + swap(sent, "replica", 1).astype(jnp.float32)
    bit = 2
    while bit < groups:
        sent = swap(total[1::2].astype(jnp.bfloat16), "replica", bit)
        bit *= 2
        total = total[0::2] + sent.astype(jnp.float32)
    average = total[0] / groups
    momentum_next = outer_beta * momentum + average
    master_next = master - outer_rate * (average + outer_beta * momentum_next)
    pieces = gather(master_next.astype(jnp.bfloat16), "replica", groups)

    rate = (1.0 - mix_weight) * inner_rate
    total, last = accumulate(mine, columns, cotangents[:-1], weight, rate)
    layer_next = finish(own, last, cotangents[-1], total, pieces, rate)
    return (layer_next[None], master_next, momentum_next)


def solution(mesh):
    in_specs = (
        P("replica", "fsdp", None),
        P(),
        P("replica", "fsdp", None),
        P("replica", "fsdp", None),
        P("fsdp", None),
        P("fsdp", "replica"),
        P("fsdp", "replica"),
    )
    out_specs = (P("replica", "fsdp", None), P("fsdp", "replica"), P("fsdp", "replica"))
    return jax.shard_map(
        on_device, mesh=mesh, in_specs=in_specs, out_specs=out_specs, check_vma=False
    )
```

```python
import functools
import math

import jax
import jax.numpy as jnp
from jax import lax
from jax.experimental import pallas as pl
from jax.experimental.pallas import tpu as pltpu
from jax.sharding import PartitionSpec as P

BLOCK = 64


norm_eps = 1e-05
inner_gain = 0.4
outer_rate = 0.7
outer_beta = 0.9
mix_weight = 0.5
code_range = 448.0


def swap(value, axis, mask):
    size = lax.axis_size(axis)
    return lax.ppermute(value, axis, [(i, i ^ mask) for i in range(size)])


def prepare_kernel(tokens_ref, gain_ref, blocks_ref, tokens, blocks, load_sems, store_sems):
    lanes = 128
    shards, rows, count = blocks.shape
    features = shards * rows
    loads, stores = [], []
    for k in range(shards):
        columns = pl.ds(k * rows, rows)
        loads.append(pltpu.make_async_copy(tokens_ref.at[:, columns], tokens.at[:, columns], load_sems.at[k]))
        loads[k].start()
        stores.append(pltpu.make_async_copy(blocks.at[k], blocks_ref.at[k], store_sems.at[k]))
    squares = jnp.zeros((count, lanes), jnp.float32)
    for k in range(shards):
        loads[k].wait()
        for start in range(k * rows, (k + 1) * rows, lanes):
            block = tokens[:, start : start + lanes].astype(jnp.float32)
            squares = squares + block * block
    mean = jnp.sum(squares, axis=-1, keepdims=True) / features
    inverse = jnp.broadcast_to(lax.rsqrt(mean + norm_eps), (count, lanes))
    for k in range(shards):
        for start in range(0, rows, lanes):
            columns = slice(k * rows + start, k * rows + start + lanes)
            normed = tokens[:, columns].astype(jnp.float32) * inverse * gain_ref[:, columns]
            blocks[k, start : start + lanes] = jnp.transpose(normed).astype(jnp.bfloat16)
        stores[k].start()
    for store in stores:
        store.wait()


def prepare(tokens, gain, shards):
    count, features = tokens.shape
    rows = features // shards
    return pl.pallas_call(
        prepare_kernel,
        out_shape=jax.ShapeDtypeStruct((shards, rows, count), jnp.bfloat16),
        in_specs=[pl.BlockSpec(memory_space=pltpu.HBM), pl.BlockSpec(memory_space=pltpu.VMEM)],
        out_specs=pl.BlockSpec(memory_space=pltpu.HBM),
        scratch_shapes=[
            pltpu.VMEM((count, features), jnp.bfloat16),
            pltpu.VMEM((shards, rows, count), jnp.bfloat16),
            pltpu.SemaphoreType.DMA((shards,)),
            pltpu.SemaphoreType.DMA((shards,)),
        ],
        compiler_params=pltpu.CompilerParams(vmem_limit_bytes=16 * 2**20),
        cost_estimate=pl.CostEstimate(
            flops=5 * count * features, bytes_accessed=4 * count * features, transcendentals=count
        ),
        name="prepare",
    )(tokens, gain.astype(jnp.float32).reshape(1, features))


def code_kernel(own_ref, shared_ref, weight_ref, kept_ref, sent_ref, shared, weight, decoded, sems):
    lanes = 2 * BLOCK
    groups, tile, share = decoded.shape
    rows, width = shared.shape
    own = own_ref[0]
    low = lax.broadcasted_iota(jnp.int32, (tile, lanes), 1) < BLOCK

    def loads(i):
        part = pl.ds(pl.multiple_of(i * tile, tile), tile)
        return (
            pltpu.make_async_copy(shared_ref.at[part], shared.at[part], sems.at[0, i]),
            pltpu.make_async_copy(weight_ref.at[part], weight.at[part], sems.at[1, i]),
        )

    for i in range(rows // tile):
        for load in loads(i):
            load.start()

    def step(i, _):
        for load in loads(i):
            load.wait()
        part = pl.ds(pl.multiple_of(i * tile, tile), tile)
        for start in range(0, width, lanes):
            columns = slice(start, start + lanes)
            delta = shared[part, columns].astype(jnp.float32) - weight[part, columns].astype(jnp.float32)
            size = jnp.abs(delta)
            largest = jnp.where(
                low,
                jnp.max(jnp.where(low, size, 0.0), axis=-1, keepdims=True),
                jnp.max(jnp.where(low, 0.0, size), axis=-1, keepdims=True),
            )
            scale = ((largest + 1e-06) * (1.0 / code_range)).astype(jnp.bfloat16).astype(jnp.float32)
            coded = (delta * pl.reciprocal(scale)).astype(jnp.bfloat16)
            value = (coded.astype(jnp.float32) * scale).astype(jnp.bfloat16)
            piece = min(share, lanes)
            for at in range(0, lanes, piece):
                group, offset = divmod(start + at, share)
                decoded[group, :, offset : offset + piece] = value[:, at : at + piece]
        for k in range(0, groups, 2):
            kept_ref[k // 2, part] = decoded[own ^ k]
            sent_ref[k // 2, part] = decoded[own ^ (k + 1)]
        return 0

    lax.fori_loop(0, rows // tile, step, 0)


def code_and_decode(own, shared, weight, groups):
    rows, width = shared.shape
    tile = min(rows, 128)
    share = width // groups
    half = jax.ShapeDtypeStruct((groups // 2, rows, share), jnp.bfloat16)
    return pl.pallas_call(
        code_kernel,
        out_shape=(half, half),
        in_specs=[pl.BlockSpec(memory_space=pltpu.SMEM)] + [pl.BlockSpec(memory_space=pltpu.HBM)] * 2,
        out_specs=(pl.BlockSpec(memory_space=pltpu.VMEM),) * 2,
        scratch_shapes=[
            pltpu.VMEM((rows, width), jnp.bfloat16),
            pltpu.VMEM((rows, width), jnp.bfloat16),
            pltpu.VMEM((groups, tile, share), jnp.bfloat16),
            pltpu.SemaphoreType.DMA((2, rows // tile)),
        ],
        compiler_params=pltpu.CompilerParams(vmem_limit_bytes=16 * 2**20),
        cost_estimate=pl.CostEstimate(flops=20 * rows * width, bytes_accessed=6 * rows * width, transcendentals=0),
        name="code_and_decode",
    )(own.reshape(1), shared, weight)


def accumulate_kernel(parts, rate, mine_ref, tokens_ref, weight_ref, *refs):
    cotangent_refs, refs = refs[:parts], refs[parts:]
    total_ref, last_ref, tokens, cotangents, weight, token_sems, cotangent_sems, last_sem, weight_sem = refs
    mine = mine_ref[0]
    depth, width = cotangent_refs[0].shape
    tile = min(width, 256)

    loads = []
    for k, ref in enumerate(cotangent_refs):
        loads.append(pltpu.make_async_copy(tokens_ref.at[mine ^ k], tokens.at[k], token_sems.at[k]))
        loads.append(pltpu.make_async_copy(ref, cotangents.at[pl.ds(k * depth, depth)], cotangent_sems.at[k]))
    loads.append(pltpu.make_async_copy(weight_ref, weight, weight_sem))
    loads.append(pltpu.make_async_copy(tokens_ref.at[mine ^ parts], last_ref, last_sem))
    for load in loads:
        load.start()
    some = 2
    for first in range(0, parts, some):
        end = min(first + some, parts)
        for load in loads[2 * first : 2 * end]:
            load.wait()
        left = jnp.concatenate([tokens[k] for k in range(first, end)], axis=1)
        for start in range(0, width, tile):
            columns = slice(start, start + tile)
            right = cotangents[first * depth : end * depth, columns]
            total = jnp.dot(left, right, preferred_element_type=jnp.float32)
            if first:
                total = total_ref[:, columns] + total
            if end == parts:
                if start == 0:
                    loads[-2].wait()
                total = mix_weight * weight[:, columns].astype(jnp.float32) - rate * total
            total_ref[:, columns] = total
    loads[-1].wait()


def accumulate(mine, tokens, cotangents, weight, rate):
    shards, rows, depth = tokens.shape
    parts = shards - 1
    width = cotangents[0].shape[1]
    return pl.pallas_call(
        functools.partial(accumulate_kernel, parts, rate),
        out_shape=(jax.ShapeDtypeStruct((rows, width), jnp.float32), jax.ShapeDtypeStruct((rows, depth), jnp.bfloat16)),
        in_specs=[pl.BlockSpec(memory_space=pltpu.SMEM)] + [pl.BlockSpec(memory_space=pltpu.HBM)] * (2 + parts),
        out_specs=(pl.BlockSpec(memory_space=pltpu.VMEM),) * 2,
        scratch_shapes=[
            pltpu.VMEM((parts, rows, depth), jnp.bfloat16),
            pltpu.VMEM((parts * depth, width), jnp.bfloat16),
            pltpu.VMEM((rows, width), jnp.bfloat16),
            pltpu.SemaphoreType.DMA((parts,)),
            pltpu.SemaphoreType.DMA((parts,)),
            pltpu.SemaphoreType.DMA,
            pltpu.SemaphoreType.DMA,
        ],
        compiler_params=pltpu.CompilerParams(vmem_limit_bytes=40 * 2**20),
        cost_estimate=pl.CostEstimate(
            flops=2 * depth * parts * rows * width,
            bytes_accessed=2 * depth * shards * (rows + width) + 4 * rows * width,
            transcendentals=0,
        ),
        name="accumulate",
    )(mine.reshape(1), tokens, weight, *cotangents)


def finish_kernel(groups, rate, own_ref, tokens_ref, cotangent_ref, total_ref, *refs):
    piece_refs, (out_ref, pieces, outs, sems) = refs[:groups], refs[groups:]
    share = pieces.shape[2]
    steps, _, tile = outs.shape
    own = own_ref[0]

    def store(step, columns):
        return pltpu.make_async_copy(outs.at[step], out_ref.at[:, columns], sems.at[step])

    def total_of(columns):
        product = jnp.dot(tokens_ref[...], cotangent_ref[:, columns], preferred_element_type=jnp.float32)
        return total_ref[:, columns] - rate * product

    places = []
    if share == tile:
        for k, ref in enumerate(piece_refs):
            places.append(pl.ds(pl.multiple_of((own ^ k) * share, share), share))
            shared = ref[...].astype(jnp.float32)
            outs[k] = (total_of(places[k]) + (1.0 - mix_weight) * shared).astype(jnp.bfloat16)
            store(k, places[k]).start()
    else:
        for k, ref in enumerate(piece_refs):
            pieces[own ^ k] = ref[...]
        for step in range(steps):
            places.append(pl.ds(step * tile, tile))
            total = total_of(slice(step * tile, (step + 1) * tile))
            for group in range(step * tile // share, (step + 1) * tile // share):
                part = slice(group * share - step * tile, (group + 1) * share - step * tile)
                shared = pieces[group].astype(jnp.float32)
                outs[step, :, part] = (total[:, part] + (1.0 - mix_weight) * shared).astype(jnp.bfloat16)
            store(step, places[step]).start()
    for step in range(steps):
        store(step, places[step]).wait()


def finish(own, tokens, cotangent, total, pieces, rate):
    rows, width = total.shape
    depth = tokens.shape[1]
    groups = len(pieces)
    share = width // groups
    tile = max(share, 256)
    return pl.pallas_call(
        functools.partial(finish_kernel, groups, rate),
        out_shape=jax.ShapeDtypeStruct((rows, width), jnp.bfloat16),
        in_specs=[pl.BlockSpec(memory_space=pltpu.SMEM)] + [pl.BlockSpec(memory_space=pltpu.VMEM)] * (3 + groups),
        out_specs=pl.BlockSpec(memory_space=pltpu.HBM),
        scratch_shapes=[
            pltpu.VMEM((groups, rows, share), jnp.bfloat16),
            pltpu.VMEM((width // tile, rows, tile), jnp.bfloat16),
            pltpu.SemaphoreType.DMA((width // tile,)),
        ],
        compiler_params=pltpu.CompilerParams(vmem_limit_bytes=16 * 2**20),
        cost_estimate=pl.CostEstimate(
            flops=2 * depth * rows * width, bytes_accessed=2 * depth * (rows + width) + 8 * rows * width, transcendentals=0
        ),
        name="finish",
    )(own.reshape(1), tokens, cotangent, total, *pieces)


def gather(piece, axis, size, after=()):
    pieces = {0: piece}
    bit = size // 2
    while bit:
        for k in sorted(pieces):
            value = lax.optimization_barrier((pieces[k], *after))[0] if k and bit == 1 else pieces[k]
            pieces[k ^ bit] = swap(value, axis, bit)
        bit //= 2
    return [pieces[k] for k in range(size)]


def on_device(tokens, norm_gain, cotangent, layer_weight, shared_copy, master, momentum):
    tokens, cotangent, weight = tokens[0], cotangent[0], layer_weight[0]
    shards = lax.axis_size("fsdp")
    groups = lax.axis_size("replica")
    mine = lax.axis_index("fsdp")
    own = lax.axis_index("replica")
    rows, width = weight.shape
    inner_rate = inner_gain / math.sqrt(tokens.shape[0] * shards)

    own_exchanges = [1 << bit for bit in range(shards.bit_length() - 1)]
    cotangents = gather(cotangent, "fsdp", shards)
    blocks = prepare(tokens, norm_gain, shards)
    *_, blocks, coded_shared, coded_weight = lax.optimization_barrier(
        (*(cotangents[k] for k in own_exchanges), blocks, shared_copy, weight)
    )
    columns = lax.all_to_all(blocks, "fsdp", split_axis=0, concat_axis=0, tiled=True)

    kept, sent = code_and_decode(own, coded_shared, coded_weight, groups)
    total = kept.astype(jnp.float32) + swap(sent, "replica", 1).astype(jnp.float32)
    bit = 2
    while bit < groups:
        sent = swap(total[1::2].astype(jnp.bfloat16), "replica", bit)
        bit *= 2
        total = total[0::2] + sent.astype(jnp.float32)
    average = total[0] / groups
    momentum_next = outer_beta * momentum + average
    master_next = master - outer_rate * (average + outer_beta * momentum_next)
    pieces = gather(master_next.astype(jnp.bfloat16), "replica", groups, after=cotangents[:-1])

    rate = (1.0 - mix_weight) * inner_rate
    total, last = accumulate(mine, columns, cotangents[:-1], weight, rate)
    layer_next = finish(own, last, cotangents[-1], total, pieces, rate)
    return (layer_next[None], master_next, momentum_next)


def solution(mesh):
    in_specs = (
        P("replica", "fsdp", None),
        P(),
        P("replica", "fsdp", None),
        P("replica", "fsdp", None),
        P("fsdp", None),
        P("fsdp", "replica"),
        P("fsdp", "replica"),
    )
    out_specs = (P("replica", "fsdp", None), P("fsdp", "replica"), P("fsdp", "replica"))
    return jax.shard_map(
        on_device, mesh=mesh, in_specs=in_specs, out_specs=out_specs, check_vma=False
    )
```

```python
import functools
import math

import jax
import jax.numpy as jnp
from jax import lax
from jax.experimental import pallas as pl
from jax.experimental.pallas import tpu as pltpu
from jax.sharding import PartitionSpec as P

BLOCK = 64


norm_eps = 1e-05
inner_gain = 0.4
outer_rate = 0.7
outer_beta = 0.9
mix_weight = 0.5
code_range = 448.0


def swap(value, axis, mask):
    size = lax.axis_size(axis)
    return lax.ppermute(value, axis, [(i, i ^ mask) for i in range(size)])


def prepare_kernel(tokens_ref, gain_ref, blocks_ref, tokens, blocks, load_sems, store_sems):
    lanes = 128
    shards, rows, count = blocks.shape
    features = shards * rows
    loads, stores = [], []
    for k in range(shards):
        columns = pl.ds(k * rows, rows)
        loads.append(pltpu.make_async_copy(tokens_ref.at[:, columns], tokens.at[:, columns], load_sems.at[k]))
        loads[k].start()
        stores.append(pltpu.make_async_copy(blocks.at[k], blocks_ref.at[k], store_sems.at[k]))
    squares = jnp.zeros((count, lanes), jnp.float32)
    for k in range(shards):
        loads[k].wait()
        for start in range(k * rows, (k + 1) * rows, lanes):
            block = tokens[:, start : start + lanes].astype(jnp.float32)
            squares = squares + block * block
    mean = jnp.sum(squares, axis=-1, keepdims=True) / features
    inverse = jnp.broadcast_to(lax.rsqrt(mean + norm_eps), (count, lanes))
    for k in range(shards):
        for start in range(0, rows, lanes):
            columns = slice(k * rows + start, k * rows + start + lanes)
            normed = tokens[:, columns].astype(jnp.float32) * inverse * gain_ref[:, columns]
            blocks[k, start : start + lanes] = jnp.transpose(normed).astype(jnp.bfloat16)
        stores[k].start()
    for store in stores:
        store.wait()


def prepare(tokens, gain, shards):
    count, features = tokens.shape
    rows = features // shards
    return pl.pallas_call(
        prepare_kernel,
        out_shape=jax.ShapeDtypeStruct((shards, rows, count), jnp.bfloat16),
        in_specs=[pl.BlockSpec(memory_space=pltpu.HBM), pl.BlockSpec(memory_space=pltpu.VMEM)],
        out_specs=pl.BlockSpec(memory_space=pltpu.HBM),
        scratch_shapes=[
            pltpu.VMEM((count, features), jnp.bfloat16),
            pltpu.VMEM((shards, rows, count), jnp.bfloat16),
            pltpu.SemaphoreType.DMA((shards,)),
            pltpu.SemaphoreType.DMA((shards,)),
        ],
        compiler_params=pltpu.CompilerParams(vmem_limit_bytes=16 * 2**20),
        cost_estimate=pl.CostEstimate(
            flops=5 * count * features, bytes_accessed=4 * count * features, transcendentals=count
        ),
        name="prepare",
    )(tokens, gain.astype(jnp.float32).reshape(1, features))


def code_kernel(own_ref, shared_ref, weight_ref, kept_ref, sent_ref, shared, weight, decoded, sems):
    lanes = 2 * BLOCK
    groups, tile, share = decoded.shape
    rows, width = shared.shape
    own = own_ref[0]
    low = lax.broadcasted_iota(jnp.int32, (tile, lanes), 1) < BLOCK

    def loads(i):
        part = pl.ds(pl.multiple_of(i * tile, tile), tile)
        return (
            pltpu.make_async_copy(shared_ref.at[part], shared.at[part], sems.at[0, i]),
            pltpu.make_async_copy(weight_ref.at[part], weight.at[part], sems.at[1, i]),
        )

    for i in range(rows // tile):
        for load in loads(i):
            load.start()

    def step(i, _):
        for load in loads(i):
            load.wait()
        part = pl.ds(pl.multiple_of(i * tile, tile), tile)
        for start in range(0, width, lanes):
            columns = slice(start, start + lanes)
            delta = shared[part, columns].astype(jnp.float32) - weight[part, columns].astype(jnp.float32)
            size = jnp.abs(delta)
            largest = jnp.where(
                low,
                jnp.max(jnp.where(low, size, 0.0), axis=-1, keepdims=True),
                jnp.max(jnp.where(low, 0.0, size), axis=-1, keepdims=True),
            )
            scale = ((largest + 1e-06) * (1.0 / code_range)).astype(jnp.bfloat16).astype(jnp.float32)
            coded = (delta * pl.reciprocal(scale)).astype(jnp.bfloat16)
            value = (coded.astype(jnp.float32) * scale).astype(jnp.bfloat16)
            piece = min(share, lanes)
            for at in range(0, lanes, piece):
                group, offset = divmod(start + at, share)
                decoded[group, :, offset : offset + piece] = value[:, at : at + piece]
        for k in range(0, groups, 2):
            kept_ref[k // 2, part] = decoded[own ^ k]
            sent_ref[k // 2, part] = decoded[own ^ (k + 1)]
        return 0

    lax.fori_loop(0, rows // tile, step, 0)


def code_and_decode(own, shared, weight, groups):
    rows, width = shared.shape
    tile = min(rows, 128)
    share = width // groups
    half = jax.ShapeDtypeStruct((groups // 2, rows, share), jnp.bfloat16)
    return pl.pallas_call(
        code_kernel,
        out_shape=(half, half),
        in_specs=[pl.BlockSpec(memory_space=pltpu.SMEM)] + [pl.BlockSpec(memory_space=pltpu.HBM)] * 2,
        out_specs=(pl.BlockSpec(memory_space=pltpu.VMEM),) * 2,
        scratch_shapes=[
            pltpu.VMEM((rows, width), jnp.bfloat16),
            pltpu.VMEM((rows, width), jnp.bfloat16),
            pltpu.VMEM((groups, tile, share), jnp.bfloat16),
            pltpu.SemaphoreType.DMA((2, rows // tile)),
        ],
        compiler_params=pltpu.CompilerParams(vmem_limit_bytes=16 * 2**20),
        cost_estimate=pl.CostEstimate(flops=20 * rows * width, bytes_accessed=6 * rows * width, transcendentals=0),
        name="code_and_decode",
    )(own.reshape(1), shared, weight)


def accumulate_kernel(parts, groups, rate, place_ref, tokens_ref, weight_ref, *refs):
    cotangent_refs, refs = refs[:parts], refs[parts:]
    piece_refs, refs = refs[: groups - 1], refs[groups - 1 :]
    total_ref, last_ref, tokens, cotangents, weight, pieces, token_sems, cotangent_sems, piece_sems, sems = refs
    mine, own = place_ref[0], place_ref[1]
    depth, width = cotangent_refs[0].shape
    share = pieces.shape[2]
    tile = max(share, 256)

    loads, rest = [], []
    for k, ref in enumerate(cotangent_refs):
        loads.append(pltpu.make_async_copy(tokens_ref.at[mine ^ k], tokens.at[k], token_sems.at[k]))
        loads.append(pltpu.make_async_copy(ref, cotangents.at[pl.ds(k * depth, depth)], cotangent_sems.at[k]))
    rest.append(pltpu.make_async_copy(weight_ref, weight, sems.at[0]))
    for k, ref in enumerate(piece_refs):
        rest.append(pltpu.make_async_copy(ref, pieces.at[own ^ k], piece_sems.at[k]))
    rest.append(pltpu.make_async_copy(tokens_ref.at[mine ^ parts], last_ref, sems.at[1]))
    for load in loads + rest:
        load.start()
    pieces[own ^ (groups - 1)] = jnp.zeros(pieces.shape[1:], pieces.dtype)
    some = 2
    for first in range(0, parts, some):
        end = min(first + some, parts)
        for load in loads[2 * first : 2 * end]:
            load.wait()
        left = jnp.concatenate([tokens[k] for k in range(first, end)], axis=1)
        for start in range(0, width, tile):
            columns = slice(start, start + tile)
            right = cotangents[first * depth : end * depth, columns]
            total = jnp.dot(left, right, preferred_element_type=jnp.float32)
            if first:
                total = total_ref[:, columns] + total
            if end < parts:
                total_ref[:, columns] = total
                continue
            if start == 0:
                for load in rest:
                    load.wait()
            for group in range(start // share, (start + tile) // share):
                place = slice(group * share, (group + 1) * share)
                part = slice(group * share - start, (group + 1) * share - start)
                mixed = mix_weight * weight[:, place].astype(jnp.float32)
                mixed = mixed + (1.0 - mix_weight) * pieces[group].astype(jnp.float32)
                total_ref[:, place] = mixed - rate * total[:, part]


def accumulate(mine, own, tokens, cotangents, weight, pieces, rate):
    shards, rows, depth = tokens.shape
    parts = shards - 1
    groups = len(pieces) + 1
    width = cotangents[0].shape[1]
    return pl.pallas_call(
        functools.partial(accumulate_kernel, parts, groups, rate),
        out_shape=(jax.ShapeDtypeStruct((rows, width), jnp.float32), jax.ShapeDtypeStruct((rows, depth), jnp.bfloat16)),
        in_specs=[pl.BlockSpec(memory_space=pltpu.SMEM)]
        + [pl.BlockSpec(memory_space=pltpu.HBM)] * (1 + parts + groups),
        out_specs=(pl.BlockSpec(memory_space=pltpu.VMEM),) * 2,
        scratch_shapes=[
            pltpu.VMEM((parts, rows, depth), jnp.bfloat16),
            pltpu.VMEM((parts * depth, width), jnp.bfloat16),
            pltpu.VMEM((rows, width), jnp.bfloat16),
            pltpu.VMEM((groups, rows, width // groups), jnp.bfloat16),
            pltpu.SemaphoreType.DMA((parts,)),
            pltpu.SemaphoreType.DMA((parts,)),
            pltpu.SemaphoreType.DMA((groups,)),
            pltpu.SemaphoreType.DMA((2,)),
        ],
        compiler_params=pltpu.CompilerParams(vmem_limit_bytes=58 * 2**20),
        cost_estimate=pl.CostEstimate(
            flops=2 * depth * parts * rows * width,
            bytes_accessed=2 * depth * shards * (rows + width) + 8 * rows * width,
            transcendentals=0,
        ),
        name="accumulate",
    )(jnp.stack([mine, own]), tokens, weight, *cotangents, *pieces)


def finish_kernel(groups, rate, own_ref, tokens_ref, cotangent_ref, total_ref, piece_ref, out_ref, outs, sems):
    share = piece_ref.shape[1]
    steps, _, tile = outs.shape
    stores = []
    for step in range(steps):
        columns = slice(step * tile, (step + 1) * tile)
        product = jnp.dot(tokens_ref[...], cotangent_ref[:, columns], preferred_element_type=jnp.float32)
        total = total_ref[:, columns] - rate * product
        for group in range(step * tile // share, (step + 1) * tile // share):
            part = slice(group * share - step * tile, (group + 1) * share - step * tile)
            factor = jnp.where((own_ref[0] ^ (groups - 1)) == group, 1.0 - mix_weight, 0.0)
            outs[step, :, part] = (total[:, part] + factor * piece_ref[...].astype(jnp.float32)).astype(jnp.bfloat16)
        stores.append(pltpu.make_async_copy(outs.at[step], out_ref.at[:, pl.ds(step * tile, tile)], sems.at[step]))
        stores[step].start()
    for store in stores:
        store.wait()


def finish(own, tokens, cotangent, total, piece, rate):
    rows, width = total.shape
    depth = tokens.shape[1]
    share = piece.shape[1]
    tile = max(share, 256)
    return pl.pallas_call(
        functools.partial(finish_kernel, width // share, rate),
        out_shape=jax.ShapeDtypeStruct((rows, width), jnp.bfloat16),
        in_specs=[pl.BlockSpec(memory_space=pltpu.SMEM)] + [pl.BlockSpec(memory_space=pltpu.VMEM)] * 4,
        out_specs=pl.BlockSpec(memory_space=pltpu.HBM),
        scratch_shapes=[pltpu.VMEM((width // tile, rows, tile), jnp.bfloat16), pltpu.SemaphoreType.DMA((width // tile,))],
        compiler_params=pltpu.CompilerParams(vmem_limit_bytes=16 * 2**20),
        cost_estimate=pl.CostEstimate(
            flops=2 * depth * rows * width, bytes_accessed=2 * depth * (rows + width) + 7 * rows * width, transcendentals=0
        ),
        name="finish",
    )(own.reshape(1), tokens, cotangent, total, piece)


def gather(piece, axis, size, after=()):
    pieces = {0: piece}
    bit = size // 2
    while bit:
        for k in sorted(pieces):
            value = lax.optimization_barrier((pieces[k], *after))[0] if k and bit == 1 else pieces[k]
            pieces[k ^ bit] = swap(value, axis, bit)
        bit //= 2
    return [pieces[k] for k in range(size)]


def on_device(tokens, norm_gain, cotangent, layer_weight, shared_copy, master, momentum):
    tokens, cotangent, weight = tokens[0], cotangent[0], layer_weight[0]
    shards = lax.axis_size("fsdp")
    groups = lax.axis_size("replica")
    mine = lax.axis_index("fsdp")
    own = lax.axis_index("replica")
    rows, width = weight.shape
    inner_rate = inner_gain / math.sqrt(tokens.shape[0] * shards)

    own_exchanges = [1 << bit for bit in range(shards.bit_length() - 1)]
    cotangents = gather(cotangent, "fsdp", shards)
    blocks = prepare(tokens, norm_gain, shards)
    *_, blocks, coded_shared, coded_weight = lax.optimization_barrier(
        (*(cotangents[k] for k in own_exchanges), blocks, shared_copy, weight)
    )
    columns = lax.all_to_all(blocks, "fsdp", split_axis=0, concat_axis=0, tiled=True)

    kept, sent = code_and_decode(own, coded_shared, coded_weight, groups)
    total = kept.astype(jnp.float32) + swap(sent, "replica", 1).astype(jnp.float32)
    bit = 2
    while bit < groups:
        sent = swap(total[1::2].astype(jnp.bfloat16), "replica", bit)
        bit *= 2
        total = total[0::2] + sent.astype(jnp.float32)
    average = total[0] / groups
    momentum_next = outer_beta * momentum + average
    master_next = master - outer_rate * (average + outer_beta * momentum_next)
    pieces = gather(master_next.astype(jnp.bfloat16), "replica", groups, after=cotangents[:-1])

    rate = (1.0 - mix_weight) * inner_rate
    total, last = accumulate(mine, own, columns, cotangents[:-1], weight, pieces[:-1], rate)
    layer_next = finish(own, last, cotangents[-1], total, pieces[-1], rate)
    return (layer_next[None], master_next, momentum_next)


def solution(mesh):
    in_specs = (
        P("replica", "fsdp", None),
        P(),
        P("replica", "fsdp", None),
        P("replica", "fsdp", None),
        P("fsdp", None),
        P("fsdp", "replica"),
        P("fsdp", "replica"),
    )
    out_specs = (P("replica", "fsdp", None), P("fsdp", "replica"), P("fsdp", "replica"))
    return jax.shard_map(
        on_device, mesh=mesh, in_specs=in_specs, out_specs=out_specs, check_vma=False
    )
```

```python
import functools
import math

import jax
import jax.numpy as jnp
from jax import lax
from jax.experimental import pallas as pl
from jax.experimental.pallas import tpu as pltpu
from jax.sharding import PartitionSpec as P

BLOCK = 64


norm_eps = 1e-05
inner_gain = 0.4
outer_rate = 0.7
outer_beta = 0.9
mix_weight = 0.5
code_range = 448.0


def swap(value, axis, mask):
    size = lax.axis_size(axis)
    return lax.ppermute(value, axis, [(i, i ^ mask) for i in range(size)])


def prepare_kernel(tokens_ref, gain_ref, blocks_ref, tokens, blocks, load_sems, store_sems):
    lanes = 128
    shards, rows, count = blocks.shape
    features = shards * rows
    loads, stores = [], []
    for k in range(shards):
        columns = pl.ds(k * rows, rows)
        loads.append(pltpu.make_async_copy(tokens_ref.at[:, columns], tokens.at[:, columns], load_sems.at[k]))
        loads[k].start()
        stores.append(pltpu.make_async_copy(blocks.at[k], blocks_ref.at[k], store_sems.at[k]))
    squares = jnp.zeros((count, lanes), jnp.float32)
    for k in range(shards):
        loads[k].wait()
        for start in range(k * rows, (k + 1) * rows, lanes):
            block = tokens[:, start : start + lanes].astype(jnp.float32)
            squares = squares + block * block
    mean = jnp.sum(squares, axis=-1, keepdims=True) / features
    inverse = jnp.broadcast_to(lax.rsqrt(mean + norm_eps), (count, lanes))
    for k in range(shards):
        for start in range(0, rows, lanes):
            columns = slice(k * rows + start, k * rows + start + lanes)
            normed = tokens[:, columns].astype(jnp.float32) * inverse * gain_ref[:, columns]
            blocks[k, start : start + lanes] = jnp.transpose(normed).astype(jnp.bfloat16)
        stores[k].start()
    for store in stores:
        store.wait()


def prepare(tokens, gain, shards):
    count, features = tokens.shape
    rows = features // shards
    return pl.pallas_call(
        prepare_kernel,
        out_shape=jax.ShapeDtypeStruct((shards, rows, count), jnp.bfloat16),
        in_specs=[pl.BlockSpec(memory_space=pltpu.HBM), pl.BlockSpec(memory_space=pltpu.VMEM)],
        out_specs=pl.BlockSpec(memory_space=pltpu.HBM),
        scratch_shapes=[
            pltpu.VMEM((count, features), jnp.bfloat16),
            pltpu.VMEM((shards, rows, count), jnp.bfloat16),
            pltpu.SemaphoreType.DMA((shards,)),
            pltpu.SemaphoreType.DMA((shards,)),
        ],
        compiler_params=pltpu.CompilerParams(vmem_limit_bytes=16 * 2**20),
        cost_estimate=pl.CostEstimate(
            flops=5 * count * features, bytes_accessed=4 * count * features, transcendentals=count
        ),
        name="prepare",
    )(tokens, gain.astype(jnp.float32).reshape(1, features))


def code_kernel(own_ref, shared_ref, weight_ref, kept_ref, sent_ref, shared, weight, decoded, sems):
    lanes = 2 * BLOCK
    groups, tile, share = decoded.shape
    rows, width = shared.shape
    own = own_ref[0]
    low = lax.broadcasted_iota(jnp.int32, (tile, lanes), 1) < BLOCK

    def loads(i):
        part = pl.ds(pl.multiple_of(i * tile, tile), tile)
        return (
            pltpu.make_async_copy(shared_ref.at[part], shared.at[part], sems.at[0, i]),
            pltpu.make_async_copy(weight_ref.at[part], weight.at[part], sems.at[1, i]),
        )

    for i in range(rows // tile):
        for load in loads(i):
            load.start()

    def step(i, _):
        for load in loads(i):
            load.wait()
        part = pl.ds(pl.multiple_of(i * tile, tile), tile)
        for start in range(0, width, lanes):
            columns = slice(start, start + lanes)
            delta = shared[part, columns].astype(jnp.float32) - weight[part, columns].astype(jnp.float32)
            size = jnp.abs(delta)
            largest = jnp.where(
                low,
                jnp.max(jnp.where(low, size, 0.0), axis=-1, keepdims=True),
                jnp.max(jnp.where(low, 0.0, size), axis=-1, keepdims=True),
            )
            scale = ((largest + 1e-06) * (1.0 / code_range)).astype(jnp.bfloat16).astype(jnp.float32)
            coded = (delta * pl.reciprocal(scale)).astype(jnp.bfloat16)
            value = (coded.astype(jnp.float32) * scale).astype(jnp.bfloat16)
            piece = min(share, lanes)
            for at in range(0, lanes, piece):
                group, offset = divmod(start + at, share)
                decoded[group, :, offset : offset + piece] = value[:, at : at + piece]
        for k in range(0, groups, 2):
            kept_ref[k // 2, part] = decoded[own ^ k]
            sent_ref[k // 2, part] = decoded[own ^ (k + 1)]
        return 0

    lax.fori_loop(0, rows // tile, step, 0)


def code_and_decode(own, shared, weight, groups):
    rows, width = shared.shape
    tile = min(rows, 128)
    share = width // groups
    half = jax.ShapeDtypeStruct((groups // 2, rows, share), jnp.bfloat16)
    return pl.pallas_call(
        code_kernel,
        out_shape=(half, half),
        in_specs=[pl.BlockSpec(memory_space=pltpu.SMEM)] + [pl.BlockSpec(memory_space=pltpu.HBM)] * 2,
        out_specs=(pl.BlockSpec(memory_space=pltpu.VMEM),) * 2,
        scratch_shapes=[
            pltpu.VMEM((rows, width), jnp.bfloat16),
            pltpu.VMEM((rows, width), jnp.bfloat16),
            pltpu.VMEM((groups, tile, share), jnp.bfloat16),
            pltpu.SemaphoreType.DMA((2, rows // tile)),
        ],
        compiler_params=pltpu.CompilerParams(vmem_limit_bytes=16 * 2**20),
        cost_estimate=pl.CostEstimate(flops=20 * rows * width, bytes_accessed=6 * rows * width, transcendentals=0),
        name="code_and_decode",
    )(own.reshape(1), shared, weight)


def accumulate_kernel(parts, groups, rate, mine_ref, own_ref, tokens_ref, weight_ref, *refs):
    cotangent_refs, refs = refs[:parts], refs[parts:]
    piece_refs, refs = refs[: groups - 1], refs[groups - 1 :]
    total_ref, last_ref, tokens, cotangents, weight, pieces, token_sems, cotangent_sems, piece_sems, sems = refs
    mine, own = mine_ref[0], own_ref[0]
    depth, width = cotangent_refs[0].shape
    share = pieces.shape[2]
    tile = max(share, 256)

    loads, rest = [], []
    for k, ref in enumerate(cotangent_refs):
        loads.append(pltpu.make_async_copy(tokens_ref.at[mine ^ k], tokens.at[k], token_sems.at[k]))
        loads.append(pltpu.make_async_copy(ref, cotangents.at[pl.ds(k * depth, depth)], cotangent_sems.at[k]))
    rest.append(pltpu.make_async_copy(weight_ref, weight, sems.at[0]))
    for k, ref in enumerate(piece_refs):
        rest.append(pltpu.make_async_copy(ref, pieces.at[own ^ k], piece_sems.at[k]))
    rest.append(pltpu.make_async_copy(tokens_ref.at[mine ^ parts], last_ref, sems.at[1]))
    for load in loads + rest:
        load.start()
    pieces[own ^ (groups - 1)] = jnp.zeros(pieces.shape[1:], pieces.dtype)
    some = 2
    for first in range(0, parts, some):
        end = min(first + some, parts)
        for load in loads[2 * first : 2 * end]:
            load.wait()
        left = jnp.concatenate([tokens[k] for k in range(first, end)], axis=1)
        for start in range(0, width, tile):
            columns = slice(start, start + tile)
            right = cotangents[first * depth : end * depth, columns]
            total = jnp.dot(left, right, preferred_element_type=jnp.float32)
            if first:
                total = total_ref[:, columns] + total
            if end < parts:
                total_ref[:, columns] = total
                continue
            if start == 0:
                for load in rest:
                    load.wait()
            for group in range(start // share, (start + tile) // share):
                place = slice(group * share, (group + 1) * share)
                part = slice(group * share - start, (group + 1) * share - start)
                mixed = mix_weight * weight[:, place].astype(jnp.float32)
                mixed = mixed + (1.0 - mix_weight) * pieces[group].astype(jnp.float32)
                total_ref[:, place] = mixed - rate * total[:, part]


def accumulate(mine, own, tokens, cotangents, weight, pieces, rate):
    shards, rows, depth = tokens.shape
    parts = shards - 1
    groups = len(pieces) + 1
    width = cotangents[0].shape[1]
    return pl.pallas_call(
        functools.partial(accumulate_kernel, parts, groups, rate),
        out_shape=(jax.ShapeDtypeStruct((rows, width), jnp.float32), jax.ShapeDtypeStruct((rows, depth), jnp.bfloat16)),
        in_specs=[pl.BlockSpec(memory_space=pltpu.SMEM)] * 2
        + [pl.BlockSpec(memory_space=pltpu.HBM)] * (1 + parts + groups),
        out_specs=(pl.BlockSpec(memory_space=pltpu.VMEM),) * 2,
        scratch_shapes=[
            pltpu.VMEM((parts, rows, depth), jnp.bfloat16),
            pltpu.VMEM((parts * depth, width), jnp.bfloat16),
            pltpu.VMEM((rows, width), jnp.bfloat16),
            pltpu.VMEM((groups, rows, width // groups), jnp.bfloat16),
            pltpu.SemaphoreType.DMA((parts,)),
            pltpu.SemaphoreType.DMA((parts,)),
            pltpu.SemaphoreType.DMA((groups,)),
            pltpu.SemaphoreType.DMA((2,)),
        ],
        compiler_params=pltpu.CompilerParams(vmem_limit_bytes=43392 * 2**10),
        cost_estimate=pl.CostEstimate(
            flops=2 * depth * parts * rows * width,
            bytes_accessed=2 * depth * shards * (rows + width) + 8 * rows * width,
            transcendentals=0,
        ),
        name="accumulate",
    )(mine.reshape(1), own.reshape(1), tokens, weight, *cotangents, *pieces)


def finish_kernel(groups, rate, own_ref, tokens_ref, cotangent_ref, total_ref, piece_ref, out_ref, outs, sems):
    share = piece_ref.shape[1]
    steps, _, tile = outs.shape
    stores = []
    for step in range(steps):
        columns = slice(step * tile, (step + 1) * tile)
        product = jnp.dot(tokens_ref[...], cotangent_ref[:, columns], preferred_element_type=jnp.float32)
        total = total_ref[:, columns] - rate * product
        for group in range(step * tile // share, (step + 1) * tile // share):
            part = slice(group * share - step * tile, (group + 1) * share - step * tile)
            factor = jnp.where((own_ref[0] ^ (groups - 1)) == group, 1.0 - mix_weight, 0.0)
            outs[step, :, part] = (total[:, part] + factor * piece_ref[...].astype(jnp.float32)).astype(jnp.bfloat16)
        stores.append(pltpu.make_async_copy(outs.at[step], out_ref.at[:, pl.ds(step * tile, tile)], sems.at[step]))
        stores[step].start()
    for store in stores:
        store.wait()


def finish(own, tokens, cotangent, total, piece, rate):
    rows, width = total.shape
    depth = tokens.shape[1]
    share = piece.shape[1]
    tile = max(share, 256)
    return pl.pallas_call(
        functools.partial(finish_kernel, width // share, rate),
        out_shape=jax.ShapeDtypeStruct((rows, width), jnp.bfloat16),
        in_specs=[pl.BlockSpec(memory_space=pltpu.SMEM)] + [pl.BlockSpec(memory_space=pltpu.VMEM)] * 4,
        out_specs=pl.BlockSpec(memory_space=pltpu.HBM),
        scratch_shapes=[pltpu.VMEM((width // tile, rows, tile), jnp.bfloat16), pltpu.SemaphoreType.DMA((width // tile,))],
        compiler_params=pltpu.CompilerParams(vmem_limit_bytes=16 * 2**20),
        cost_estimate=pl.CostEstimate(
            flops=2 * depth * rows * width, bytes_accessed=2 * depth * (rows + width) + 7 * rows * width, transcendentals=0
        ),
        name="finish",
    )(own.reshape(1), tokens, cotangent, total, piece)


def gather(piece, axis, size, after=()):
    pieces = {0: piece}
    bit = size // 2
    while bit:
        for k in sorted(pieces):
            value = lax.optimization_barrier((pieces[k], *after))[0] if k and bit == 1 else pieces[k]
            pieces[k ^ bit] = swap(value, axis, bit)
        bit //= 2
    return [pieces[k] for k in range(size)]


def on_device(tokens, norm_gain, cotangent, layer_weight, shared_copy, master, momentum):
    tokens, cotangent, weight = tokens[0], cotangent[0], layer_weight[0]
    shards = lax.axis_size("fsdp")
    groups = lax.axis_size("replica")
    mine = lax.axis_index("fsdp")
    own = lax.axis_index("replica")
    rows, width = weight.shape
    inner_rate = inner_gain / math.sqrt(tokens.shape[0] * shards)

    own_exchanges = [1 << bit for bit in range(shards.bit_length() - 1)]
    cotangents = gather(cotangent, "fsdp", shards)
    blocks = prepare(tokens, norm_gain, shards)
    *_, blocks, coded_shared, coded_weight = lax.optimization_barrier(
        (*(cotangents[k] for k in own_exchanges), blocks, shared_copy, weight)
    )
    columns = lax.all_to_all(blocks, "fsdp", split_axis=0, concat_axis=0, tiled=True)

    kept, sent = code_and_decode(own, coded_shared, coded_weight, groups)
    total = kept.astype(jnp.float32) + swap(sent, "replica", 1).astype(jnp.float32)
    bit = 2
    while bit < groups:
        sent = swap(total[1::2].astype(jnp.bfloat16), "replica", bit)
        bit *= 2
        total = total[0::2] + sent.astype(jnp.float32)
    average = total[0] / groups
    momentum_next = outer_beta * momentum + average
    master_next = master - outer_rate * (average + outer_beta * momentum_next)
    pieces = gather(master_next.astype(jnp.bfloat16), "replica", groups, after=cotangents[:-1])

    rate = (1.0 - mix_weight) * inner_rate
    total, last = accumulate(mine, own, columns, cotangents[:-1], weight, pieces[:-1], rate)
    layer_next = finish(own, last, cotangents[-1], total, pieces[-1], rate)
    return (layer_next[None], master_next, momentum_next)


def solution(mesh):
    in_specs = (
        P("replica", "fsdp", None),
        P(),
        P("replica", "fsdp", None),
        P("replica", "fsdp", None),
        P("fsdp", None),
        P("fsdp", "replica"),
        P("fsdp", "replica"),
    )
    out_specs = (P("replica", "fsdp", None), P("fsdp", "replica"), P("fsdp", "replica"))
    return jax.shard_map(
        on_device, mesh=mesh, in_specs=in_specs, out_specs=out_specs, check_vma=False
    )
```

```python
import functools
import math

import jax
import jax.numpy as jnp
from jax import lax
from jax.experimental import pallas as pl
from jax.experimental.pallas import tpu as pltpu
from jax.sharding import PartitionSpec as P

BLOCK = 64


norm_eps = 1e-05
inner_gain = 0.4
outer_rate = 0.7
outer_beta = 0.9
mix_weight = 0.5
code_range = 448.0


def swap(value, axis, mask):
    size = lax.axis_size(axis)
    return lax.ppermute(value, axis, [(i, i ^ mask) for i in range(size)])


def prepare_kernel(tokens_ref, gain_ref, blocks_ref, tokens, blocks, load_sems, store_sems):
    lanes = 128
    shards, rows, count = blocks.shape
    features = shards * rows
    loads, stores = [], []
    for k in range(shards):
        columns = pl.ds(k * rows, rows)
        loads.append(pltpu.make_async_copy(tokens_ref.at[:, columns], tokens.at[:, columns], load_sems.at[k]))
        loads[k].start()
        stores.append(pltpu.make_async_copy(blocks.at[k], blocks_ref.at[k], store_sems.at[k]))
    squares = jnp.zeros((count, lanes), jnp.float32)
    for k in range(shards):
        loads[k].wait()
        for start in range(k * rows, (k + 1) * rows, lanes):
            block = tokens[:, start : start + lanes].astype(jnp.float32)
            squares = squares + block * block
    mean = jnp.sum(squares, axis=-1, keepdims=True) / features
    inverse = jnp.broadcast_to(lax.rsqrt(mean + norm_eps), (count, lanes))
    for k in range(shards):
        for start in range(0, rows, lanes):
            columns = slice(k * rows + start, k * rows + start + lanes)
            normed = tokens[:, columns].astype(jnp.float32) * inverse * gain_ref[:, columns]
            blocks[k, start : start + lanes] = jnp.transpose(normed).astype(jnp.bfloat16)
        stores[k].start()
    for store in stores:
        store.wait()


def prepare(tokens, gain, shards):
    count, features = tokens.shape
    rows = features // shards
    return pl.pallas_call(
        prepare_kernel,
        out_shape=jax.ShapeDtypeStruct((shards, rows, count), jnp.bfloat16),
        in_specs=[pl.BlockSpec(memory_space=pltpu.HBM), pl.BlockSpec(memory_space=pltpu.VMEM)],
        out_specs=pl.BlockSpec(memory_space=pltpu.HBM),
        scratch_shapes=[
            pltpu.VMEM((count, features), jnp.bfloat16),
            pltpu.VMEM((shards, rows, count), jnp.bfloat16),
            pltpu.SemaphoreType.DMA((shards,)),
            pltpu.SemaphoreType.DMA((shards,)),
        ],
        compiler_params=pltpu.CompilerParams(vmem_limit_bytes=16 * 2**20),
        cost_estimate=pl.CostEstimate(
            flops=5 * count * features, bytes_accessed=4 * count * features, transcendentals=count
        ),
        name="prepare",
    )(tokens, gain.astype(jnp.float32).reshape(1, features))


def code_kernel(own_ref, shared_ref, weight_ref, kept_ref, sent_ref, shared, weight, decoded, sems):
    lanes = 2 * BLOCK
    groups, tile, share = decoded.shape
    rows, width = shared.shape
    own = own_ref[0]
    low = lax.broadcasted_iota(jnp.int32, (tile, lanes), 1) < BLOCK

    def loads(i):
        part = pl.ds(pl.multiple_of(i * tile, tile), tile)
        return (
            pltpu.make_async_copy(shared_ref.at[part], shared.at[part], sems.at[0, i]),
            pltpu.make_async_copy(weight_ref.at[part], weight.at[part], sems.at[1, i]),
        )

    for i in range(rows // tile):
        for load in loads(i):
            load.start()

    def step(i, _):
        for load in loads(i):
            load.wait()
        part = pl.ds(pl.multiple_of(i * tile, tile), tile)
        for start in range(0, width, lanes):
            columns = slice(start, start + lanes)
            delta = shared[part, columns].astype(jnp.float32) - weight[part, columns].astype(jnp.float32)
            size = jnp.abs(delta)
            largest = jnp.where(
                low,
                jnp.max(jnp.where(low, size, 0.0), axis=-1, keepdims=True),
                jnp.max(jnp.where(low, 0.0, size), axis=-1, keepdims=True),
            )
            scale = ((largest + 1e-06) * (1.0 / code_range)).astype(jnp.bfloat16).astype(jnp.float32)
            coded = (delta * pl.reciprocal(scale)).astype(jnp.bfloat16)
            value = (coded.astype(jnp.float32) * scale).astype(jnp.bfloat16)
            piece = min(share, lanes)
            for at in range(0, lanes, piece):
                group, offset = divmod(start + at, share)
                decoded[group, :, offset : offset + piece] = value[:, at : at + piece]
        for k in range(0, groups, 2):
            kept_ref[k // 2, part] = decoded[own ^ k]
            sent_ref[k // 2, part] = decoded[own ^ (k + 1)]
        return 0

    lax.fori_loop(0, rows // tile, step, 0)


def code_and_decode(own, shared, weight, groups):
    rows, width = shared.shape
    tile = min(rows, 128)
    share = width // groups
    half = jax.ShapeDtypeStruct((groups // 2, rows, share), jnp.bfloat16)
    return pl.pallas_call(
        code_kernel,
        out_shape=(half, half),
        in_specs=[pl.BlockSpec(memory_space=pltpu.SMEM)] + [pl.BlockSpec(memory_space=pltpu.HBM)] * 2,
        out_specs=(pl.BlockSpec(memory_space=pltpu.VMEM),) * 2,
        scratch_shapes=[
            pltpu.VMEM((rows, width), jnp.bfloat16),
            pltpu.VMEM((rows, width), jnp.bfloat16),
            pltpu.VMEM((groups, tile, share), jnp.bfloat16),
            pltpu.SemaphoreType.DMA((2, rows // tile)),
        ],
        compiler_params=pltpu.CompilerParams(vmem_limit_bytes=16 * 2**20),
        cost_estimate=pl.CostEstimate(flops=20 * rows * width, bytes_accessed=6 * rows * width, transcendentals=0),
        name="code_and_decode",
    )(own.reshape(1), shared, weight)


def accumulate_kernel(parts, groups, rate, mine_ref, own_ref, tokens_ref, weight_ref, *refs):
    cotangent_refs, refs = refs[:parts], refs[parts:]
    piece_refs, refs = refs[: groups - 1], refs[groups - 1 :]
    total_ref, last_ref, tokens, cotangents, weight, pieces, token_sems, cotangent_sems, piece_sems, sems = refs
    mine, own = mine_ref[0], own_ref[0]
    depth, width = cotangent_refs[0].shape
    share = pieces.shape[2]
    tile = max(share, 256)

    loads, rest = [], []
    for k, ref in enumerate(cotangent_refs):
        loads.append(pltpu.make_async_copy(tokens_ref.at[mine ^ k], tokens.at[k], token_sems.at[k]))
        loads.append(pltpu.make_async_copy(ref, cotangents.at[pl.ds(k * depth, depth)], cotangent_sems.at[k]))
    rest.append(pltpu.make_async_copy(weight_ref, weight, sems.at[0]))
    for k, ref in enumerate(piece_refs):
        rest.append(pltpu.make_async_copy(ref, pieces.at[own ^ k], piece_sems.at[k]))
    rest.append(pltpu.make_async_copy(tokens_ref.at[mine ^ parts], last_ref, sems.at[1]))
    for load in loads + rest:
        load.start()
    pieces[own ^ (groups - 1)] = jnp.zeros(pieces.shape[1:], pieces.dtype)
    some = 2
    for first in range(0, parts, some):
        end = min(first + some, parts)
        for load in loads[2 * first : 2 * end]:
            load.wait()
        left = jnp.concatenate([tokens[k] for k in range(first, end)], axis=1)
        for start in range(0, width, tile):
            columns = slice(start, start + tile)
            right = cotangents[first * depth : end * depth, columns]
            total = jnp.dot(left, right, preferred_element_type=jnp.float32)
            if first:
                total = total_ref[:, columns] + total
            if end < parts:
                total_ref[:, columns] = total
                continue
            if start == 0:
                for load in rest:
                    load.wait()
            for group in range(start // share, (start + tile) // share):
                place = slice(group * share, (group + 1) * share)
                part = slice(group * share - start, (group + 1) * share - start)
                mixed = mix_weight * weight[:, place].astype(jnp.float32)
                mixed = mixed + (1.0 - mix_weight) * pieces[group].astype(jnp.float32)
                total_ref[:, place] = mixed - rate * total[:, part]


def accumulate(mine, own, tokens, cotangents, weight, pieces, rate):
    shards, rows, depth = tokens.shape
    parts = shards - 1
    groups = len(pieces) + 1
    width = cotangents[0].shape[1]
    return pl.pallas_call(
        functools.partial(accumulate_kernel, parts, groups, rate),
        out_shape=(jax.ShapeDtypeStruct((rows, width), jnp.float32), jax.ShapeDtypeStruct((rows, depth), jnp.bfloat16)),
        in_specs=[pl.BlockSpec(memory_space=pltpu.SMEM)] * 2
        + [pl.BlockSpec(memory_space=pltpu.HBM)] * (1 + parts + groups),
        out_specs=(pl.BlockSpec(memory_space=pltpu.VMEM),) * 2,
        scratch_shapes=[
            pltpu.VMEM((parts, rows, depth), jnp.bfloat16),
            pltpu.VMEM((parts * depth, width), jnp.bfloat16),
            pltpu.VMEM((rows, width), jnp.bfloat16),
            pltpu.VMEM((groups, rows, width // groups), jnp.bfloat16),
            pltpu.SemaphoreType.DMA((parts,)),
            pltpu.SemaphoreType.DMA((parts,)),
            pltpu.SemaphoreType.DMA((groups,)),
            pltpu.SemaphoreType.DMA((2,)),
        ],
        compiler_params=pltpu.CompilerParams(vmem_limit_bytes=58880 * 2**10),
        cost_estimate=pl.CostEstimate(
            flops=2 * depth * parts * rows * width,
            bytes_accessed=2 * depth * shards * (rows + width) + 8 * rows * width,
            transcendentals=0,
        ),
        name="accumulate",
    )(mine.reshape(1), own.reshape(1), tokens, weight, *cotangents, *pieces)


def finish_kernel(groups, rate, own_ref, tokens_ref, cotangent_ref, total_ref, piece_ref, out_ref, outs, sems):
    share = piece_ref.shape[1]
    steps, _, tile = outs.shape
    stores = []
    for step in range(steps):
        columns = slice(step * tile, (step + 1) * tile)
        product = jnp.dot(tokens_ref[...], cotangent_ref[:, columns], preferred_element_type=jnp.float32)
        total = total_ref[:, columns] - rate * product
        for group in range(step * tile // share, (step + 1) * tile // share):
            part = slice(group * share - step * tile, (group + 1) * share - step * tile)
            factor = jnp.where((own_ref[0] ^ (groups - 1)) == group, 1.0 - mix_weight, 0.0)
            outs[step, :, part] = (total[:, part] + factor * piece_ref[...].astype(jnp.float32)).astype(jnp.bfloat16)
        stores.append(pltpu.make_async_copy(outs.at[step], out_ref.at[:, pl.ds(step * tile, tile)], sems.at[step]))
        stores[step].start()
    for store in stores:
        store.wait()


def finish(own, tokens, cotangent, total, piece, rate):
    rows, width = total.shape
    depth = tokens.shape[1]
    share = piece.shape[1]
    tile = max(share, 256)
    return pl.pallas_call(
        functools.partial(finish_kernel, width // share, rate),
        out_shape=jax.ShapeDtypeStruct((rows, width), jnp.bfloat16),
        in_specs=[pl.BlockSpec(memory_space=pltpu.SMEM)] + [pl.BlockSpec(memory_space=pltpu.VMEM)] * 4,
        out_specs=pl.BlockSpec(memory_space=pltpu.HBM),
        scratch_shapes=[pltpu.VMEM((width // tile, rows, tile), jnp.bfloat16), pltpu.SemaphoreType.DMA((width // tile,))],
        compiler_params=pltpu.CompilerParams(vmem_limit_bytes=16 * 2**20),
        cost_estimate=pl.CostEstimate(
            flops=2 * depth * rows * width, bytes_accessed=2 * depth * (rows + width) + 7 * rows * width, transcendentals=0
        ),
        name="finish",
    )(own.reshape(1), tokens, cotangent, total, piece)


def gather(piece, axis, size, after=()):
    pieces = {0: piece}
    bit = size // 2
    while bit:
        for k in sorted(pieces):
            value = lax.optimization_barrier((pieces[k], *after))[0] if k and bit == 1 else pieces[k]
            pieces[k ^ bit] = swap(value, axis, bit)
        bit //= 2
    return [pieces[k] for k in range(size)]


def on_device(tokens, norm_gain, cotangent, layer_weight, shared_copy, master, momentum):
    tokens, cotangent, weight = tokens[0], cotangent[0], layer_weight[0]
    shards = lax.axis_size("fsdp")
    groups = lax.axis_size("replica")
    mine = lax.axis_index("fsdp")
    own = lax.axis_index("replica")
    rows, width = weight.shape
    inner_rate = inner_gain / math.sqrt(tokens.shape[0] * shards)

    own_exchanges = [1 << bit for bit in range(shards.bit_length() - 1)]
    cotangents = gather(cotangent, "fsdp", shards)
    blocks = prepare(tokens, norm_gain, shards)
    *_, blocks, coded_shared, coded_weight = lax.optimization_barrier(
        (*(cotangents[k] for k in own_exchanges), blocks, shared_copy, weight)
    )
    columns = lax.all_to_all(blocks, "fsdp", split_axis=0, concat_axis=0, tiled=True)

    kept, sent = code_and_decode(own, coded_shared, coded_weight, groups)
    total = kept.astype(jnp.float32) + swap(sent, "replica", 1).astype(jnp.float32)
    bit = 2
    while bit < groups:
        sent = swap(total[1::2].astype(jnp.bfloat16), "replica", bit)
        bit *= 2
        total = total[0::2] + sent.astype(jnp.float32)
    average = total[0] / groups
    momentum_next = outer_beta * momentum + average
    master_next = master - outer_rate * (average + outer_beta * momentum_next)
    pieces = gather(master_next.astype(jnp.bfloat16), "replica", groups, after=cotangents[:-1])

    rate = (1.0 - mix_weight) * inner_rate
    total, last = accumulate(mine, own, columns, cotangents[:-1], weight, pieces[:-1], rate)
    layer_next = finish(own, last, cotangents[-1], total, pieces[-1], rate)
    return (layer_next[None], master_next, momentum_next)


def solution(mesh):
    in_specs = (
        P("replica", "fsdp", None),
        P(),
        P("replica", "fsdp", None),
        P("replica", "fsdp", None),
        P("fsdp", None),
        P("fsdp", "replica"),
        P("fsdp", "replica"),
    )
    out_specs = (P("replica", "fsdp", None), P("fsdp", "replica"), P("fsdp", "replica"))
    return jax.shard_map(
        on_device, mesh=mesh, in_specs=in_specs, out_specs=out_specs, check_vma=False
    )
```

```python
import functools
import math

import jax
import jax.numpy as jnp
from jax import lax
from jax.experimental import pallas as pl
from jax.experimental.pallas import tpu as pltpu
from jax.sharding import PartitionSpec as P

BLOCK = 64


norm_eps = 1e-05
inner_gain = 0.4
outer_rate = 0.7
outer_beta = 0.9
mix_weight = 0.5
code_range = 448.0


def swap(value, axis, mask):
    size = lax.axis_size(axis)
    return lax.ppermute(value, axis, [(i, i ^ mask) for i in range(size)])


def prepare_kernel(tokens_ref, gain_ref, blocks_ref, tokens, blocks, load_sems, store_sems):
    lanes = 128
    shards, rows, count = blocks.shape
    features = shards * rows
    loads, stores = [], []
    for k in range(shards):
        columns = pl.ds(k * rows, rows)
        loads.append(pltpu.make_async_copy(tokens_ref.at[:, columns], tokens.at[:, columns], load_sems.at[k]))
        loads[k].start()
        stores.append(pltpu.make_async_copy(blocks.at[k], blocks_ref.at[k], store_sems.at[k]))
    squares = jnp.zeros((count, lanes), jnp.float32)
    for k in range(shards):
        loads[k].wait()
        for start in range(k * rows, (k + 1) * rows, lanes):
            block = tokens[:, start : start + lanes].astype(jnp.float32)
            squares = squares + block * block
    mean = jnp.sum(squares, axis=-1, keepdims=True) / features
    inverse = jnp.broadcast_to(lax.rsqrt(mean + norm_eps), (count, lanes))
    for k in range(shards):
        for start in range(0, rows, lanes):
            columns = slice(k * rows + start, k * rows + start + lanes)
            normed = tokens[:, columns].astype(jnp.float32) * inverse * gain_ref[:, columns]
            blocks[k, start : start + lanes] = jnp.transpose(normed).astype(jnp.bfloat16)
        stores[k].start()
    for store in stores:
        store.wait()


def prepare(tokens, gain, shards):
    count, features = tokens.shape
    rows = features // shards
    return pl.pallas_call(
        prepare_kernel,
        out_shape=jax.ShapeDtypeStruct((shards, rows, count), jnp.bfloat16),
        in_specs=[pl.BlockSpec(memory_space=pltpu.HBM), pl.BlockSpec(memory_space=pltpu.VMEM)],
        out_specs=pl.BlockSpec(memory_space=pltpu.HBM),
        scratch_shapes=[
            pltpu.VMEM((count, features), jnp.bfloat16),
            pltpu.VMEM((shards, rows, count), jnp.bfloat16),
            pltpu.SemaphoreType.DMA((shards,)),
            pltpu.SemaphoreType.DMA((shards,)),
        ],
        compiler_params=pltpu.CompilerParams(vmem_limit_bytes=16 * 2**20),
        cost_estimate=pl.CostEstimate(
            flops=5 * count * features, bytes_accessed=4 * count * features, transcendentals=count
        ),
        name="prepare",
    )(tokens, gain.astype(jnp.float32).reshape(1, features))


def code_kernel(own_ref, shared_ref, weight_ref, kept_ref, sent_ref, shared, weight, decoded, sems):
    lanes = 2 * BLOCK
    groups, tile, share = decoded.shape
    rows, width = shared.shape
    own = own_ref[0]
    low = lax.broadcasted_iota(jnp.int32, (tile, lanes), 1) < BLOCK

    def loads(i):
        part = pl.ds(pl.multiple_of(i * tile, tile), tile)
        return (
            pltpu.make_async_copy(shared_ref.at[part], shared.at[part], sems.at[0, i]),
            pltpu.make_async_copy(weight_ref.at[part], weight.at[part], sems.at[1, i]),
        )

    for i in range(rows // tile):
        for load in loads(i):
            load.start()

    def step(i, _):
        for load in loads(i):
            load.wait()
        part = pl.ds(pl.multiple_of(i * tile, tile), tile)
        for start in range(0, width, lanes):
            columns = slice(start, start + lanes)
            delta = shared[part, columns].astype(jnp.float32) - weight[part, columns].astype(jnp.float32)
            size = jnp.abs(delta)
            largest = jnp.where(
                low,
                jnp.max(jnp.where(low, size, 0.0), axis=-1, keepdims=True),
                jnp.max(jnp.where(low, 0.0, size), axis=-1, keepdims=True),
            )
            scale = ((largest + 1e-06) * (1.0 / code_range)).astype(jnp.bfloat16).astype(jnp.float32)
            coded = (delta * pl.reciprocal(scale)).astype(jnp.bfloat16)
            value = (coded.astype(jnp.float32) * scale).astype(jnp.bfloat16)
            piece = min(share, lanes)
            for at in range(0, lanes, piece):
                group, offset = divmod(start + at, share)
                decoded[group, :, offset : offset + piece] = value[:, at : at + piece]
        for k in range(0, groups, 2):
            kept_ref[k // 2, part] = decoded[own ^ k]
            sent_ref[k // 2, part] = decoded[own ^ (k + 1)]
        return 0

    lax.fori_loop(0, rows // tile, step, 0)


def code_and_decode(own, shared, weight, groups):
    rows, width = shared.shape
    tile = min(rows, 128)
    share = width // groups
    half = jax.ShapeDtypeStruct((groups // 2, rows, share), jnp.bfloat16)
    return pl.pallas_call(
        code_kernel,
        out_shape=(half, half),
        in_specs=[pl.BlockSpec(memory_space=pltpu.SMEM)] + [pl.BlockSpec(memory_space=pltpu.HBM)] * 2,
        out_specs=(pl.BlockSpec(memory_space=pltpu.VMEM),) * 2,
        scratch_shapes=[
            pltpu.VMEM((rows, width), jnp.bfloat16),
            pltpu.VMEM((rows, width), jnp.bfloat16),
            pltpu.VMEM((groups, tile, share), jnp.bfloat16),
            pltpu.SemaphoreType.DMA((2, rows // tile)),
        ],
        compiler_params=pltpu.CompilerParams(vmem_limit_bytes=16 * 2**20),
        cost_estimate=pl.CostEstimate(flops=20 * rows * width, bytes_accessed=6 * rows * width, transcendentals=0),
        name="code_and_decode",
    )(own.reshape(1), shared, weight)


def mix_kernel(shards, groups, rate, mine_ref, own_ref, tokens_ref, weight_ref, *refs):
    cotangent_refs, refs = refs[:shards], refs[shards:]
    piece_refs, refs = refs[:groups], refs[groups:]
    out_ref, tokens, cotangents, weight, pieces, totals, outs, token_sems, cotangent_sems, piece_sems, weight_sem, out_sems = refs
    mine, own = mine_ref[0], own_ref[0]
    depth, width = cotangent_refs[0].shape
    share = pieces.shape[2]
    steps, _, tile = outs.shape

    loads, rest = [], []
    for k, ref in enumerate(cotangent_refs):
        loads.append(pltpu.make_async_copy(tokens_ref.at[mine ^ k], tokens.at[k], token_sems.at[k]))
        loads.append(pltpu.make_async_copy(ref, cotangents.at[pl.ds(k * depth, depth)], cotangent_sems.at[k]))
    rest.append(pltpu.make_async_copy(weight_ref, weight, weight_sem))
    for k, ref in enumerate(piece_refs):
        rest.append(pltpu.make_async_copy(ref, pieces.at[own ^ k], piece_sems.at[k]))
    for load in loads + rest:
        load.start()
    stores = []
    some = 2
    for first in range(0, shards, some):
        end = first + some
        for load in loads[2 * first : 2 * end]:
            load.wait()
        if end == shards:
            for load in rest:
                load.wait()
        left = jnp.concatenate([tokens[k] for k in range(first, end)], axis=1)
        for step in range(steps):
            columns = slice(step * tile, (step + 1) * tile)
            right = cotangents[first * depth : end * depth, columns]
            total = jnp.dot(left, right, preferred_element_type=jnp.float32)
            if first:
                total = totals[step] + total
            if end < shards:
                totals[step] = total
                continue
            for group in range(step * tile // share, (step + 1) * tile // share):
                place = slice(group * share, (group + 1) * share)
                part = slice(group * share - step * tile, (group + 1) * share - step * tile)
                mixed = weight[:, place].astype(jnp.float32) + pieces[group].astype(jnp.float32)
                outs[step, :, part] = (mix_weight * mixed - rate * total[:, part]).astype(jnp.bfloat16)
            place = pl.ds(step * tile, tile)
            stores.append(pltpu.make_async_copy(outs.at[step], out_ref.at[:, place], out_sems.at[step]))
            stores[step].start()
    for store in stores:
        store.wait()


def mix(mine, own, tokens, cotangents, weight, pieces, rate):
    shards, rows, depth = tokens.shape
    groups = len(pieces)
    width = weight.shape[1]
    share = width // groups
    tile = max(share, 256)
    remote = pl.BlockSpec(memory_space=pltpu.HBM)
    return pl.pallas_call(
        functools.partial(mix_kernel, shards, groups, rate),
        out_shape=jax.ShapeDtypeStruct((rows, width), jnp.bfloat16),
        in_specs=[pl.BlockSpec(memory_space=pltpu.SMEM)] * 2 + [remote] * (2 + shards + groups),
        out_specs=remote,
        scratch_shapes=[
            pltpu.VMEM((shards, rows, depth), jnp.bfloat16),
            pltpu.VMEM((shards * depth, width), jnp.bfloat16),
            pltpu.VMEM((rows, width), jnp.bfloat16),
            pltpu.VMEM((groups, rows, share), jnp.bfloat16),
            pltpu.VMEM((width // tile, rows, tile), jnp.float32),
            pltpu.VMEM((width // tile, rows, tile), jnp.bfloat16),
            pltpu.SemaphoreType.DMA((shards,)),
            pltpu.SemaphoreType.DMA((shards,)),
            pltpu.SemaphoreType.DMA((groups,)),
            pltpu.SemaphoreType.DMA,
            pltpu.SemaphoreType.DMA((width // tile,)),
        ],
        compiler_params=pltpu.CompilerParams(vmem_limit_bytes=58 * 2**20),
        cost_estimate=pl.CostEstimate(
            flops=2 * depth * shards * rows * width,
            bytes_accessed=2 * depth * shards * (rows + width) + 6 * rows * width,
            transcendentals=0,
        ),
        name="mix",
    )(mine.reshape(1), own.reshape(1), tokens, weight, *cotangents, *pieces)


def gather(piece, axis, size, after=()):
    pieces = {0: piece}
    bit = size // 2
    while bit:
        for k in sorted(pieces):
            value = lax.optimization_barrier((pieces[k], *after))[0] if k and bit == 1 else pieces[k]
            pieces[k ^ bit] = swap(value, axis, bit)
        bit //= 2
    return [pieces[k] for k in range(size)]


def on_device(tokens, norm_gain, cotangent, layer_weight, shared_copy, master, momentum):
    tokens, cotangent, weight = tokens[0], cotangent[0], layer_weight[0]
    shards = lax.axis_size("fsdp")
    groups = lax.axis_size("replica")
    mine = lax.axis_index("fsdp")
    own = lax.axis_index("replica")
    rows, width = weight.shape
    inner_rate = inner_gain / math.sqrt(tokens.shape[0] * shards)

    own_exchanges = [1 << bit for bit in range(shards.bit_length() - 1)]
    cotangents = gather(cotangent, "fsdp", shards)
    blocks = prepare(tokens, norm_gain, shards)
    *_, blocks, coded_shared, coded_weight = lax.optimization_barrier(
        (*(cotangents[k] for k in own_exchanges), blocks, shared_copy, weight)
    )
    columns = lax.all_to_all(blocks, "fsdp", split_axis=0, concat_axis=0, tiled=True)

    kept, sent = code_and_decode(own, coded_shared, coded_weight, groups)
    total = kept.astype(jnp.float32) + swap(sent, "replica", 1).astype(jnp.float32)
    bit = 2
    while bit < groups:
        sent = swap(total[1::2].astype(jnp.bfloat16), "replica", bit)
        bit *= 2
        total = total[0::2] + sent.astype(jnp.float32)
    average = total[0] / groups
    momentum_next = outer_beta * momentum + average
    master_next = master - outer_rate * (average + outer_beta * momentum_next)
    pieces = gather(master_next.astype(jnp.bfloat16), "replica", groups, after=(cotangents[shards // 2 - 1], cotangents[shards // 2 + 1]))

    rate = (1.0 - mix_weight) * inner_rate
    layer_next = mix(mine, own, columns, cotangents, weight, pieces, rate)
    return (layer_next[None], master_next, momentum_next)


def solution(mesh):
    in_specs = (
        P("replica", "fsdp", None),
        P(),
        P("replica", "fsdp", None),
        P("replica", "fsdp", None),
        P("fsdp", None),
        P("fsdp", "replica"),
        P("fsdp", "replica"),
    )
    out_specs = (P("replica", "fsdp", None), P("fsdp", "replica"), P("fsdp", "replica"))
    return jax.shard_map(
        on_device, mesh=mesh, in_specs=in_specs, out_specs=out_specs, check_vma=False
    )
```

```python
import functools
import math

import jax
import jax.numpy as jnp
from jax import lax
from jax.experimental import pallas as pl
from jax.experimental.pallas import tpu as pltpu
from jax.sharding import PartitionSpec as P

BLOCK = 64


norm_eps = 1e-05
inner_gain = 0.4
outer_rate = 0.7
outer_beta = 0.9
mix_weight = 0.5
code_range = 448.0


def swap(value, axis, mask):
    size = lax.axis_size(axis)
    return lax.ppermute(value, axis, [(i, i ^ mask) for i in range(size)])


def prepare_kernel(tokens_ref, gain_ref, blocks_ref, tokens, blocks, load_sems, store_sems):
    lanes = 128
    shards, rows, count = blocks.shape
    features = shards * rows
    loads, stores = [], []
    for k in range(shards):
        columns = pl.ds(k * rows, rows)
        loads.append(pltpu.make_async_copy(tokens_ref.at[:, columns], tokens.at[:, columns], load_sems.at[k]))
        loads[k].start()
        stores.append(pltpu.make_async_copy(blocks.at[k], blocks_ref.at[k], store_sems.at[k]))
    squares = jnp.zeros((count, lanes), jnp.float32)
    for k in range(shards):
        loads[k].wait()
        for start in range(k * rows, (k + 1) * rows, lanes):
            block = tokens[:, start : start + lanes].astype(jnp.float32)
            squares = squares + block * block
    mean = jnp.sum(squares, axis=-1, keepdims=True) / features
    inverse = jnp.broadcast_to(lax.rsqrt(mean + norm_eps), (count, lanes))
    for k in range(shards):
        for start in range(0, rows, lanes):
            columns = slice(k * rows + start, k * rows + start + lanes)
            normed = tokens[:, columns].astype(jnp.float32) * inverse * gain_ref[:, columns]
            blocks[k, start : start + lanes] = jnp.transpose(normed).astype(jnp.bfloat16)
        stores[k].start()
    for store in stores:
        store.wait()


def prepare(tokens, gain, shards):
    count, features = tokens.shape
    rows = features // shards
    return pl.pallas_call(
        prepare_kernel,
        out_shape=jax.ShapeDtypeStruct((shards, rows, count), jnp.bfloat16),
        in_specs=[pl.BlockSpec(memory_space=pltpu.HBM), pl.BlockSpec(memory_space=pltpu.VMEM)],
        out_specs=pl.BlockSpec(memory_space=pltpu.HBM),
        scratch_shapes=[
            pltpu.VMEM((count, features), jnp.bfloat16),
            pltpu.VMEM((shards, rows, count), jnp.bfloat16),
            pltpu.SemaphoreType.DMA((shards,)),
            pltpu.SemaphoreType.DMA((shards,)),
        ],
        compiler_params=pltpu.CompilerParams(vmem_limit_bytes=16 * 2**20),
        cost_estimate=pl.CostEstimate(
            flops=5 * count * features, bytes_accessed=4 * count * features, transcendentals=count
        ),
        name="prepare",
    )(tokens, gain.astype(jnp.float32).reshape(1, features))


def code_kernel(own_ref, shared_ref, weight_ref, kept_ref, sent_ref, shared, weight, decoded, sems):
    lanes = 2 * BLOCK
    groups, tile, share = decoded.shape
    rows, width = shared.shape
    own = own_ref[0]
    low = lax.broadcasted_iota(jnp.int32, (tile, lanes), 1) < BLOCK

    def loads(i):
        part = pl.ds(pl.multiple_of(i * tile, tile), tile)
        return (
            pltpu.make_async_copy(shared_ref.at[part], shared.at[part], sems.at[0, i]),
            pltpu.make_async_copy(weight_ref.at[part], weight.at[part], sems.at[1, i]),
        )

    for i in range(rows // tile):
        for load in loads(i):
            load.start()

    def step(i, _):
        for load in loads(i):
            load.wait()
        part = pl.ds(pl.multiple_of(i * tile, tile), tile)
        for start in range(0, width, lanes):
            columns = slice(start, start + lanes)
            delta = shared[part, columns].astype(jnp.float32) - weight[part, columns].astype(jnp.float32)
            size = jnp.abs(delta)
            largest = jnp.where(
                low,
                jnp.max(jnp.where(low, size, 0.0), axis=-1, keepdims=True),
                jnp.max(jnp.where(low, 0.0, size), axis=-1, keepdims=True),
            )
            scale = ((largest + 1e-06) * (1.0 / code_range)).astype(jnp.bfloat16).astype(jnp.float32)
            coded = (delta * pl.reciprocal(scale)).astype(jnp.bfloat16)
            value = (coded.astype(jnp.float32) * scale).astype(jnp.bfloat16)
            piece = min(share, lanes)
            for at in range(0, lanes, piece):
                group, offset = divmod(start + at, share)
                decoded[group, :, offset : offset + piece] = value[:, at : at + piece]
        for k in range(0, groups, 2):
            kept_ref[k // 2, part] = decoded[own ^ k]
            sent_ref[k // 2, part] = decoded[own ^ (k + 1)]
        return 0

    lax.fori_loop(0, rows // tile, step, 0)


def code_and_decode(own, shared, weight, groups):
    rows, width = shared.shape
    tile = min(rows, 128)
    share = width // groups
    half = jax.ShapeDtypeStruct((groups // 2, rows, share), jnp.bfloat16)
    return pl.pallas_call(
        code_kernel,
        out_shape=(half, half),
        in_specs=[pl.BlockSpec(memory_space=pltpu.SMEM)] + [pl.BlockSpec(memory_space=pltpu.HBM)] * 2,
        out_specs=(pl.BlockSpec(memory_space=pltpu.VMEM),) * 2,
        scratch_shapes=[
            pltpu.VMEM((rows, width), jnp.bfloat16),
            pltpu.VMEM((rows, width), jnp.bfloat16),
            pltpu.VMEM((groups, tile, share), jnp.bfloat16),
            pltpu.SemaphoreType.DMA((2, rows // tile)),
        ],
        compiler_params=pltpu.CompilerParams(vmem_limit_bytes=16 * 2**20),
        cost_estimate=pl.CostEstimate(flops=20 * rows * width, bytes_accessed=6 * rows * width, transcendentals=0),
        name="code_and_decode",
    )(own.reshape(1), shared, weight)


def mix_kernel(shards, groups, rate, mine_ref, own_ref, tokens_ref, weight_ref, *refs):
    cotangent_refs, refs = refs[:shards], refs[shards:]
    piece_refs, refs = refs[:groups], refs[groups:]
    out_ref, tokens, cotangents, weight, pieces, totals, outs, token_sems, cotangent_sems, piece_sems, weight_sem, out_sems = refs
    mine, own = mine_ref[0], own_ref[0]
    depth, width = cotangent_refs[0].shape
    share = pieces.shape[2]
    steps, _, tile = outs.shape

    loads, rest = [], []
    for k, ref in enumerate(cotangent_refs):
        loads.append(pltpu.make_async_copy(tokens_ref.at[mine ^ k], tokens.at[k], token_sems.at[k]))
        loads.append(pltpu.make_async_copy(ref, cotangents.at[pl.ds(k * depth, depth)], cotangent_sems.at[k]))
    rest.append(pltpu.make_async_copy(weight_ref, weight, weight_sem))
    for k, ref in enumerate(piece_refs):
        rest.append(pltpu.make_async_copy(ref, pieces.at[own ^ k], piece_sems.at[k]))
    for load in loads + rest:
        load.start()
    stores = []
    some = 2
    for first in range(0, shards, some):
        end = first + some
        for load in loads[2 * first : 2 * end]:
            load.wait()
        if end == shards:
            for load in rest:
                load.wait()
        left = jnp.concatenate([tokens[k] for k in range(first, end)], axis=1)
        for step in range(steps):
            columns = slice(step * tile, (step + 1) * tile)
            right = cotangents[first * depth : end * depth, columns]
            total = jnp.dot(left, right, preferred_element_type=jnp.float32)
            if first:
                total = totals[step] + total
            if end < shards:
                totals[step] = total
                continue
            for group in range(step * tile // share, (step + 1) * tile // share):
                place = slice(group * share, (group + 1) * share)
                part = slice(group * share - step * tile, (group + 1) * share - step * tile)
                mixed = weight[:, place].astype(jnp.float32) + pieces[group].astype(jnp.float32)
                outs[step, :, part] = (mix_weight * mixed - rate * total[:, part]).astype(jnp.bfloat16)
            place = pl.ds(step * tile, tile)
            stores.append(pltpu.make_async_copy(outs.at[step], out_ref.at[:, place], out_sems.at[step]))
            stores[step].start()
    for store in stores:
        store.wait()


def mix(mine, own, tokens, cotangents, weight, pieces, rate):
    shards, rows, depth = tokens.shape
    groups = len(pieces)
    width = weight.shape[1]
    share = width // groups
    tile = max(share, 256)
    remote = pl.BlockSpec(memory_space=pltpu.HBM)
    return pl.pallas_call(
        functools.partial(mix_kernel, shards, groups, rate),
        out_shape=jax.ShapeDtypeStruct((rows, width), jnp.bfloat16),
        in_specs=[pl.BlockSpec(memory_space=pltpu.SMEM)] * 2 + [remote] * (2 + shards + groups),
        out_specs=remote,
        scratch_shapes=[
            pltpu.VMEM((shards, rows, depth), jnp.bfloat16),
            pltpu.VMEM((shards * depth, width), jnp.bfloat16),
            pltpu.VMEM((rows, width), jnp.bfloat16),
            pltpu.VMEM((groups, rows, share), jnp.bfloat16),
            pltpu.VMEM((width // tile, rows, tile), jnp.float32),
            pltpu.VMEM((width // tile, rows, tile), jnp.bfloat16),
            pltpu.SemaphoreType.DMA((shards,)),
            pltpu.SemaphoreType.DMA((shards,)),
            pltpu.SemaphoreType.DMA((groups,)),
            pltpu.SemaphoreType.DMA,
            pltpu.SemaphoreType.DMA((width // tile,)),
        ],
        compiler_params=pltpu.CompilerParams(vmem_limit_bytes=58 * 2**20),
        cost_estimate=pl.CostEstimate(
            flops=2 * depth * shards * rows * width,
            bytes_accessed=2 * depth * shards * (rows + width) + 6 * rows * width,
            transcendentals=0,
        ),
        name="mix",
    )(mine.reshape(1), own.reshape(1), tokens, weight, *cotangents, *pieces)


def hand_on_kernel(value_ref, out_ref, sem):
    copy = pltpu.make_async_copy(value_ref, out_ref, sem)
    copy.start()
    copy.wait()


def hand_on(value):
    return pl.pallas_call(
        hand_on_kernel,
        out_shape=jax.ShapeDtypeStruct(value.shape, value.dtype),
        in_specs=[pl.BlockSpec(memory_space=pltpu.VMEM)],
        out_specs=pl.BlockSpec(memory_space=pltpu.HBM),
        scratch_shapes=[pltpu.SemaphoreType.DMA],
        compiler_params=pltpu.CompilerParams(vmem_limit_bytes=16 * 2**20),
        cost_estimate=pl.CostEstimate(flops=0, bytes_accessed=48 * value.size, transcendentals=0),
        name="hand_on",
    )(value)


def gather(piece, axis, size, after=()):
    pieces = {0: piece}
    bit = size // 2
    while bit:
        for k in sorted(pieces):
            value = lax.optimization_barrier((pieces[k], *after))[0] if k and bit == 1 else pieces[k]
            pieces[k ^ bit] = swap(value, axis, bit)
        bit //= 2
    return [pieces[k] for k in range(size)]


def on_device(tokens, norm_gain, cotangent, layer_weight, shared_copy, master, momentum):
    tokens, cotangent, weight = tokens[0], cotangent[0], layer_weight[0]
    shards = lax.axis_size("fsdp")
    groups = lax.axis_size("replica")
    mine = lax.axis_index("fsdp")
    own = lax.axis_index("replica")
    rows, width = weight.shape
    inner_rate = inner_gain / math.sqrt(tokens.shape[0] * shards)

    own_exchanges = [1 << bit for bit in range(shards.bit_length() - 1)]
    cotangents = gather(cotangent, "fsdp", shards)
    blocks = prepare(tokens, norm_gain, shards)
    *_, blocks, coded_shared, coded_weight = lax.optimization_barrier(
        (*(cotangents[k] for k in own_exchanges), blocks, shared_copy, weight)
    )
    columns = lax.all_to_all(blocks, "fsdp", split_axis=0, concat_axis=0, tiled=True)

    kept, sent = code_and_decode(own, coded_shared, coded_weight, groups)
    total = kept.astype(jnp.float32) + swap(sent, "replica", 1).astype(jnp.float32)
    bit = 2
    while bit < groups:
        sent = swap(total[1::2].astype(jnp.bfloat16), "replica", bit)
        bit *= 2
        total = total[0::2] + sent.astype(jnp.float32)
    average = total[0] / groups
    momentum_next = outer_beta * momentum + average
    master_next = master - outer_rate * (average + outer_beta * momentum_next)
    pieces = gather(master_next.astype(jnp.bfloat16), "replica", groups, after=(cotangents[shards // 2 - 1], cotangents[shards // 2 + 1]))

    rate = (1.0 - mix_weight) * inner_rate
    layer_next = mix(mine, own, columns, cotangents[:-1] + [hand_on(cotangents[-1])], weight, pieces, rate)
    return (layer_next[None], master_next, momentum_next)


def solution(mesh):
    in_specs = (
        P("replica", "fsdp", None),
        P(),
        P("replica", "fsdp", None),
        P("replica", "fsdp", None),
        P("fsdp", None),
        P("fsdp", "replica"),
        P("fsdp", "replica"),
    )
    out_specs = (P("replica", "fsdp", None), P("fsdp", "replica"), P("fsdp", "replica"))
    return jax.shard_map(
        on_device, mesh=mesh, in_specs=in_specs, out_specs=out_specs, check_vma=False
    )
```

```python
import functools
import math

import jax
import jax.numpy as jnp
from jax import lax
from jax.experimental import pallas as pl
from jax.experimental.pallas import tpu as pltpu
from jax.sharding import PartitionSpec as P

BLOCK = 64


norm_eps = 1e-05
inner_gain = 0.4
outer_rate = 0.7
outer_beta = 0.9
mix_weight = 0.5
code_range = 448.0


def swap(value, axis, mask):
    size = lax.axis_size(axis)
    return lax.ppermute(value, axis, [(i, i ^ mask) for i in range(size)])


def prepare_kernel(tokens_ref, gain_ref, blocks_ref, tokens, blocks, load_sems, store_sems):
    lanes = 128
    shards, rows, count = blocks.shape
    features = shards * rows
    loads, stores = [], []
    for k in range(shards):
        columns = pl.ds(k * rows, rows)
        loads.append(pltpu.make_async_copy(tokens_ref.at[:, columns], tokens.at[:, columns], load_sems.at[k]))
        loads[k].start()
        stores.append(pltpu.make_async_copy(blocks.at[k], blocks_ref.at[k], store_sems.at[k]))
    squares = jnp.zeros((count, lanes), jnp.float32)
    for k in range(shards):
        loads[k].wait()
        for start in range(k * rows, (k + 1) * rows, lanes):
            block = tokens[:, start : start + lanes].astype(jnp.float32)
            squares = squares + block * block
    mean = jnp.sum(squares, axis=-1, keepdims=True) / features
    inverse = jnp.broadcast_to(lax.rsqrt(mean + norm_eps), (count, lanes))
    for k in range(shards):
        for start in range(0, rows, lanes):
            columns = slice(k * rows + start, k * rows + start + lanes)
            normed = tokens[:, columns].astype(jnp.float32) * inverse * gain_ref[:, columns]
            blocks[k, start : start + lanes] = jnp.transpose(normed).astype(jnp.bfloat16)
        stores[k].start()
    for store in stores:
        store.wait()


def prepare(tokens, gain, shards):
    count, features = tokens.shape
    rows = features // shards
    return pl.pallas_call(
        prepare_kernel,
        out_shape=jax.ShapeDtypeStruct((shards, rows, count), jnp.bfloat16),
        in_specs=[pl.BlockSpec(memory_space=pltpu.HBM), pl.BlockSpec(memory_space=pltpu.VMEM)],
        out_specs=pl.BlockSpec(memory_space=pltpu.HBM),
        scratch_shapes=[
            pltpu.VMEM((count, features), jnp.bfloat16),
            pltpu.VMEM((shards, rows, count), jnp.bfloat16),
            pltpu.SemaphoreType.DMA((shards,)),
            pltpu.SemaphoreType.DMA((shards,)),
        ],
        compiler_params=pltpu.CompilerParams(vmem_limit_bytes=16 * 2**20),
        cost_estimate=pl.CostEstimate(
            flops=5 * count * features, bytes_accessed=4 * count * features, transcendentals=count
        ),
        name="prepare",
    )(tokens, gain.astype(jnp.float32).reshape(1, features))


def code_kernel(own_ref, shared_ref, weight_ref, kept_ref, sent_ref, shared, weight, decoded, sems):
    lanes = 2 * BLOCK
    groups, tile, share = decoded.shape
    rows, width = shared.shape
    own = own_ref[0]
    low = lax.broadcasted_iota(jnp.int32, (tile, lanes), 1) < BLOCK

    def loads(i):
        part = pl.ds(pl.multiple_of(i * tile, tile), tile)
        return (
            pltpu.make_async_copy(shared_ref.at[part], shared.at[part], sems.at[0, i]),
            pltpu.make_async_copy(weight_ref.at[part], weight.at[part], sems.at[1, i]),
        )

    for i in range(rows // tile):
        for load in loads(i):
            load.start()

    def step(i, _):
        for load in loads(i):
            load.wait()
        part = pl.ds(pl.multiple_of(i * tile, tile), tile)
        for start in range(0, width, lanes):
            columns = slice(start, start + lanes)
            delta = shared[part, columns].astype(jnp.float32) - weight[part, columns].astype(jnp.float32)
            size = jnp.abs(delta)
            largest = jnp.where(
                low,
                jnp.max(jnp.where(low, size, 0.0), axis=-1, keepdims=True),
                jnp.max(jnp.where(low, 0.0, size), axis=-1, keepdims=True),
            )
            scale = ((largest + 1e-06) * (1.0 / code_range)).astype(jnp.bfloat16).astype(jnp.float32)
            coded = (delta * pl.reciprocal(scale)).astype(jnp.bfloat16)
            value = (coded.astype(jnp.float32) * scale).astype(jnp.bfloat16)
            piece = min(share, lanes)
            for at in range(0, lanes, piece):
                group, offset = divmod(start + at, share)
                decoded[group, :, offset : offset + piece] = value[:, at : at + piece]
        for k in range(0, groups, 2):
            kept_ref[k // 2, part] = decoded[own ^ k]
            sent_ref[k // 2, part] = decoded[own ^ (k + 1)]
        return 0

    lax.fori_loop(0, rows // tile, step, 0)


def code_and_decode(own, shared, weight, groups):
    rows, width = shared.shape
    tile = min(rows, 128)
    share = width // groups
    half = jax.ShapeDtypeStruct((groups // 2, rows, share), jnp.bfloat16)
    return pl.pallas_call(
        code_kernel,
        out_shape=(half, half),
        in_specs=[pl.BlockSpec(memory_space=pltpu.SMEM)] + [pl.BlockSpec(memory_space=pltpu.HBM)] * 2,
        out_specs=(pl.BlockSpec(memory_space=pltpu.VMEM),) * 2,
        scratch_shapes=[
            pltpu.VMEM((rows, width), jnp.bfloat16),
            pltpu.VMEM((rows, width), jnp.bfloat16),
            pltpu.VMEM((groups, tile, share), jnp.bfloat16),
            pltpu.SemaphoreType.DMA((2, rows // tile)),
        ],
        compiler_params=pltpu.CompilerParams(vmem_limit_bytes=16 * 2**20),
        cost_estimate=pl.CostEstimate(flops=20 * rows * width, bytes_accessed=6 * rows * width, transcendentals=0),
        name="code_and_decode",
    )(own.reshape(1), shared, weight)


def accumulate_kernel(parts, groups, rate, mine_ref, own_ref, tokens_ref, weight_ref, *refs):
    cotangent_refs, refs = refs[:parts], refs[parts:]
    piece_refs, refs = refs[: groups - 1], refs[groups - 1 :]
    total_ref, last_ref, tokens, cotangents, weight, pieces, token_sems, cotangent_sems, piece_sems, sems = refs
    mine, own = mine_ref[0], own_ref[0]
    depth, width = cotangent_refs[0].shape
    share = pieces.shape[2]
    tile = max(share, 256)

    loads, rest = [], []
    for k, ref in enumerate(cotangent_refs):
        loads.append(pltpu.make_async_copy(tokens_ref.at[mine ^ k], tokens.at[k], token_sems.at[k]))
        loads.append(pltpu.make_async_copy(ref, cotangents.at[pl.ds(k * depth, depth)], cotangent_sems.at[k]))
    rest.append(pltpu.make_async_copy(weight_ref, weight, sems.at[0]))
    for k, ref in enumerate(piece_refs):
        rest.append(pltpu.make_async_copy(ref, pieces.at[own ^ k], piece_sems.at[k]))
    rest.append(pltpu.make_async_copy(tokens_ref.at[mine ^ parts], last_ref, sems.at[1]))
    for load in loads + rest:
        load.start()
    pieces[own ^ (groups - 1)] = jnp.zeros(pieces.shape[1:], pieces.dtype)
    some = 2
    for first in range(0, parts, some):
        end = min(first + some, parts)
        for load in loads[2 * first : 2 * end]:
            load.wait()
        left = jnp.concatenate([tokens[k] for k in range(first, end)], axis=1)
        for start in range(0, width, tile):
            columns = slice(start, start + tile)
            right = cotangents[first * depth : end * depth, columns]
            total = jnp.dot(left, right, preferred_element_type=jnp.float32)
            if first:
                total = total_ref[:, columns] + total
            if end < parts:
                total_ref[:, columns] = total
                continue
            if start == 0:
                for load in rest:
                    load.wait()
            for group in range(start // share, (start + tile) // share):
                place = slice(group * share, (group + 1) * share)
                part = slice(group * share - start, (group + 1) * share - start)
                mixed = mix_weight * weight[:, place].astype(jnp.float32)
                mixed = mixed + (1.0 - mix_weight) * pieces[group].astype(jnp.float32)
                total_ref[:, place] = mixed - rate * total[:, part]


def accumulate(mine, own, tokens, cotangents, weight, pieces, rate):
    shards, rows, depth = tokens.shape
    parts = shards - 1
    groups = len(pieces) + 1
    width = cotangents[0].shape[1]
    return pl.pallas_call(
        functools.partial(accumulate_kernel, parts, groups, rate),
        out_shape=(jax.ShapeDtypeStruct((rows, width), jnp.float32), jax.ShapeDtypeStruct((rows, depth), jnp.bfloat16)),
        in_specs=[pl.BlockSpec(memory_space=pltpu.SMEM)] * 2
        + [pl.BlockSpec(memory_space=pltpu.HBM)] * (1 + parts + groups),
        out_specs=(pl.BlockSpec(memory_space=pltpu.VMEM),) * 2,
        scratch_shapes=[
            pltpu.VMEM((parts, rows, depth), jnp.bfloat16),
            pltpu.VMEM((parts * depth, width), jnp.bfloat16),
            pltpu.VMEM((rows, width), jnp.bfloat16),
            pltpu.VMEM((groups, rows, width // groups), jnp.bfloat16),
            pltpu.SemaphoreType.DMA((parts,)),
            pltpu.SemaphoreType.DMA((parts,)),
            pltpu.SemaphoreType.DMA((groups,)),
            pltpu.SemaphoreType.DMA((2,)),
        ],
        compiler_params=pltpu.CompilerParams(vmem_limit_bytes=54 * 2**20),
        cost_estimate=pl.CostEstimate(
            flops=2 * depth * parts * rows * width,
            bytes_accessed=2 * depth * shards * (rows + width) + 8 * rows * width,
            transcendentals=0,
        ),
        name="accumulate",
    )(mine.reshape(1), own.reshape(1), tokens, weight, *cotangents, *pieces)


def finish_kernel(groups, rate, own_ref, tokens_ref, cotangent_ref, total_ref, piece_ref, out_ref, outs, sems):
    share = piece_ref.shape[1]
    steps, _, tile = outs.shape
    stores = []
    for step in range(steps):
        columns = slice(step * tile, (step + 1) * tile)
        product = jnp.dot(tokens_ref[...], cotangent_ref[:, columns], preferred_element_type=jnp.float32)
        total = total_ref[:, columns] - rate * product
        for group in range(step * tile // share, (step + 1) * tile // share):
            part = slice(group * share - step * tile, (group + 1) * share - step * tile)
            factor = jnp.where((own_ref[0] ^ (groups - 1)) == group, 1.0 - mix_weight, 0.0)
            outs[step, :, part] = (total[:, part] + factor * piece_ref[...].astype(jnp.float32)).astype(jnp.bfloat16)
        stores.append(pltpu.make_async_copy(outs.at[step], out_ref.at[:, pl.ds(step * tile, tile)], sems.at[step]))
        stores[step].start()
    for store in stores:
        store.wait()


def finish(own, tokens, cotangent, total, piece, rate):
    rows, width = total.shape
    depth = tokens.shape[1]
    share = piece.shape[1]
    tile = max(share, 256)
    return pl.pallas_call(
        functools.partial(finish_kernel, width // share, rate),
        out_shape=jax.ShapeDtypeStruct((rows, width), jnp.bfloat16),
        in_specs=[pl.BlockSpec(memory_space=pltpu.SMEM)] + [pl.BlockSpec(memory_space=pltpu.VMEM)] * 4,
        out_specs=pl.BlockSpec(memory_space=pltpu.HBM),
        scratch_shapes=[pltpu.VMEM((width // tile, rows, tile), jnp.bfloat16), pltpu.SemaphoreType.DMA((width // tile,))],
        compiler_params=pltpu.CompilerParams(vmem_limit_bytes=16 * 2**20),
        cost_estimate=pl.CostEstimate(
            flops=2 * depth * rows * width, bytes_accessed=2 * depth * (rows + width) + 7 * rows * width, transcendentals=0
        ),
        name="finish",
    )(own.reshape(1), tokens, cotangent, total, piece)


def gather(piece, axis, size, after=()):
    pieces = {0: piece}
    bit = size // 2
    while bit:
        for k in sorted(pieces):
            value = lax.optimization_barrier((pieces[k], *after))[0] if k and bit == 1 else pieces[k]
            pieces[k ^ bit] = swap(value, axis, bit)
        bit //= 2
    return [pieces[k] for k in range(size)]


def on_device(tokens, norm_gain, cotangent, layer_weight, shared_copy, master, momentum):
    tokens, cotangent, weight = tokens[0], cotangent[0], layer_weight[0]
    shards = lax.axis_size("fsdp")
    groups = lax.axis_size("replica")
    mine = lax.axis_index("fsdp")
    own = lax.axis_index("replica")
    rows, width = weight.shape
    inner_rate = inner_gain / math.sqrt(tokens.shape[0] * shards)

    own_exchanges = [1 << bit for bit in range(shards.bit_length() - 1)]
    cotangents = gather(cotangent, "fsdp", shards)
    blocks = prepare(tokens, norm_gain, shards)
    *_, blocks, coded_shared, coded_weight = lax.optimization_barrier(
        (*(cotangents[k] for k in own_exchanges), blocks, shared_copy, weight)
    )
    columns = lax.all_to_all(blocks, "fsdp", split_axis=0, concat_axis=0, tiled=True)

    kept, sent = code_and_decode(own, coded_shared, coded_weight, groups)
    total = kept.astype(jnp.float32) + swap(sent, "replica", 1).astype(jnp.float32)
    bit = 2
    while bit < groups:
        sent = swap(total[1::2].astype(jnp.bfloat16), "replica", bit)
        bit *= 2
        total = total[0::2] + sent.astype(jnp.float32)
    average = total[0] / groups
    momentum_next = outer_beta * momentum + average
    master_next = master - outer_rate * (average + outer_beta * momentum_next)
    pieces = gather(master_next.astype(jnp.bfloat16), "replica", groups, after=cotangents[:-1])

    rate = (1.0 - mix_weight) * inner_rate
    total, last = accumulate(mine, own, columns, cotangents[:-1], weight, pieces[:-1], rate)
    layer_next = finish(own, last, cotangents[-1], total, pieces[-1], rate)
    return (layer_next[None], master_next, momentum_next)


def solution(mesh):
    in_specs = (
        P("replica", "fsdp", None),
        P(),
        P("replica", "fsdp", None),
        P("replica", "fsdp", None),
        P("fsdp", None),
        P("fsdp", "replica"),
        P("fsdp", "replica"),
    )
    out_specs = (P("replica", "fsdp", None), P("fsdp", "replica"), P("fsdp", "replica"))
    return jax.shard_map(
        on_device, mesh=mesh, in_specs=in_specs, out_specs=out_specs, check_vma=False
    )
```

```python
import functools
import math

import jax
import jax.numpy as jnp
from jax import lax
from jax.experimental import pallas as pl
from jax.experimental.pallas import tpu as pltpu
from jax.sharding import PartitionSpec as P

BLOCK = 64


norm_eps = 1e-05
inner_gain = 0.4
outer_rate = 0.7
outer_beta = 0.9
mix_weight = 0.5
code_range = 448.0


def swap(value, axis, mask):
    size = lax.axis_size(axis)
    return lax.ppermute(value, axis, [(i, i ^ mask) for i in range(size)])


def prepare_kernel(tokens_ref, gain_ref, blocks_ref, tokens, blocks, load_sems, store_sems):
    lanes = 128
    shards, rows, count = blocks.shape
    features = shards * rows
    loads, stores = [], []
    for k in range(shards):
        columns = pl.ds(k * rows, rows)
        loads.append(pltpu.make_async_copy(tokens_ref.at[:, columns], tokens.at[:, columns], load_sems.at[k]))
        loads[k].start()
        stores.append(pltpu.make_async_copy(blocks.at[k], blocks_ref.at[k], store_sems.at[k]))
    squares = jnp.zeros((count, lanes), jnp.float32)
    for k in range(shards):
        loads[k].wait()
        for start in range(k * rows, (k + 1) * rows, lanes):
            block = tokens[:, start : start + lanes].astype(jnp.float32)
            squares = squares + block * block
    mean = jnp.sum(squares, axis=-1, keepdims=True) / features
    inverse = jnp.broadcast_to(lax.rsqrt(mean + norm_eps), (count, lanes))
    for k in range(shards):
        for start in range(0, rows, lanes):
            columns = slice(k * rows + start, k * rows + start + lanes)
            normed = tokens[:, columns].astype(jnp.float32) * inverse * gain_ref[:, columns]
            blocks[k, start : start + lanes] = jnp.transpose(normed).astype(jnp.bfloat16)
        stores[k].start()
    for store in stores:
        store.wait()


def prepare(tokens, gain, shards):
    count, features = tokens.shape
    rows = features // shards
    return pl.pallas_call(
        prepare_kernel,
        out_shape=jax.ShapeDtypeStruct((shards, rows, count), jnp.bfloat16),
        in_specs=[pl.BlockSpec(memory_space=pltpu.HBM), pl.BlockSpec(memory_space=pltpu.VMEM)],
        out_specs=pl.BlockSpec(memory_space=pltpu.HBM),
        scratch_shapes=[
            pltpu.VMEM((count, features), jnp.bfloat16),
            pltpu.VMEM((shards, rows, count), jnp.bfloat16),
            pltpu.SemaphoreType.DMA((shards,)),
            pltpu.SemaphoreType.DMA((shards,)),
        ],
        compiler_params=pltpu.CompilerParams(vmem_limit_bytes=16 * 2**20),
        cost_estimate=pl.CostEstimate(
            flops=5 * count * features, bytes_accessed=4 * count * features, transcendentals=count
        ),
        name="prepare",
    )(tokens, gain.astype(jnp.float32).reshape(1, features))


def code_kernel(own_ref, shared_ref, weight_ref, kept_ref, sent_ref, shared, weight, decoded, sems):
    lanes = 2 * BLOCK
    groups, tile, share = decoded.shape
    rows, width = shared.shape
    own = own_ref[0]
    low = lax.broadcasted_iota(jnp.int32, (tile, lanes), 1) < BLOCK

    def loads(i):
        part = pl.ds(pl.multiple_of(i * tile, tile), tile)
        return (
            pltpu.make_async_copy(shared_ref.at[part], shared.at[part], sems.at[0, i]),
            pltpu.make_async_copy(weight_ref.at[part], weight.at[part], sems.at[1, i]),
        )

    for i in range(rows // tile):
        for load in loads(i):
            load.start()

    def step(i, _):
        for load in loads(i):
            load.wait()
        part = pl.ds(pl.multiple_of(i * tile, tile), tile)
        for start in range(0, width, lanes):
            columns = slice(start, start + lanes)
            delta = shared[part, columns].astype(jnp.float32) - weight[part, columns].astype(jnp.float32)
            size = jnp.abs(delta)
            largest = jnp.where(
                low,
                jnp.max(jnp.where(low, size, 0.0), axis=-1, keepdims=True),
                jnp.max(jnp.where(low, 0.0, size), axis=-1, keepdims=True),
            )
            scale = ((largest + 1e-06) * (1.0 / code_range)).astype(jnp.bfloat16).astype(jnp.float32)
            coded = (delta * pl.reciprocal(scale)).astype(jnp.bfloat16)
            value = (coded.astype(jnp.float32) * scale).astype(jnp.bfloat16)
            piece = min(share, lanes)
            for at in range(0, lanes, piece):
                group, offset = divmod(start + at, share)
                decoded[group, :, offset : offset + piece] = value[:, at : at + piece]
        for k in range(0, groups, 2):
            kept_ref[k // 2, part] = decoded[own ^ k]
            sent_ref[k // 2, part] = decoded[own ^ (k + 1)]
        return 0

    lax.fori_loop(0, rows // tile, step, 0)


def code_and_decode(own, shared, weight, groups):
    rows, width = shared.shape
    tile = min(rows, 128)
    share = width // groups
    half = jax.ShapeDtypeStruct((groups // 2, rows, share), jnp.bfloat16)
    return pl.pallas_call(
        code_kernel,
        out_shape=(half, half),
        in_specs=[pl.BlockSpec(memory_space=pltpu.SMEM)] + [pl.BlockSpec(memory_space=pltpu.HBM)] * 2,
        out_specs=(pl.BlockSpec(memory_space=pltpu.VMEM),) * 2,
        scratch_shapes=[
            pltpu.VMEM((rows, width), jnp.bfloat16),
            pltpu.VMEM((rows, width), jnp.bfloat16),
            pltpu.VMEM((groups, tile, share), jnp.bfloat16),
            pltpu.SemaphoreType.DMA((2, rows // tile)),
        ],
        compiler_params=pltpu.CompilerParams(vmem_limit_bytes=16 * 2**20),
        cost_estimate=pl.CostEstimate(flops=20 * rows * width, bytes_accessed=6 * rows * width, transcendentals=0),
        name="code_and_decode",
    )(own.reshape(1), shared, weight)


def accumulate_kernel(parts, groups, rate, mine_ref, own_ref, tokens_ref, weight_ref, *refs):
    cotangent_refs, refs = refs[:parts], refs[parts:]
    piece_refs, refs = refs[: groups - 1], refs[groups - 1 :]
    total_ref, tokens, cotangents, weight, pieces, totals, token_sems, cotangent_sems, piece_sems, weight_sem, sems = refs
    mine, own = mine_ref[0], own_ref[0]
    depth, width = cotangent_refs[0].shape
    share = pieces.shape[2]
    tile = max(share, 256)

    loads, rest = [], []
    for k, ref in enumerate(cotangent_refs):
        loads.append(pltpu.make_async_copy(tokens_ref.at[mine ^ k], tokens.at[k], token_sems.at[k]))
        loads.append(pltpu.make_async_copy(ref, cotangents.at[pl.ds(k * depth, depth)], cotangent_sems.at[k]))
    rest.append(pltpu.make_async_copy(weight_ref, weight, weight_sem))
    for k, ref in enumerate(piece_refs):
        rest.append(pltpu.make_async_copy(ref, pieces.at[own ^ k], piece_sems.at[k]))
    for load in loads + rest:
        load.start()
    pieces[own ^ (groups - 1)] = jnp.zeros(pieces.shape[1:], pieces.dtype)
    stores = []
    some = 2
    for first in range(0, parts, some):
        end = min(first + some, parts)
        for load in loads[2 * first : 2 * end]:
            load.wait()
        left = jnp.concatenate([tokens[k] for k in range(first, end)], axis=1)
        for start in range(0, width, tile):
            columns = pl.ds(start, tile)
            right = cotangents[first * depth : end * depth, columns]
            total = jnp.dot(left, right, preferred_element_type=jnp.float32)
            if first:
                total = totals[:, columns] + total
            if end < parts:
                totals[:, columns] = total
                continue
            if start == 0:
                for load in rest:
                    load.wait()
            for group in range(start // share, (start + tile) // share):
                place = slice(group * share, (group + 1) * share)
                part = slice(group * share - start, (group + 1) * share - start)
                mixed = mix_weight * weight[:, place].astype(jnp.float32)
                mixed = mixed + (1.0 - mix_weight) * pieces[group].astype(jnp.float32)
                totals[:, place] = mixed - rate * total[:, part]
            stores.append(pltpu.make_async_copy(totals.at[:, columns], total_ref.at[:, columns], sems.at[start // tile]))
            stores[-1].start()
    for store in stores:
        store.wait()


def accumulate(mine, own, tokens, cotangents, weight, pieces, rate):
    shards, rows, depth = tokens.shape
    parts = shards - 1
    groups = len(pieces) + 1
    width = cotangents[0].shape[1]
    return pl.pallas_call(
        functools.partial(accumulate_kernel, parts, groups, rate),
        out_shape=jax.ShapeDtypeStruct((rows, width), jnp.float32),
        in_specs=[pl.BlockSpec(memory_space=pltpu.SMEM)] * 2
        + [pl.BlockSpec(memory_space=pltpu.HBM)] * (1 + parts + groups),
        out_specs=pl.BlockSpec(memory_space=pltpu.HBM),
        scratch_shapes=[
            pltpu.VMEM((parts, rows, depth), jnp.bfloat16),
            pltpu.VMEM((parts * depth, width), jnp.bfloat16),
            pltpu.VMEM((rows, width), jnp.bfloat16),
            pltpu.VMEM((groups, rows, width // groups), jnp.bfloat16),
            pltpu.VMEM((rows, width), jnp.float32),
            pltpu.SemaphoreType.DMA((parts,)),
            pltpu.SemaphoreType.DMA((parts,)),
            pltpu.SemaphoreType.DMA((groups,)),
            pltpu.SemaphoreType.DMA,
            pltpu.SemaphoreType.DMA((width // max(width // groups, 256),)),
        ],
        compiler_params=pltpu.CompilerParams(vmem_limit_bytes=58880 * 2**10),
        cost_estimate=pl.CostEstimate(
            flops=2 * depth * parts * rows * width,
            bytes_accessed=2 * depth * shards * (rows + width) + 8 * rows * width,
            transcendentals=0,
        ),
        name="accumulate",
    )(mine.reshape(1), own.reshape(1), tokens, weight, *cotangents, *pieces)


def finish_kernel(groups, rate, mine_ref, own_ref, tokens_ref, total_ref, cotangent_ref, piece_ref, out_ref, *refs):
    outs, tokens, totals, sems, token_sem, total_sems = refs
    share = piece_ref.shape[1]
    steps, _, tile = outs.shape
    last = tokens_ref.shape[0] - 1
    loads = [pltpu.make_async_copy(tokens_ref.at[mine_ref[0] ^ last], tokens, token_sem)]
    for step in range(steps):
        place = pl.ds(step * tile, tile)
        loads.append(pltpu.make_async_copy(total_ref.at[:, place], totals.at[:, place], total_sems.at[step]))
    for load in loads:
        load.start()
    loads[0].wait()
    stores = []
    for step in range(steps):
        columns = slice(step * tile, (step + 1) * tile)
        loads[step + 1].wait()
        product = jnp.dot(tokens[...], cotangent_ref[:, columns], preferred_element_type=jnp.float32)
        total = totals[:, columns] - rate * product
        for group in range(step * tile // share, (step + 1) * tile // share):
            part = slice(group * share - step * tile, (group + 1) * share - step * tile)
            factor = jnp.where((own_ref[0] ^ (groups - 1)) == group, 1.0 - mix_weight, 0.0)
            outs[step, :, part] = (total[:, part] + factor * piece_ref[...].astype(jnp.float32)).astype(jnp.bfloat16)
        stores.append(pltpu.make_async_copy(outs.at[step], out_ref.at[:, pl.ds(step * tile, tile)], sems.at[step]))
        stores[step].start()
    for store in stores:
        store.wait()


def finish(mine, own, tokens, cotangent, total, piece, rate):
    rows, width = total.shape
    depth = tokens.shape[2]
    share = piece.shape[1]
    tile = max(share, 256)
    return pl.pallas_call(
        functools.partial(finish_kernel, width // share, rate),
        out_shape=jax.ShapeDtypeStruct((rows, width), jnp.bfloat16),
        in_specs=[pl.BlockSpec(memory_space=pltpu.SMEM)] * 2
        + [pl.BlockSpec(memory_space=pltpu.HBM)] * 2
        + [pl.BlockSpec(memory_space=pltpu.VMEM)] * 2,
        out_specs=pl.BlockSpec(memory_space=pltpu.HBM),
        scratch_shapes=[
            pltpu.VMEM((width // tile, rows, tile), jnp.bfloat16),
            pltpu.VMEM((rows, depth), jnp.bfloat16),
            pltpu.VMEM((rows, width), jnp.float32),
            pltpu.SemaphoreType.DMA((width // tile,)),
            pltpu.SemaphoreType.DMA,
            pltpu.SemaphoreType.DMA((width // tile,)),
        ],
        compiler_params=pltpu.CompilerParams(vmem_limit_bytes=46 * 2**20),
        cost_estimate=pl.CostEstimate(
            flops=2 * depth * rows * width, bytes_accessed=2 * depth * (rows + width) + 7 * rows * width, transcendentals=0
        ),
        name="finish",
    )(mine.reshape(1), own.reshape(1), tokens, total, cotangent, piece)


def gather(piece, axis, size, after=()):
    pieces = {0: piece}
    bit = size // 2
    while bit:
        for k in sorted(pieces):
            value = lax.optimization_barrier((pieces[k], *after))[0] if k and bit == 1 else pieces[k]
            pieces[k ^ bit] = swap(value, axis, bit)
        bit //= 2
    return [pieces[k] for k in range(size)]


def on_device(tokens, norm_gain, cotangent, layer_weight, shared_copy, master, momentum):
    tokens, cotangent, weight = tokens[0], cotangent[0], layer_weight[0]
    shards = lax.axis_size("fsdp")
    groups = lax.axis_size("replica")
    mine = lax.axis_index("fsdp")
    own = lax.axis_index("replica")
    rows, width = weight.shape
    inner_rate = inner_gain / math.sqrt(tokens.shape[0] * shards)

    own_exchanges = [1 << bit for bit in range(shards.bit_length() - 1)]
    cotangents = gather(cotangent, "fsdp", shards)
    blocks = prepare(tokens, norm_gain, shards)
    *_, blocks, coded_shared, coded_weight = lax.optimization_barrier(
        (*(cotangents[k] for k in own_exchanges), blocks, shared_copy, weight)
    )
    columns = lax.all_to_all(blocks, "fsdp", split_axis=0, concat_axis=0, tiled=True)

    kept, sent = code_and_decode(own, coded_shared, coded_weight, groups)
    total = kept.astype(jnp.float32) + swap(sent, "replica", 1).astype(jnp.float32)
    bit = 2
    while bit < groups:
        sent = swap(total[1::2].astype(jnp.bfloat16), "replica", bit)
        bit *= 2
        total = total[0::2] + sent.astype(jnp.float32)
    average = total[0] / groups
    momentum_next = outer_beta * momentum + average
    master_next = master - outer_rate * (average + outer_beta * momentum_next)
    pieces = gather(master_next.astype(jnp.bfloat16), "replica", groups, after=cotangents[:-1])

    rate = (1.0 - mix_weight) * inner_rate
    total = accumulate(mine, own, columns, cotangents[:-1], weight, pieces[:-1], rate)
    layer_next = finish(mine, own, columns, cotangents[-1], total, pieces[-1], rate)
    return (layer_next[None], master_next, momentum_next)


def solution(mesh):
    in_specs = (
        P("replica", "fsdp", None),
        P(),
        P("replica", "fsdp", None),
        P("replica", "fsdp", None),
        P("fsdp", None),
        P("fsdp", "replica"),
        P("fsdp", "replica"),
    )
    out_specs = (P("replica", "fsdp", None), P("fsdp", "replica"), P("fsdp", "replica"))
    return jax.shard_map(
        on_device, mesh=mesh, in_specs=in_specs, out_specs=out_specs, check_vma=False
    )
```

```python
import functools
import math

import jax
import jax.numpy as jnp
from jax import lax
from jax.experimental import pallas as pl
from jax.experimental.pallas import tpu as pltpu
from jax.sharding import PartitionSpec as P

BLOCK = 64


norm_eps = 1e-05
inner_gain = 0.4
outer_rate = 0.7
outer_beta = 0.9
mix_weight = 0.5
code_range = 448.0


def swap(value, axis, mask):
    size = lax.axis_size(axis)
    return lax.ppermute(value, axis, [(i, i ^ mask) for i in range(size)])


def prepare_kernel(tokens_ref, gain_ref, blocks_ref, tokens, blocks, load_sems, store_sems):
    lanes = 128
    shards, rows, count = blocks.shape
    features = shards * rows
    loads, stores = [], []
    for k in range(shards):
        columns = pl.ds(k * rows, rows)
        loads.append(pltpu.make_async_copy(tokens_ref.at[:, columns], tokens.at[:, columns], load_sems.at[k]))
        loads[k].start()
        stores.append(pltpu.make_async_copy(blocks.at[k], blocks_ref.at[k], store_sems.at[k]))
    squares = jnp.zeros((count, lanes), jnp.float32)
    for k in range(shards):
        loads[k].wait()
        for start in range(k * rows, (k + 1) * rows, lanes):
            block = tokens[:, start : start + lanes].astype(jnp.float32)
            squares = squares + block * block
    mean = jnp.sum(squares, axis=-1, keepdims=True) / features
    inverse = jnp.broadcast_to(lax.rsqrt(mean + norm_eps), (count, lanes))
    for k in range(shards):
        for start in range(0, rows, lanes):
            columns = slice(k * rows + start, k * rows + start + lanes)
            normed = tokens[:, columns].astype(jnp.float32) * inverse * gain_ref[:, columns]
            blocks[k, start : start + lanes] = jnp.transpose(normed).astype(jnp.bfloat16)
        stores[k].start()
    for store in stores:
        store.wait()


def prepare(tokens, gain, shards):
    count, features = tokens.shape
    rows = features // shards
    return pl.pallas_call(
        prepare_kernel,
        out_shape=jax.ShapeDtypeStruct((shards, rows, count), jnp.bfloat16),
        in_specs=[pl.BlockSpec(memory_space=pltpu.HBM), pl.BlockSpec(memory_space=pltpu.VMEM)],
        out_specs=pl.BlockSpec(memory_space=pltpu.HBM),
        scratch_shapes=[
            pltpu.VMEM((count, features), jnp.bfloat16),
            pltpu.VMEM((shards, rows, count), jnp.bfloat16),
            pltpu.SemaphoreType.DMA((shards,)),
            pltpu.SemaphoreType.DMA((shards,)),
        ],
        compiler_params=pltpu.CompilerParams(vmem_limit_bytes=16 * 2**20),
        cost_estimate=pl.CostEstimate(
            flops=5 * count * features, bytes_accessed=4 * count * features, transcendentals=count
        ),
        name="prepare",
    )(tokens, gain.astype(jnp.float32).reshape(1, features))


def code_kernel(own_ref, shared_ref, weight_ref, kept_ref, sent_ref, shared, weight, decoded, sems):
    lanes = 2 * BLOCK
    groups, tile, share = decoded.shape
    rows, width = shared.shape
    own = own_ref[0]
    low = lax.broadcasted_iota(jnp.int32, (tile, lanes), 1) < BLOCK

    def loads(i):
        part = pl.ds(pl.multiple_of(i * tile, tile), tile)
        return (
            pltpu.make_async_copy(shared_ref.at[part], shared.at[part], sems.at[0, i]),
            pltpu.make_async_copy(weight_ref.at[part], weight.at[part], sems.at[1, i]),
        )

    for i in range(rows // tile):
        for load in loads(i):
            load.start()

    def step(i, _):
        for load in loads(i):
            load.wait()
        part = pl.ds(pl.multiple_of(i * tile, tile), tile)
        for start in range(0, width, lanes):
            columns = slice(start, start + lanes)
            delta = shared[part, columns].astype(jnp.float32) - weight[part, columns].astype(jnp.float32)
            size = jnp.abs(delta)
            largest = jnp.where(
                low,
                jnp.max(jnp.where(low, size, 0.0), axis=-1, keepdims=True),
                jnp.max(jnp.where(low, 0.0, size), axis=-1, keepdims=True),
            )
            scale = ((largest + 1e-06) * (1.0 / code_range)).astype(jnp.bfloat16).astype(jnp.float32)
            coded = (delta * pl.reciprocal(scale)).astype(jnp.bfloat16)
            value = (coded.astype(jnp.float32) * scale).astype(jnp.bfloat16)
            piece = min(share, lanes)
            for at in range(0, lanes, piece):
                group, offset = divmod(start + at, share)
                decoded[group, :, offset : offset + piece] = value[:, at : at + piece]
        for k in range(0, groups, 2):
            kept_ref[k // 2, part] = decoded[own ^ k]
            sent_ref[k // 2, part] = decoded[own ^ (k + 1)]
        return 0

    lax.fori_loop(0, rows // tile, step, 0)


def code_and_decode(own, shared, weight, groups):
    rows, width = shared.shape
    tile = min(rows, 128)
    share = width // groups
    half = jax.ShapeDtypeStruct((groups // 2, rows, share), jnp.bfloat16)
    return pl.pallas_call(
        code_kernel,
        out_shape=(half, half),
        in_specs=[pl.BlockSpec(memory_space=pltpu.SMEM)] + [pl.BlockSpec(memory_space=pltpu.HBM)] * 2,
        out_specs=(pl.BlockSpec(memory_space=pltpu.VMEM),) * 2,
        scratch_shapes=[
            pltpu.VMEM((rows, width), jnp.bfloat16),
            pltpu.VMEM((rows, width), jnp.bfloat16),
            pltpu.VMEM((groups, tile, share), jnp.bfloat16),
            pltpu.SemaphoreType.DMA((2, rows // tile)),
        ],
        compiler_params=pltpu.CompilerParams(vmem_limit_bytes=16 * 2**20),
        cost_estimate=pl.CostEstimate(flops=20 * rows * width, bytes_accessed=6 * rows * width, transcendentals=0),
        name="code_and_decode",
    )(own.reshape(1), shared, weight)


def accumulate_kernel(parts, groups, rate, mine_ref, own_ref, tokens_ref, weight_ref, *refs):
    cotangent_refs, refs = refs[:parts], refs[parts:]
    piece_refs, refs = refs[: groups - 1], refs[groups - 1 :]
    total_ref, tokens, cotangents, weight, pieces, totals, token_sems, cotangent_sems, piece_sems, weight_sem, sems = refs
    mine, own = mine_ref[0], own_ref[0]
    depth, width = cotangent_refs[0].shape
    share = pieces.shape[2]
    tile = max(share, 256)

    loads, rest = [], []
    for k, ref in enumerate(cotangent_refs):
        loads.append(pltpu.make_async_copy(tokens_ref.at[mine ^ k], tokens.at[k], token_sems.at[k]))
        loads.append(pltpu.make_async_copy(ref, cotangents.at[pl.ds(k * depth, depth)], cotangent_sems.at[k]))
    rest.append(pltpu.make_async_copy(weight_ref, weight, weight_sem))
    for k, ref in enumerate(piece_refs):
        rest.append(pltpu.make_async_copy(ref, pieces.at[own ^ k], piece_sems.at[k]))
    for load in loads + rest:
        load.start()
    pieces[own ^ (groups - 1)] = jnp.zeros(pieces.shape[1:], pieces.dtype)
    stores = []
    some = 2
    for first in range(0, parts, some):
        end = min(first + some, parts)
        for load in loads[2 * first : 2 * end]:
            load.wait()
        left = jnp.concatenate([tokens[k] for k in range(first, end)], axis=1)
        for start in range(0, width, tile):
            columns = pl.ds(start, tile)
            right = cotangents[first * depth : end * depth, columns]
            total = jnp.dot(left, right, preferred_element_type=jnp.float32)
            if first:
                total = totals[:, columns] + total
            if end < parts:
                totals[:, columns] = total
                continue
            if start == 0:
                for load in rest:
                    load.wait()
            for group in range(start // share, (start + tile) // share):
                place = slice(group * share, (group + 1) * share)
                part = slice(group * share - start, (group + 1) * share - start)
                mixed = mix_weight * weight[:, place].astype(jnp.float32)
                mixed = mixed + (1.0 - mix_weight) * pieces[group].astype(jnp.float32)
                totals[:, place] = mixed - rate * total[:, part]
            stores.append(pltpu.make_async_copy(totals.at[:, columns], total_ref.at[:, columns], sems.at[start // tile]))
            stores[-1].start()
    for store in stores:
        store.wait()


def accumulate(mine, own, tokens, cotangents, weight, pieces, rate):
    shards, rows, depth = tokens.shape
    parts = shards - 1
    groups = len(pieces) + 1
    width = cotangents[0].shape[1]
    return pl.pallas_call(
        functools.partial(accumulate_kernel, parts, groups, rate),
        out_shape=jax.ShapeDtypeStruct((rows, width), jnp.float32),
        in_specs=[pl.BlockSpec(memory_space=pltpu.SMEM)] * 2
        + [pl.BlockSpec(memory_space=pltpu.HBM)] * (1 + parts + groups),
        out_specs=pl.BlockSpec(memory_space=pltpu.HBM),
        scratch_shapes=[
            pltpu.VMEM((parts, rows, depth), jnp.bfloat16),
            pltpu.VMEM((parts * depth, width), jnp.bfloat16),
            pltpu.VMEM((rows, width), jnp.bfloat16),
            pltpu.VMEM((groups, rows, width // groups), jnp.bfloat16),
            pltpu.VMEM((rows, width), jnp.float32),
            pltpu.SemaphoreType.DMA((parts,)),
            pltpu.SemaphoreType.DMA((parts,)),
            pltpu.SemaphoreType.DMA((groups,)),
            pltpu.SemaphoreType.DMA,
            pltpu.SemaphoreType.DMA((width // max(width // groups, 256),)),
        ],
        compiler_params=pltpu.CompilerParams(vmem_limit_bytes=58880 * 2**10),
        cost_estimate=pl.CostEstimate(
            flops=2 * depth * parts * rows * width,
            bytes_accessed=2 * depth * shards * (rows + width) + 8 * rows * width,
            transcendentals=0,
        ),
        name="accumulate",
    )(mine.reshape(1), own.reshape(1), tokens, weight, *cotangents, *pieces)


def finish_kernel(groups, rate, mine_ref, own_ref, tokens_ref, total_ref, cotangent_ref, piece_ref, out_ref, *refs):
    outs, tokens, totals, sems, token_sem, total_sems = refs
    share = piece_ref.shape[1]
    steps, _, tile = outs.shape
    last = tokens_ref.shape[0] - 1
    loads = [pltpu.make_async_copy(tokens_ref.at[mine_ref[0] ^ last], tokens, token_sem)]
    for step in range(steps):
        place = pl.ds(step * tile, tile)
        loads.append(pltpu.make_async_copy(total_ref.at[:, place], totals.at[:, place], total_sems.at[step]))
    for load in loads:
        load.start()
    loads[0].wait()
    stores = []
    for step in range(steps):
        columns = slice(step * tile, (step + 1) * tile)
        loads[step + 1].wait()
        product = jnp.dot(tokens[...], cotangent_ref[:, columns], preferred_element_type=jnp.float32)
        total = totals[:, columns] - rate * product
        for group in range(step * tile // share, (step + 1) * tile // share):
            part = slice(group * share - step * tile, (group + 1) * share - step * tile)
            factor = jnp.where((own_ref[0] ^ (groups - 1)) == group, 1.0 - mix_weight, 0.0)
            outs[step, :, part] = (total[:, part] + factor * piece_ref[...].astype(jnp.float32)).astype(jnp.bfloat16)
        stores.append(pltpu.make_async_copy(outs.at[step], out_ref.at[:, pl.ds(step * tile, tile)], sems.at[step]))
        stores[step].start()
    for store in stores:
        store.wait()


def finish(mine, own, tokens, cotangent, total, piece, rate):
    rows, width = total.shape
    depth = tokens.shape[2]
    share = piece.shape[1]
    tile = max(share, 256)
    return pl.pallas_call(
        functools.partial(finish_kernel, width // share, rate),
        out_shape=jax.ShapeDtypeStruct((rows, width), jnp.bfloat16),
        in_specs=[pl.BlockSpec(memory_space=pltpu.SMEM)] * 2
        + [pl.BlockSpec(memory_space=pltpu.HBM)] * 2
        + [pl.BlockSpec(memory_space=pltpu.VMEM)] * 2,
        out_specs=pl.BlockSpec(memory_space=pltpu.HBM),
        scratch_shapes=[
            pltpu.VMEM((width // tile, rows, tile), jnp.bfloat16),
            pltpu.VMEM((rows, depth), jnp.bfloat16),
            pltpu.VMEM((rows, width), jnp.float32),
            pltpu.SemaphoreType.DMA((width // tile,)),
            pltpu.SemaphoreType.DMA,
            pltpu.SemaphoreType.DMA((width // tile,)),
        ],
        compiler_params=pltpu.CompilerParams(vmem_limit_bytes=58 * 2**20),
        cost_estimate=pl.CostEstimate(
            flops=2 * depth * rows * width, bytes_accessed=2 * depth * (rows + width) + 7 * rows * width, transcendentals=0
        ),
        name="finish",
    )(mine.reshape(1), own.reshape(1), tokens, total, cotangent, piece)


def gather(piece, axis, size, after=()):
    pieces = {0: piece}
    bit = size // 2
    while bit:
        for k in sorted(pieces):
            value = lax.optimization_barrier((pieces[k], *after))[0] if k and bit == 1 else pieces[k]
            pieces[k ^ bit] = swap(value, axis, bit)
        bit //= 2
    return [pieces[k] for k in range(size)]


def on_device(tokens, norm_gain, cotangent, layer_weight, shared_copy, master, momentum):
    tokens, cotangent, weight = tokens[0], cotangent[0], layer_weight[0]
    shards = lax.axis_size("fsdp")
    groups = lax.axis_size("replica")
    mine = lax.axis_index("fsdp")
    own = lax.axis_index("replica")
    rows, width = weight.shape
    inner_rate = inner_gain / math.sqrt(tokens.shape[0] * shards)

    own_exchanges = [1 << bit for bit in range(shards.bit_length() - 1)]
    cotangents = gather(cotangent, "fsdp", shards)
    blocks = prepare(tokens, norm_gain, shards)
    *_, blocks, coded_shared, coded_weight = lax.optimization_barrier(
        (*(cotangents[k] for k in own_exchanges), blocks, shared_copy, weight)
    )
    columns = lax.all_to_all(blocks, "fsdp", split_axis=0, concat_axis=0, tiled=True)

    kept, sent = code_and_decode(own, coded_shared, coded_weight, groups)
    total = kept.astype(jnp.float32) + swap(sent, "replica", 1).astype(jnp.float32)
    bit = 2
    while bit < groups:
        sent = swap(total[1::2].astype(jnp.bfloat16), "replica", bit)
        bit *= 2
        total = total[0::2] + sent.astype(jnp.float32)
    average = total[0] / groups
    momentum_next = outer_beta * momentum + average
    master_next = master - outer_rate * (average + outer_beta * momentum_next)
    pieces = gather(master_next.astype(jnp.bfloat16), "replica", groups, after=cotangents[:-1])

    rate = (1.0 - mix_weight) * inner_rate
    total = accumulate(mine, own, columns, cotangents[:-1], weight, pieces[:-1], rate)
    layer_next = finish(mine, own, columns, cotangents[-1], total, pieces[-1], rate)
    return (layer_next[None], master_next, momentum_next)


def solution(mesh):
    in_specs = (
        P("replica", "fsdp", None),
        P(),
        P("replica", "fsdp", None),
        P("replica", "fsdp", None),
        P("fsdp", None),
        P("fsdp", "replica"),
        P("fsdp", "replica"),
    )
    out_specs = (P("replica", "fsdp", None), P("fsdp", "replica"), P("fsdp", "replica"))
    return jax.shard_map(
        on_device, mesh=mesh, in_specs=in_specs, out_specs=out_specs, check_vma=False
    )
```
